32 devices in a mesh: dp: 16 (over z, x, core), head: 2 (over y).
Axes of the slice: x: 2, y: 2, z: 4, core: 2. Of those that a mesh axis runs over, the one named last changes fastest.
Arguments:
- tokens_in: bfloat16 [24576, 512], P(('dp', 'head')), may hold values from -6 to 6
- cotangent: float32 [24576, 512], P(('dp', 'head')), may hold values from -6 to 6
- data_table: float32 [2, 512], replicated, may hold values from -6 to 6
- window_group: int32 [256], P('dp'), may hold values from 0 to 1
- query_picks: int32 [256, 8, 25], P('dp', 'head'), may hold values from 0 to 95, as said below
- owner_list: int32 [6], replicated, may hold values from 0 to 15
- weight_qkv: float32 [3, 512, 512], P(None, None, 'head'), may hold values from -0.25 to 0.25
- head_bias: float32 [2, 512], P(None, 'head'), may hold values from -3 to 3
- weight_out: float32 [512, 512], P('head'), may hold values from -2 to 2
- weight_up: float32 [512, 2048], P(None, 'head'), may hold values from -0.25 to 0.25
- ff_bias: float32 [2048], P('head'), may hold values from -3 to 3
- weight_down: float32 [2048, 512], P('head'), may hold values from -0.125 to 0.125
- norm_gains: float32 [2, 512], replicated, may hold values from 0.5 to 1.5
- shifts: float32 [4, 512], replicated, may hold values from -3 to 3
- first_qkv: float32 [3, 512, 512], P(None, None, 'head'), may hold values from -512 to 512
- second_qkv: float32 [3, 512, 512], P(None, None, 'head'), may hold values from 8847.36 to 35389.44
- first_out: float32 [512, 512], P('head'), may hold values from -80 to 80
- second_out: float32 [512, 512], P('head'), may hold values from 184.32 to 742.4
- first_up: float32 [512, 2048], P(None, 'head'), may hold values from -224 to 224
- second_up: float32 [512, 2048], P(None, 'head'), may hold values from 1536 to 6144
- first_down: float32 [2048, 512], P('head'), may hold values from -448 to 448
- second_down: float32 [2048, 512], P('head'), may hold values from 4915.2 to 19660.8
- basis_qkv_left: float32 [3, 512, 512], replicated
- basis_qkv_right: float32 [3, 8, 64, 64], P(None, 'head')
- basis_out_left: float32 [8, 64, 64], P('head')
- basis_out_right: float32 [512, 512], replicated
- basis_up_left: float32 [512, 512], replicated
- basis_up_right: float32 [8, 256, 256], P('head')
- basis_down_left: float32 [8, 256, 256], P('head')
- basis_down_right: float32 [512, 512], replicated
Outputs:
- output: float32 [24576, 512], P(('dp', 'head'))
- grad_input: float32 [24576, 512], P(('dp', 'head'))
- grad_table: float32 [2, 512], replicated
- grad_gains: float32 [2, 512], replicated
- grad_shifts: float32 [4, 512], replicated
- grad_head_bias: float32 [2, 512], P(None, 'head')
- grad_ff_bias: float32 [2048], P('head')
- grad_qkv: float32 [3, 512, 512], P(None, None, 'head')
- grad_out_proj: float32 [512, 512], P('head')
- grad_up: float32 [512, 2048], P(None, 'head')
- grad_down: float32 [2048, 512], P('head')
- new_qkv: float32 [16, 3, 512, 512], P('dp', None, None, 'head')
- momentum_qkv: float32 [16, 3, 512, 512], P('dp', None, None, 'head')
- variance_qkv: float32 [16, 3, 512, 512], P('dp', None, None, 'head')
- copy_qkv: bfloat16 [16, 3, 512, 512], P('dp', None, None, 'head')
- new_out_proj: float32 [16, 512, 512], P('dp', 'head')
- moments_out_proj: float32 [16, 2, 512, 512], P('dp', None, 'head')
- copy_out_proj: bfloat16 [16, 512, 512], P('dp', 'head')
- new_up: float32 [16, 512, 2048], P('dp', None, 'head')
- momentum_up: float32 [16, 512, 2048], P('dp', None, 'head')
- variance_up: float32 [16, 512, 2048], P('dp', None, 'head')
- copy_up: bfloat16 [16, 512, 2048], P('dp', None, 'head')
- new_down: float32 [16, 2048, 512], P('dp', 'head')
- momentum_down: float32 [16, 2048, 512], P('dp', 'head')
- variance_down: float32 [16, 2048, 512], P('dp', 'head')
- copy_down: bfloat16 [16, 2048, 512], P('dp', 'head')
The draws below stay inside these ranges and needn't reach their ends.
Inputs may be any that keep to these rules, and one draw needn't show every extreme that they name: `query_picks`: within one window and head the 25 positions are distinct.
All inputs are finite; a program needn't handle non-finite values.
Results may differ from the reference program's by a relative error of at most 0.019.
Values may be sent and summed in bfloat16 or wider, within the bound.
No kernel may reach another device: no remote copies, remote signals or barrier semaphores. Data moves between devices by JAX's collectives and lax.ppermute only.
A program may use at most 192 MiB of HBM per device.

```python
import math
import jax
import jax.numpy as jnp
from jax import lax

H = 8
DH = 64
D = 512
FF = 2048
FB = 256
L = 96
TOPU = 25
NDATA = 2
WIN_DEV = 16
TOK_DEV = 1536
BATCH = 256
TOKENS = 24576
RANKS = 16


def orthogonal(key, leading, order):
    gauss = jax.random.normal(key, leading + (order, order), jnp.float32)
    ortho, unused = jnp.linalg.qr(gauss)
    return ortho


def draw_query_picks(key, part):
    subkeys = jax.random.split(jax.random.fold_in(key, 3), BATCH * H)
    orders = jax.vmap(lambda subkey: jax.random.permutation(subkey, L))(subkeys)
    return orders[:, :TOPU].reshape(BATCH, H, TOPU).astype(jnp.int32)


def draw_basis_qkv_left(key, part):
    return orthogonal(jax.random.fold_in(key, 11), (3,), D)


def draw_basis_qkv_right(key, part):
    return orthogonal(jax.random.fold_in(key, 12), (3, H), DH)


def draw_basis_out_left(key, part):
    return orthogonal(jax.random.fold_in(key, 13), (H,), DH)


def draw_basis_out_right(key, part):
    return orthogonal(jax.random.fold_in(key, 14), (), D)


def draw_basis_up_left(key, part):
    return orthogonal(jax.random.fold_in(key, 15), (), D)


def draw_basis_up_right(key, part):
    return orthogonal(jax.random.fold_in(key, 16), (H,), FB)


def draw_basis_down_left(key, part):
    return orthogonal(jax.random.fold_in(key, 17), (H,), FB)


def draw_basis_down_right(key, part):
    return orthogonal(jax.random.fold_in(key, 18), (), D)


def set_ends(entries, key, smallest, largest):
    dims = entries.shape
    spot = [jax.random.randint(jax.random.fold_in(key, axis), (), 0, dims[axis]) for axis in range(len(dims))]
    entries = entries.at[tuple(spot)].set(smallest)
    longest = dims.index(max(dims))
    spot[longest] = (spot[longest] + 1) % dims[longest]
    return entries.at[tuple(spot)].set(largest)


def block_levels(own_key, shape, cuts, smallest, largest):
    def one(dim, blocks):
        draws = jax.random.uniform(jax.random.fold_in(jax.random.fold_in(own_key, 6), dim), (blocks,), jnp.float32, smallest / len(cuts), largest / len(cuts))
        return jnp.repeat(jnp.exp(draws), shape[dim] // blocks).reshape((-1,) + (1,) * (len(shape) - dim - 1))

    level = one(*cuts[0])
    for cut in cuts[1:]:
        level = level * one(*cut)
    return level


def normal_values(own_key, dims, deviation, limit, cuts=(), kind=jnp.bfloat16):
    entries = deviation * jax.random.normal(own_key, dims, jnp.float32)
    if cuts:
        entries = entries * block_levels(own_key, dims, cuts, -0.22, 0.18)
    return jnp.clip(entries, -limit, limit).astype(kind)


def setup_inputs(seed: int = 0) -> dict:
    splits = jax.random.split(jax.random.key(seed), 31)
    tokens_in = normal_values(splits[0], (TOKENS, D), 1.0, 6.0, ((0, 32),))
    cotangent = normal_values(splits[1], (TOKENS, D), 1.0, 6.0, ((0, 32),), jnp.float32)
    data_table = normal_values(splits[2], (NDATA, D), 1.0, 6.0, (), jnp.float32)
    window_group = set_ends(jax.random.randint(splits[3], (BATCH,), 0, NDATA), jax.random.fold_in(splits[3], 1), 0, NDATA - 1).astype(jnp.int32)
    query_picks = draw_query_picks(jax.random.fold_in(splits[30], 71), 0)
    owner_list = set_ends(jax.random.randint(splits[5], (6,), 0, RANKS), jax.random.fold_in(splits[5], 1), 0, RANKS - 1).astype(jnp.int32)
    weight_qkv = normal_values(splits[6], (3, D, D), D ** -0.5, 0.25, ((2, 2),), jnp.float32)
    head_bias = normal_values(splits[7], (2, D), 0.5, 3.0, ((1, 2),), jnp.float32)
    weight_out = normal_values(splits[8], (D, D), (max(D // 64, 1)) ** -0.5, 2.0, ((0, 2),), jnp.float32)
    weight_up = normal_values(splits[9], (D, FF), D ** -0.5, 0.25, ((1, 2),), jnp.float32)
    ff_bias = normal_values(splits[10], (FF,), 0.5, 3.0, ((0, 2),), jnp.float32)
    weight_down = normal_values(splits[11], (FF, D), FF ** -0.5, 0.125, ((0, 2),), jnp.float32)
    norm_gains = jnp.clip(1.0 + 0.1 * jax.random.normal(splits[12], (2, D), jnp.float32), 0.5, 1.5)
    shifts = normal_values(splits[13], (4, D), 0.5, 3.0, (), jnp.float32)
    first_qkv = normal_values(splits[14], (3, D, D), (0.6 * TOKENS ** 0.5), 512.0, ((2, 2),), jnp.float32)
    second_qkv = jnp.clip(jnp.exp(math.log(35389.44) - 1.3862944 * jax.random.uniform(splits[15], (3, D, D), jnp.float32) ** block_levels(splits[15], (3, D, D), ((2, 2),), -0.2, 0.2)), 8847.36, 35389.44)
    first_out = normal_values(splits[16], (D, D), (0.85 * BATCH ** 0.5), 80.0, ((0, 2),), jnp.float32)
    second_out = jnp.clip(jnp.exp(math.log(742.4) - 1.3932148 * jax.random.uniform(splits[17], (D, D), jnp.float32) ** block_levels(splits[17], (D, D), ((0, 2),), -0.2, 0.2)), 184.32, 742.4)
    first_up = normal_values(splits[18], (D, FF), (0.25 * TOKENS ** 0.5), 224.0, ((1, 2),), jnp.float32)
    second_up = jnp.clip(jnp.exp(math.log(6144.0) - 1.3862944 * jax.random.uniform(splits[19], (D, FF), jnp.float32) ** block_levels(splits[19], (D, FF), ((1, 2),), -0.2, 0.2)), 1536.0, 6144.0)
    first_down = normal_values(splits[20], (FF, D), (0.45 * TOKENS ** 0.5), 448.0, ((0, 2),), jnp.float32)
    second_down = jnp.clip(jnp.exp(math.log(19660.8) - 1.3862944 * jax.random.uniform(splits[21], (FF, D), jnp.float32) ** block_levels(splits[21], (FF, D), ((0, 2),), -0.2, 0.2)), 4915.2, 19660.8)
    basis_qkv_left = draw_basis_qkv_left(jax.random.fold_in(splits[30], 71), 0)
    basis_qkv_right = draw_basis_qkv_right(jax.random.fold_in(splits[30], 71), 0)
    basis_out_left = draw_basis_out_left(jax.random.fold_in(splits[30], 71), 0)
    basis_out_right = draw_basis_out_right(jax.random.fold_in(splits[30], 71), 0)
    basis_up_left = draw_basis_up_left(jax.random.fold_in(splits[30], 71), 0)
    basis_up_right = draw_basis_up_right(jax.random.fold_in(splits[30], 71), 0)
    basis_down_left = draw_basis_down_left(jax.random.fold_in(splits[30], 71), 0)
    basis_down_right = draw_basis_down_right(jax.random.fold_in(splits[30], 71), 0)
    return {"tokens_in": tokens_in, "cotangent": cotangent, "data_table": data_table, "window_group": window_group, "query_picks": query_picks, "owner_list": owner_list, "weight_qkv": weight_qkv, "head_bias": head_bias, "weight_out": weight_out, "weight_up": weight_up, "ff_bias": ff_bias, "weight_down": weight_down, "norm_gains": norm_gains, "shifts": shifts, "first_qkv": first_qkv, "second_qkv": second_qkv, "first_out": first_out, "second_out": second_out, "first_up": first_up, "second_up": second_up, "first_down": first_down, "second_down": second_down, "basis_qkv_left": basis_qkv_left, "basis_qkv_right": basis_qkv_right, "basis_out_left": basis_out_left, "basis_out_right": basis_out_right, "basis_up_left": basis_up_left, "basis_up_right": basis_up_right, "basis_down_left": basis_down_left, "basis_down_right": basis_down_right}


EPS_NORM = 1e-05
EPS_ADAM = 1e-08
BETA_ONE = 0.5
BETA_TWO = 0.5

@jax.custom_vjp
def low(v):
    return lax.optimization_barrier(v.astype(jnp.bfloat16)).astype(jnp.float32)

@jax.custom_vjp
def low_back(v):
    return v

def low_keep(v):
    return (low(v), None)

def low_pass(kept, grad):
    return (grad,)

def back_keep(v):
    return (v, None)

def back_low(kept, grad):
    return (low(grad),)
low.defvjp(low_keep, low_pass)
low_back.defvjp(back_keep, back_low)

def layer_norm(rows, gain, shift):
    center = rows - lax.optimization_barrier(jnp.mean(rows, axis=-1, keepdims=True))
    inverse = lax.rsqrt(lax.optimization_barrier(jnp.mean(center * center, axis=-1, keepdims=True)) + EPS_NORM)
    return center * inverse * gain + shift

def forward(tokens, table, weight_qkv, head_bias, weight_out, weight_up, ff_bias, weight_down, norm_gains, shifts, groups, picks):
    highest = lax.Precision.HIGHEST
    row_count = tokens.shape[0]
    windows = groups.shape[0]
    choose = (jnp.repeat(groups, L)[:, None] == jnp.arange(NDATA)[None, :]).astype(tokens.dtype)
    embedded = tokens + jnp.dot(choose, table, precision=highest)
    embedded_low = low(embedded)
    bias_three = jnp.stack([head_bias[0], jnp.zeros_like(head_bias[0]), head_bias[1]])
    projected = jnp.einsum('td,jde->jte', embedded_low, low(weight_qkv), precision=highest) + bias_three[:, None, :]
    projected = low_back(low(projected))
    heads_view = projected.reshape(3, windows, L, H, DH)
    queries, keys_all, values = (heads_view[0], heads_view[1], heads_view[2])
    onehot = (picks[..., None] == jnp.arange(L)).astype(tokens.dtype)
    picked = jnp.einsum('whul,wlhd->whud', onehot, queries, precision=highest)
    raw_scores = low_back(jnp.einsum('whud,wlhd->whul', picked, keys_all, precision=highest))
    attention = jax.nn.softmax(raw_scores * (1.0 / math.sqrt(DH)), axis=-1)
    attention_low = low(attention)
    attended = jnp.einsum('whul,wlhd->whud', attention_low, values, precision=highest)
    value_mean = lax.optimization_barrier(jnp.mean(values, axis=1))
    context = value_mean[:, None] + jnp.einsum('whul,whud->wlhd', onehot, attended - value_mean[:, :, None], precision=highest)
    context = low_back(low(context)).reshape(row_count, D)
    attn_branch = low_back(jnp.dot(context, low(weight_out), precision=highest) + shifts[0])
    normed = layer_norm(embedded + attn_branch, norm_gains[0], shifts[2])
    pre_act = low_back(jnp.dot(low(normed), low(weight_up), precision=highest) + ff_bias)
    activated = low(jax.nn.gelu(pre_act, approximate=False))
    ffn_branch = low_back(jnp.dot(activated, low(weight_down), precision=highest) + shifts[1])
    return layer_norm(normed + ffn_branch, norm_gains[1], shifts[3])

def left_turn(rotation, matrix, inverse):
    highest = lax.Precision.HIGHEST
    if rotation.ndim == 2:
        return jnp.dot(rotation if inverse else rotation.T, matrix, precision=highest)
    number_blocks, block = (rotation.shape[0], rotation.shape[1])
    pieces = matrix.reshape(number_blocks, block, matrix.shape[1])
    pattern = 'kab,kbn->kan' if inverse else 'kab,kan->kbn'
    return jnp.einsum(pattern, rotation, pieces, precision=highest).reshape(matrix.shape)

def right_turn(rotation, matrix, inverse):
    highest = lax.Precision.HIGHEST
    if rotation.ndim == 2:
        return jnp.dot(matrix, rotation.T if inverse else rotation, precision=highest)
    number_blocks, block = (rotation.shape[0], rotation.shape[1])
    pieces = matrix.reshape(matrix.shape[0], number_blocks, block)
    pattern = 'mkb,kab->mka' if inverse else 'mka,kab->mkb'
    return jnp.einsum(pattern, pieces, rotation, precision=highest).reshape(matrix.shape)

def adam_rotated(gradient, weight, moment_one, moment_two, left_basis, right_basis, step_rate):
    turned = right_turn(right_basis, left_turn(left_basis, gradient, False), False)
    first_new = BETA_ONE * moment_one + (1.0 - BETA_ONE) * turned
    second_new = BETA_TWO * moment_two + (1.0 - BETA_TWO) * turned * turned
    update = left_turn(left_basis, right_turn(right_basis, first_new / (jnp.sqrt(second_new) + EPS_ADAM), True), True)
    return (weight - step_rate * update, first_new, second_new)

def place(values, owner):
    ranks_line = jnp.arange(RANKS)
    owned = (owner == ranks_line).reshape((RANKS,) + (1,) * values.ndim)
    return jnp.where(owned, values[None], jnp.zeros_like(values[None]))

def reference(tokens_in, cotangent, data_table, window_group, query_picks, owner_list, weight_qkv, head_bias, weight_out, weight_up, ff_bias, weight_down, norm_gains, shifts, first_qkv, second_qkv, first_out, second_out, first_up, second_up, first_down, second_down, basis_qkv_left, basis_qkv_right, basis_out_left, basis_out_right, basis_up_left, basis_up_right, basis_down_left, basis_down_right):
    params = (data_table, weight_qkv, head_bias, weight_out, weight_up, ff_bias, weight_down, norm_gains, shifts)
    token_groups = tokens_in.astype(jnp.float32).reshape(RANKS, TOK_DEV, D)
    cotangent_groups = cotangent.reshape(RANKS, TOK_DEV, D)
    group_ids = window_group.reshape(RANKS, WIN_DEV)
    pick_groups = query_picks.reshape(RANKS, WIN_DEV, H, TOPU)

    def one_group(totals, window_block):
        tokens_here, cotangent_here, groups_here, picks_here = window_block

        def forward_group(tokens_now, *pars):
            return forward(tokens_now, *pars, groups_here, picks_here)
        group_out, pullback = jax.vjp(forward_group, tokens_here, *params)
        grads = pullback(cotangent_here)
        totals = tuple((total + piece for total, piece in zip(totals, grads[1:])))
        return (totals, (group_out, grads[0]))
    zeros_init = tuple((jnp.zeros_like(param) for param in params))
    totals, (outs, grads_in) = lax.scan(one_group, zeros_init, (token_groups, cotangent_groups, group_ids, pick_groups))
    g_table, g_qkv, g_head_bias, g_out, g_up, g_ff_bias, g_down, g_gains, g_shifts = totals
    output = outs.reshape(TOKENS, D)
    grad_input = grads_in.reshape(TOKENS, D)
    rate_wide = D ** (-0.5)
    rate_out = max(D // 64, 1) ** (-0.5)
    rate_down = FF ** (-0.5)
    new_list, first_list, second_list = ([], [], [])
    for which in range(3):
        new_w, first_new, second_new = adam_rotated(g_qkv[which], weight_qkv[which], first_qkv[which], second_qkv[which], basis_qkv_left[which], basis_qkv_right[which], rate_wide)
        new_list.append(place(new_w, owner_list[which]))
        first_list.append(place(first_new, owner_list[which]))
        second_list.append(place(second_new, owner_list[which]))
    new_qkv = jnp.stack(new_list, axis=1)
    momentum_qkv = jnp.stack(first_list, axis=1)
    variance_qkv = jnp.stack(second_list, axis=1)
    new_o, first_o, second_o = adam_rotated(g_out, weight_out, first_out, second_out, basis_out_left, basis_out_right, rate_out)
    new_u, first_u, second_u = adam_rotated(g_up, weight_up, first_up, second_up, basis_up_left, basis_up_right, rate_wide)
    new_d, first_d, second_d = adam_rotated(g_down, weight_down, first_down, second_down, basis_down_left, basis_down_right, rate_down)
    new_out_proj = place(new_o, owner_list[3])
    moments_out_proj = place(jnp.stack([first_o, second_o]), owner_list[3])
    new_up = place(new_u, owner_list[4])
    momentum_up = place(first_u, owner_list[4])
    variance_up = place(second_u, owner_list[4])
    new_down = place(new_d, owner_list[5])
    momentum_down = place(first_d, owner_list[5])
    variance_down = place(second_d, owner_list[5])
    return (output, grad_input, g_table, g_gains, g_shifts, g_head_bias, g_ff_bias, g_qkv, g_out, g_up, g_down, new_qkv, momentum_qkv, variance_qkv, new_qkv.astype(jnp.bfloat16), new_out_proj, moments_out_proj, new_out_proj.astype(jnp.bfloat16), new_up, momentum_up, variance_up, new_up.astype(jnp.bfloat16), new_down, momentum_down, variance_down, new_down.astype(jnp.bfloat16))
```

```python
import math

import jax
import jax.numpy as jnp
from jax import lax
from jax.experimental import pallas as pl
from jax.experimental.pallas import tpu as pltpu
from jax.sharding import PartitionSpec as P

f32 = jnp.float32
bf16 = jnp.bfloat16

NDATA = 2
EPS_NORM = 1e-05
EPS_ADAM = 1e-08
BETA_ONE = 0.5
BETA_TWO = 0.5

GROUP = 4
SLOTS = 32
MB = 1 << 20


def nn(a, b):
    return jnp.dot(a, b, preferred_element_type=f32)


def nt(a, b):
    return lax.dot_general(a, b, (((1,), (1,)), ((), ())), preferred_element_type=f32)


def col_sum(x):
    return jnp.sum(x, axis=0, keepdims=True)


def row_mean(x):
    return jnp.mean(x, axis=-1, keepdims=True)


VMEM = pl.BlockSpec(memory_space=pltpu.VMEM)
SMEM = pl.BlockSpec(memory_space=pltpu.SMEM)
HBM = pl.BlockSpec(memory_space=pl.ANY)


US = 1_000_000_000


def call(body, outs, ins, args, scratch, limit, flops, nbytes, aliases={}):
    return pl.pallas_call(
        body,
        out_shape=tuple(jax.ShapeDtypeStruct(s, d) for s, d, _ in outs),
        in_specs=ins,
        out_specs=tuple(spec for _, _, spec in outs),
        scratch_shapes=scratch,
        input_output_aliases=aliases,
        compiler_params=pltpu.CompilerParams(vmem_limit_bytes=limit * MB),
        cost_estimate=pl.CostEstimate(
            flops=int(flops), bytes_accessed=int(nbytes), transcendentals=0
        ),
    )(*args)


def head_mask(cols):
    width = cols // GROUP
    shape = (GROUP * SLOTS, cols)
    return (
        lax.broadcasted_iota(jnp.int32, shape, 0) // SLOTS
        == lax.broadcasted_iota(jnp.int32, shape, 1) // width
    )


def one_hot(picks, w, length):
    row = picks[pl.ds(w, 1), :]
    spots = lax.broadcasted_iota(jnp.int32, (length, GROUP * SLOTS), 0).astype(f32)
    columns = (spots == row).astype(f32)
    return columns.astype(bf16), columns.T.astype(bf16)


def attend(info, emb, wq, bias, picks, q_out, k_out, v_out, ctx, att, picked, windows, length, scale):
    cols = wq.shape[2]
    rows = emb.shape[0]
    step = 2 * length

    def project(b, carry):
        here = pl.ds(pl.multiple_of(b * step, 32), step)
        e = emb[here, :]
        for j, out in enumerate((q_out, k_out, v_out)):
            out[here, :] = (nn(e, wq[j]) + bias[j : j + 1, :]).astype(bf16)
        return carry

    lax.fori_loop(0, rows // step, project, 0)
    mask = head_mask(cols)
    mask_low = mask.astype(f32).astype(bf16)

    def window(w, carry):
        here = pl.ds(pl.multiple_of(w * length, 32), length)
        up, down = one_hot(picks, w, length)
        q, k, v = q_out[here, :], k_out[here, :], v_out[here, :]
        sel = jnp.where(mask, nn(down, q), 0.0).astype(bf16)
        scores = nt(sel, k) * scale
        exponent = jnp.exp(scores - jnp.max(scores, axis=-1, keepdims=True))
        probs = exponent / jnp.sum(exponent, axis=-1, keepdims=True)
        mixed = jnp.where(mask, nn(probs.astype(bf16), v), 0.0).astype(bf16)
        mean = col_sum(v.astype(f32)) * (1.0 / length)
        active = nn(up, mask_low)
        ctx[here, :] = (nn(up, mixed) + (1.0 - active) * mean).astype(bf16)
        att[w] = probs
        picked[w] = sel
        return carry

    lax.fori_loop(0, windows, window, 0)


def attend_own(windows, length, scale, info, tokens, table, w_in, bias, picks_in,
               q, k, v, ctx, att, picked, wq, emb, picks):
    picks[...] = picks_in[:, : GROUP * SLOTS].astype(f32)
    for j in range(3):
        wq[j] = w_in[j].astype(bf16)
    for w in range(windows):
        here = pl.ds(w * length, length)
        emb[here, :] = (tokens[here, :].astype(f32) + table[pl.ds(info[1 + w], 1), :]).astype(bf16)
    attend(info, emb, wq, bias, picks, q, k, v, ctx, att, picked, windows, length, scale)


def attend_far(windows, length, scale, info, emb, y_piece, c_piece,
               q, k, v, ctx, att, picked, wq, picks, extra, bias, sems):
    core = info[0]
    half = wq.shape[1] // 2
    copies = []
    for j in range(3):
        for i, (piece, spot) in enumerate(((y_piece, core), (c_piece, 1 - core))):
            copies.append(
                pltpu.make_async_copy(
                    piece.at[pl.ds(j * half, half), :],
                    wq.at[j, pl.ds(pl.multiple_of(spot * half, half), half), :],
                    sems.at[2 * j + i],
                )
            )
    copies.append(
        pltpu.make_async_copy(
            y_piece.at[pl.ds(3 * half, extra.shape[0]), :], extra, sems.at[6]
        )
    )
    for copy in copies:
        copy.start()
    for copy in copies:
        copy.wait()
    rest = extra[...].astype(f32)
    pw = picks.shape[0]
    picks[...] = rest[:pw, : GROUP * SLOTS]
    base = windows
    for j, at in ((0, 0), (2, 3)):
        spot = base + at
        bias[j : j + 1, :] = (
            rest[spot : spot + 1] + rest[spot + 1 : spot + 2] + rest[spot + 2 : spot + 3]
        )
    bias[1:2, :] = jnp.zeros_like(bias[1:2, :])
    attend(info, emb, wq, bias, picks, q, k, v, ctx, att, picked, windows, length, scale)


def gelu_pair(x):
    bell = jnp.exp(-0.5 * (x * x))
    t = 1.0 / (1.0 + (0.3275911 * math.sqrt(0.5)) * jnp.abs(x))
    poly = t * (
        0.5 * 0.254829592
        + t * (0.5 * -0.284496736 + t * (0.5 * 1.421413741 + t * (0.5 * -1.453152027 + t * (0.5 * 1.061405429))))
    )
    tail = poly * bell
    phi = jnp.where(x >= 0.0, 1.0 - tail, tail)
    return x * phi, phi + x * bell * (1.0 / math.sqrt(2.0 * math.pi))


def feed_forward(length, block, info, tokens, table, ctx0, ctx1, wout, y_piece, c_piece, wup, wdown,
                 ff_bias, gains, shifts, cot,
                 out, gp1, ga, keep, send, sums, wo,
                 up, dn, act, gpre, gelu_d, nl, gb, nl_t, gb_t, pre, ffb, extra, buf, sems):
    core = info[0]
    rows, width = tokens.shape
    cols = wout.shape[0]
    hid = wup.shape[1]
    half = hid // 2
    places = []
    at = 0
    for dst, n in ((wo.at[1], cols // 2),):
        places.append((at, n, lambda spot, n=n: wo.at[1, pl.ds(pl.multiple_of(spot * n, n), n), :]))
        at += n
    n = width // 2
    for h in range(2):
        places.append(
            (at, n, lambda spot, n=n, h=h: up.at[1, pl.ds(pl.multiple_of(spot * n, n), n), pl.ds(h * half, half)])
        )
        at += n
    n = hid // 2
    places.append((at, n, lambda spot, n=n: dn.at[1, pl.ds(pl.multiple_of(spot * n, n), n), :]))
    at += n
    copies = []
    for piece, spot in ((y_piece, core), (c_piece, 1 - core)):
        for start, n, place in places:
            copies.append(
                pltpu.make_async_copy(piece.at[pl.ds(start, n), :], place(spot), sems.at[len(copies)])
            )
    copies.append(pltpu.make_async_copy(y_piece.at[pl.ds(at, 16), :], extra, sems.at[len(copies)]))
    for copy in copies:
        copy.start()
    wo[0] = wout[...].astype(bf16)
    up[0] = wup[...].astype(bf16)
    dn[0] = wdown[...].astype(bf16)
    sums[...] = jnp.zeros_like(sums)
    ffb[0:1, :] = ff_bias[...]
    for copy in copies:
        copy.wait()
    rest = extra[...].astype(f32)
    for h in range(2):
        ffb[1:2, h * half : (h + 1) * half] = rest[h : h + 1] + rest[2 + h : 3 + h] + rest[4 + h : 5 + h]

    per = block // length

    def rows_block(b, carry):
        start = pl.multiple_of(b * block, 32)
        here = pl.ds(start, block)
        for i in range(per):
            part = pl.ds(pl.multiple_of(start + i * length, 32), length)
            pre[i * length : (i + 1) * length, :] = (
                tokens[part, :].astype(f32) + table[pl.ds(info[1 + b * per + i], 1), :]
            )
        x = pre[...] + (nn(ctx0[here, :], wo[0]) + nn(ctx1[here, :], wo[1]) + shifts[0:1, :])
        center = x - row_mean(x)
        inv_one = lax.rsqrt(row_mean(center * center) + EPS_NORM)
        unit_one = center * inv_one
        normed = unit_one * gains[0:1, :] + shifts[2:3, :]
        low = normed.astype(bf16)
        nl[here, :] = low
        branch = shifts[1:2, :]
        for ch in range(4):
            g, o = ch // 2, (ch % 2) * half
            z = nn(low, up[g, :, o : o + half]) + ffb[g : g + 1, o : o + half]
            a, d = gelu_pair(z)
            a = a.astype(bf16)
            act[here, ch * half : (ch + 1) * half] = a
            gelu_d[:, ch * half : (ch + 1) * half] = d.astype(bf16)
            branch = branch + nn(a, dn[g, o : o + half, :])
        y = normed + branch
        center = y - row_mean(y)
        inv_two = lax.rsqrt(row_mean(center * center) + EPS_NORM)
        unit_two = center * inv_two
        out[here, :] = unit_two * gains[1:2, :] + shifts[3:4, :]
        c = cot[here, :]
        sums[1:2, :] += col_sum(c * unit_two)
        sums[5:6, :] += col_sum(c)
        g2 = c * gains[1:2, :]
        gp2 = (g2 - row_mean(g2) - unit_two * row_mean(g2 * unit_two)) * inv_two
        low = gp2.astype(bf16)
        gb[here, :] = low
        sums[3:4, :] += col_sum(low.astype(f32))
        total = gp2
        for ch in range(4):
            g, o = ch // 2, (ch % 2) * half
            p = nt(low, dn[g, o : o + half, :]) * gelu_d[:, ch * half : (ch + 1) * half].astype(f32)
            p = p.astype(bf16)
            gpre[here, ch * half : (ch + 1) * half] = p
            sums[6 + ch : 7 + ch, :] += col_sum(p.astype(f32))
            total = total + nt(p, up[g, :, o : o + half])
        sums[0:1, :] += col_sum(total * unit_one)
        sums[4:5, :] += col_sum(total)
        g1 = total * gains[0:1, :]
        gp = (g1 - row_mean(g1) - unit_one * row_mean(g1 * unit_one)) * inv_one
        gp1[here, :] = gp
        low = gp.astype(bf16)
        ga[here, :] = low
        sums[2:3, :] += col_sum(low.astype(f32))
        for i in range(per):
            spot = pl.ds(10 + info[1 + b * per + i], 1)
            sums[spot, :] += col_sum(gp[i * length : (i + 1) * length, :])
        return carry

    lax.fori_loop(0, rows // block, rows_block, 0)
    nl_t[...] = nl[...].astype(f32).T.astype(bf16)
    gb_t[...] = gb[...].astype(f32).T.astype(bf16)
    for ch in range(4):
        g, o = ch // 2, (ch % 2) * half
        here = slice(ch * half, (ch + 1) * half)
        buf[g, o : o + half, :] = nn(nl_t[...], gpre[:, here]).astype(bf16)
        buf[g, hid + o : hid + o + half, :] = nn(gb_t[...], act[:, here]).astype(bf16)
    for g, ctx in enumerate((ctx0, ctx1)):
        buf[g, 2 * hid : 2 * hid + cols, :] = nn(ctx[...].astype(f32).T.astype(bf16), ga[...]).astype(bf16)
    n = buf.shape[1] // 2
    copies = []
    for g in range(2):
        for i, (dst, spot) in enumerate(((keep, core), (send, 1 - core))):
            copies.append(
                pltpu.make_async_copy(
                    buf.at[g, pl.ds(pl.multiple_of(spot * n, 32), n), :], dst.at[g], sems.at[2 * g + i]
                )
            )
    for copy in copies:
        copy.start()
    for copy in copies:
        copy.wait()


def attend_back(windows, length, scale, info, ga, emb, wo, sums,
                k0, v0, att0, picked0, picks0, wq0, k1, v1, att1, picked1, picks1, wq1,
                gq, gk, gv, keep, send,
                gctx, emb_t, tsum, buf, small, sems):
    core = info[0]
    rows, width = emb.shape
    cols = wq0.shape[2]
    mask = head_mask(cols)
    mask_low = mask.astype(f32).astype(bf16)
    step = 2 * length

    def back(b, carry):
        here = pl.ds(pl.multiple_of(b * step, 32), step)
        e = ga[here, :]
        for g in range(2):
            gctx[here, g * cols : (g + 1) * cols] = nt(e, wo[g]).astype(bf16)
        return carry

    lax.fori_loop(0, rows // step, back, 0)
    tsum[...] = jnp.zeros_like(tsum)
    sides = ((k0, v0, att0, picked0, picks0), (k1, v1, att1, picked1, picks1))

    def window(w, carry):
        here = pl.ds(pl.multiple_of(w * length, 32), length)
        for g, (k_in, v_in, att, picked, picks) in enumerate(sides):
            at = slice(g * cols, (g + 1) * cols)
            up, down = one_hot(picks, w, length)
            k, v = k_in[here, :], v_in[here, :]
            gc = gctx[here, at]
            ge = jnp.where(mask, nn(down, gc), 0.0).astype(bf16)
            active = nn(up, mask_low)
            gmean = col_sum((1.0 - active) * gc.astype(f32)) * (1.0 / length)
            probs = att[w]
            gprobs = nt(ge, v)
            low_t = probs.T.astype(bf16)
            g_value = (nn(low_t, ge) + gmean).astype(bf16)
            weighted = probs * gprobs
            graw = (weighted - probs * jnp.sum(weighted, axis=-1, keepdims=True)) * scale
            g_key = nn(graw.T.astype(bf16), picked[w]).astype(bf16)
            gpick = jnp.where(mask, nn(graw.astype(bf16), k), 0.0).astype(bf16)
            g_query = nn(up, gpick).astype(bf16)
            gq[here, at] = g_query
            gk[here, at] = g_key
            gv[here, at] = g_value
            for j, x in enumerate((g_query, g_key, g_value)):
                spot = pl.ds(2 * j + info[1 + w], 1)
                tsum[spot, at] += col_sum(x.astype(f32))
        return carry

    lax.fori_loop(0, windows, window, 0)
    emb_t[...] = emb[...].astype(f32).T.astype(bf16)
    half = width // 2
    for g in range(2):
        at = slice(g * cols, (g + 1) * cols)
        for j, x in enumerate((gq, gk, gv)):
            r = nn(emb_t[...], x[:, at]).astype(bf16)
            buf[g, j * half : (j + 1) * half, :cols] = r[:half]
            buf[g, j * half : (j + 1) * half, cols:] = r[half:]
    total = jnp.zeros((8, width), f32)
    for j in range(3):
        for g, wq in enumerate((wq0, wq1)):
            x = tsum[2 * j : 2 * j + 8, g * cols : (g + 1) * cols]
            hi = x.astype(bf16)
            lo = (x - hi.astype(f32)).astype(bf16)
            total = total + nt(hi, wq[j]) + nt(lo, wq[j])
    for g in range(2):
        at = slice(g * cols, (g + 1) * cols)
        small[g] = jnp.zeros_like(small[g])
        small[g, 0:2, :] = total[0:2] + sums[10:12, :]
        small[g, 2:8, :] = sums[0:6, :]
        small[g, 8:10, :] = sums[6 + 2 * g : 8 + 2 * g, :]
        small[g, 10:11, :cols] = tsum[0:1, at] + tsum[1:2, at]
        small[g, 10:11, cols:] = tsum[4:5, at] + tsum[5:6, at]
        buf[g, 3 * half : 3 * half + 16, :] = small[g].astype(bf16)
    n = 3 * half // 2
    copies = []
    for g in range(2):
        for dst, spot in ((keep, core), (send, 1 - core)):
            copies.append(
                pltpu.make_async_copy(
                    buf.at[g, pl.ds(pl.multiple_of(spot * n, 32), n), :],
                    dst.at[g, pl.ds(0, n), :],
                    sems.at[len(copies)],
                )
            )
            copies.append(
                pltpu.make_async_copy(
                    buf.at[g, pl.ds(2 * n, 16), :], dst.at[g, pl.ds(n, 16), :], sems.at[len(copies)]
                )
            )
    for copy in copies:
        copy.start()
    for copy in copies:
        copy.wait()


def input_grad(gq, gk, gv, wq0, wq1, gp1, out):
    rows = gp1.shape[0]
    cols = wq0.shape[2]
    step = min(rows, 192)

    def block(b, carry):
        here = pl.ds(pl.multiple_of(b * step, 32), step)
        total = gp1[here, :]
        for j, x in enumerate((gq, gk, gv)):
            for g, wq in enumerate((wq0, wq1)):
                total = total + nt(x[here, g * cols : (g + 1) * cols], wq[j])
        out[here, :] = total
        return carry

    lax.fori_loop(0, rows // step, block, 0)


def hop(x, *bits):
    heads = lax.axis_size("head")
    flip = sum((1 << k) * (heads if axis == "dp" else 1) for axis, k in bits)
    count = lax.axis_size("dp") * heads
    return lax.ppermute(x, ("dp", "head"), [(i, i ^ flip) for i in range(count)])


def side(bit):
    axis, k = bit
    return (lax.axis_index(axis) >> k) & 1


def subsets(bits):
    return [[b for i, b in enumerate(bits) if (r >> i) & 1] for r in range(1 << len(bits))]


def pair_sum(terms):
    while len(terms) > 1:
        terms = [terms[i] + terms[i + 1] for i in range(0, len(terms), 2)]
    return terms[0]


def pick(x, bits, far, flips):
    for bit in bits:
        flipped = bit in flips
        if bit == far:
            x = x[1:] if flipped else x[:1]
        else:
            n = x.shape[1] // 2
            x = lax.dynamic_slice_in_dim(x, (side(bit) ^ int(flipped)) * n, n, 1)
    return x


def scatter_sum(x, bits, far, small=None):
    terms, rest = [], []
    for flips in subsets(bits):
        part = pick(x, bits, far, flips)
        if small is not None:
            part = jnp.concatenate([part, pick(small, [far] if far in bits else [], far, flips)], 1)
        if flips:
            part = hop(part, *flips)
        terms.append(part.astype(f32))
    total = pair_sum(terms).astype(bf16)
    if small is None:
        return total
    n = total.shape[1] - small.shape[1]
    return total[:, :n], total[:, n:]


def gather(x, bits):
    parts = {}
    for r, flips in enumerate(subsets(bits)):
        parts[r] = hop(x, *flips) if flips else x
    for i, bit in enumerate(bits):
        m = side(bit) == 0
        parts = {
            r: jnp.where(m, parts[r], parts[r ^ (1 << i)]) for r in parts
        }
    order = sorted(parts, key=lambda r: [(r >> i) & 1 for i in range(len(bits))])
    return jnp.concatenate([parts[r] for r in order], axis=0)


def plus(a, b):
    return (a.astype(f32) + b.astype(f32)).astype(bf16)


def total_late(keep, send, small_rows, bits, far, core):
    x = plus(keep, hop(send, core))
    x, small = x[:, :-small_rows], x[:, -small_rows:]
    stages = [[far, bits[0]]] + [bits[i : i + 2] for i in range(1, len(bits), 2)]
    for stage in stages:
        x, small = scatter_sum(x, stage, far, small)
    x = x[0]
    for stage in reversed(stages):
        x = gather(x, [b for b in stage if b != far])
    return gather(x, [core]), small[0]


def total_early(keep, send, bits, far, core):
    x = plus(keep, hop(send, core))
    part = x.shape[1] // 3
    first, second, rest = bits[0], bits[1], bits[2:]
    orders = ((far, first, second), (first, second, far), (second, far, first))
    chunks = [x[:, i * part : (i + 1) * part] for i in range(3)]
    for stage in range(3):
        chunks = [scatter_sum(chunk, [order[stage]], far) for chunk, order in zip(chunks, orders)]
    held = chunks[0].shape[1]
    x = jnp.concatenate(chunks, axis=2)
    for bit in rest:
        x = scatter_sum(x, [bit], far)
    x = x[0]
    for bit in reversed(rest):
        x = gather(x, [bit])
    width = x.shape[1] // 3
    two, one = x[:, : 2 * width], x[:, 2 * width :]
    two, one = gather(two, [second]), gather(one, [first])
    two, one = gather(two, [first]), gather(one, [second])
    x = jnp.concatenate([two[:, :width], two[:, width:], one], axis=0)
    return gather(x, [core])


def wipe(*refs):
    sems = refs[-1]
    count = sems.shape[0]
    outs, zeros = refs[1 : 1 + count], refs[1 + count : -1]
    for zero in zeros:
        zero[...] = jnp.zeros_like(zero)
    copies = []
    for i, out in enumerate(outs):
        src = next(z for z in zeros if z.dtype == out.dtype and z.shape[1] == out.shape[1])
        rows = out.shape[0]
        n = next(c for c in (256, 192, 128, 64, 32, 16) if rows % c == 0)
        for at in range(0, rows, n):
            copies.append(
                pltpu.make_async_copy(
                    src.at[pl.ds(0, n), :], out.at[pl.ds(at, n), :], sems.at[i]
                )
            )
    for copy in copies:
        copy.start()
    for copy in copies:
        copy.wait()


def moments(turned, m, v):
    first = BETA_ONE * m[...] + (1.0 - BETA_ONE) * turned
    second = BETA_TWO * v[...] + (1.0 - BETA_TWO) * (turned * turned)
    m[...] = first
    v[...] = second
    return (first / (jnp.sqrt(second) + EPS_ADAM)).astype(bf16)


def fetch(pairs, sems):
    copies = [pltpu.make_async_copy(a, b, sems.at[i]) for i, (a, b) in enumerate(pairs)]
    for copy in copies:
        copy.start()
    for copy in copies:
        copy.wait()


def step_wide(g, w, m, v, ql, qr, rate, scratch):
    low_l, low_r, mid, back = scratch
    low_l[...] = ql[...].astype(bf16)
    low_r[...] = qr[...].astype(bf16)
    blocks, size = qr.shape[0], qr.shape[1]
    mid[...] = nn(ql[...].T.astype(bf16), g).astype(bf16)
    for b in range(blocks):
        at = slice(b * size, (b + 1) * size)
        u = moments(nn(mid[:, at], low_r[b]), m.at[:, at], v.at[:, at])
        back[:, at] = nt(u, low_r[b]).astype(bf16)
    w[...] = w[...] - rate * nn(low_l[...], back[...])


def step_tall(g, w, m, v, ql, qr, rate, scratch):
    low_r, mid, back = scratch
    low_r[...] = qr[...].astype(bf16)
    blocks, size = ql.shape[0], ql.shape[1]
    for b in range(blocks):
        at = slice(b * size, (b + 1) * size)
        mid[at, :] = nn(ql[b].T.astype(bf16), g[at, :]).astype(bf16)
    u = moments(nn(mid[...], low_r[...]), m, v)
    back[...] = nt(u, low_r[...]).astype(bf16)
    for b in range(blocks):
        at = slice(b * size, (b + 1) * size)
        w[at, :] = w[at, :] - rate * nn(ql[b].astype(bf16), back[at, :])


def update_qkv(rate, mine, g, w_in, m_in, v_in, ql_in, qr_in, *refs):
    outs, (grad, new, mom, var, copy) = refs[:4], refs[4:9]
    w, m, v, c, ql, qr, low_l, low_r, mid, back, sems = refs[9:]
    for j in range(3):
        grad[j] = g[j].astype(f32)

        @pl.when(mine[j] == 1)
        def _():
            fetch(
                [(w_in.at[j], w), (m_in.at[j], m), (v_in.at[j], v), (ql_in.at[j], ql), (qr_in.at[j], qr)], sems
            )
            step_wide(g[j], w, m, v, ql, qr, rate, (low_l, low_r, mid, back))
            c[...] = w[...].astype(bf16)
            fetch([(w, new.at[j]), (m, mom.at[j]), (v, var.at[j]), (c, copy.at[j])], sems)


def update_rest(rate_out, rate_up, rate_down, mine, g_out, g_up, g_down_t, *refs):
    (wo_in, mo_in, vo_in, lo_in, ro_in, wu_in, mu_in, vu_in, lu_in, ru_in,
     wd_in, md_in, vd_in, ld_in, rd_in) = refs[:15]
    refs = refs[15 + 11 :]
    grad_o, grad_u, grad_d = refs[:3]
    new_o, moments_o, copy_o, new_u, mom_u, var_u, copy_u, new_d, mom_d, var_d, copy_d = refs[3:14]
    (wo, mo, vo, co, lo, ro, low_ro, mid_o, back_o,
     wu, mu, vu, cu, lu, ru, low_lu, low_ru, mid_u, back_u,
     wd, md, vd, cd, mid_d, back_d, sems) = refs[14:]
    grad_o[...] = g_out[...].astype(f32)
    grad_u[...] = g_up[...].astype(f32)
    grad_d[...] = g_down_t[...].astype(f32).T

    @pl.when(mine[3] == 1)
    def _():
        fetch([(wo_in, wo), (mo_in, mo), (vo_in, vo), (lo_in, lo), (ro_in, ro)], sems)
        step_tall(g_out[...], wo, mo, vo, lo, ro, rate_out, (low_ro, mid_o, back_o))
        co[...] = wo[...].astype(bf16)
        fetch([(wo, new_o), (mo, moments_o.at[0]), (vo, moments_o.at[1]), (co, copy_o)], sems)

    @pl.when(mine[4] == 1)
    def _():
        fetch([(wu_in, wu), (mu_in, mu), (vu_in, vu), (lu_in, lu), (ru_in, ru)], sems)
        step_wide(g_up[...], wu, mu, vu, lu, ru, rate_up, (low_lu, low_ru, mid_u, back_u))
        cu[...] = wu[...].astype(bf16)
        fetch([(wu, new_u), (mu, mom_u), (vu, var_u), (cu, copy_u)], sems)

    @pl.when(mine[5] == 1)
    def _():
        fetch([(wd_in, wd), (md_in, md), (vd_in, vd), (ld_in, ru), (rd_in, lu)], sems)
        step_tall(grad_d[...].astype(bf16), wd, md, vd, ru, lu, rate_down, (low_lu, mid_d, back_d))
        cd[...] = wd[...].astype(bf16)
        fetch([(wd, new_d), (md, mom_d), (vd, var_d), (cd, copy_d)], sems)


def three_parts(x):
    parts = []
    for _ in range(3):
        part = lax.reduce_precision(x, exponent_bits=8, mantissa_bits=7)
        parts.append(part.astype(bf16))
        x = x - part
    return parts


def pad_picks(picks):
    windows, heads, slots = picks.shape
    return jnp.pad(picks, ((0, 0), (0, 0), (0, SLOTS - slots)), constant_values=-1).reshape(
        windows, heads * SLOTS
    )


def per_device(
    tokens_in,
    cotangent,
    data_table,
    window_group,
    query_picks,
    owner_list,
    weight_qkv,
    head_bias,
    weight_out,
    weight_up,
    ff_bias,
    weight_down,
    norm_gains,
    shifts,
    first_qkv,
    second_qkv,
    first_out,
    second_out,
    first_up,
    second_up,
    first_down,
    second_down,
    basis_qkv_left,
    basis_qkv_right,
    basis_out_left,
    basis_out_right,
    basis_up_left,
    basis_up_right,
    basis_down_left,
    basis_down_right,
):
    head_count = lax.axis_size("head")
    head = lax.axis_index("head")
    my_rank = lax.axis_index("dp")
    rows, width = tokens_in.shape
    length = rows * head_count // window_group.shape[0]
    windows = rows // length
    head_dim = basis_qkv_right.shape[-1]
    cols = GROUP * head_dim
    scale = 1.0 / math.sqrt(head_dim)
    head_bits = head_count.bit_length() - 1
    far = ("head", head_bits - 1)
    core_bit = ("dp", 0)
    dp_bits = lax.axis_size("dp").bit_length() - 1
    bits = [("dp", k) for k in range(1, dp_bits)] + [("head", k) for k in range(head_bits - 1)]
    core = my_rank & 1

    groups = lax.dynamic_slice_in_dim(window_group, head * windows, windows, 0)
    info = jnp.concatenate([core[None], groups]).astype(jnp.int32)

    def half_of(x, dim, m):
        return lax.dynamic_slice_in_dim(x, m * (x.shape[dim] // 2), x.shape[dim] // 2, dim)

    def pack_qkv(w, hb, picks, m):
        w = half_of(w, 1, m).astype(bf16).reshape(-1, cols)
        extra = [jnp.pad(picks, ((0, 0), (0, cols - picks.shape[1]))).astype(bf16)]
        for j in range(2):
            extra += [p[None] for p in three_parts(hb[j])]
        extra = jnp.concatenate(extra, 0)
        return jnp.concatenate([w, jnp.pad(extra, ((0, -extra.shape[0] % 16), (0, 0)))], 0)

    def pack_rest(w_out, w_up, w_down, fb, m):
        w_up = half_of(w_up, 1 - 1, m).astype(bf16)
        hid = w_up.shape[1] // 2
        extra = jnp.concatenate([p.reshape(2, hid) for p in three_parts(fb)], 0)
        return jnp.concatenate(
            [
                half_of(w_out, 0, m).astype(bf16),
                w_up[:, :hid],
                w_up[:, hid:],
                half_of(w_down, 0, m).astype(bf16),
                jnp.pad(extra, ((0, 16 - extra.shape[0]), (0, 0))),
            ],
            0,
        )

    if head_count == 2:
        near = (weight_qkv, head_bias, weight_out, weight_up, ff_bias, weight_down)
        far_picks = lax.dynamic_slice_in_dim(query_picks, (1 - head) * windows, windows, 0)
        near_picks = pad_picks(lax.dynamic_slice_in_dim(query_picks, head * windows, windows, 0))
        qkv_y = hop(pack_qkv(weight_qkv, head_bias, pad_picks(far_picks), core), far)
        rest_near = pack_rest(weight_out, weight_up, weight_down, ff_bias, core)
        rest_near, qkv_y = lax.optimization_barrier((rest_near, qkv_y))
        rest_y = hop(rest_near, far)
        qkv_c = hop(qkv_y, core_bit)
        rest_c = hop(rest_y, core_bit)
    else:
        def whole_of(x, dim):
            return lax.all_gather(x, "head", axis=dim, tiled=True)

        def pick_group(x, dim, g):
            n = x.shape[dim] // 2
            return lax.dynamic_slice_in_dim(x, (side(far) ^ g) * n, n, dim)

        whole = [
            (whole_of(weight_qkv.astype(bf16), 2).astype(f32), 2),
            (whole_of(head_bias, 1), 1),
            (whole_of(weight_out.astype(bf16), 0).astype(f32), 0),
            (whole_of(weight_up.astype(bf16), 1).astype(f32), 1),
            (whole_of(ff_bias, 0), 0),
            (whole_of(weight_down.astype(bf16), 0).astype(f32), 0),
        ]
        near = [pick_group(x, d, 0) for x, d in whole]
        away = [pick_group(x, d, 1) for x, d in whole]
        picks = lax.dynamic_slice_in_dim(whole_of(query_picks, 1), head * windows, windows, 0)
        near_picks = pad_picks(pick_group(picks, 1, 0))
        far_picks = pad_picks(pick_group(picks, 1, 1))
        qkv_y, qkv_c = (pack_qkv(away[0], away[1], far_picks, m) for m in (core, 1 - core))
        rest_y, rest_c = (pack_rest(away[2], away[3], away[5], away[4], m) for m in (core, 1 - core))
    n_qkv, n_bias, n_out, n_up, n_ff, n_down = near
    hid = n_up.shape[1]
    extra_rows = qkv_y.shape[0] - 3 * (width // 2)
    pick_rows = windows
    slots = GROUP * SLOTS

    near_bias = jnp.stack([n_bias[0], jnp.zeros_like(n_bias[0]), n_bias[1]])
    near_picks = near_picks.astype(f32)

    seen = [
        ((rows, cols), bf16, VMEM),
        ((rows, cols), bf16, VMEM),
        ((rows, cols), bf16, VMEM),
        ((rows, cols), bf16, VMEM),
        ((windows, slots, length), f32, VMEM),
        ((windows, slots, cols), bf16, VMEM),
        ((3, width, cols), bf16, VMEM),
    ]

    def own(*refs):
        attend_own(windows, length, scale, *refs)

    q0, k0, v0, ctx0, att0, picked0, wq0, emb, picks0 = call(
        own,
        seen + [((rows, width), bf16, VMEM), ((pick_rows, slots), f32, VMEM)],
        [SMEM, VMEM, VMEM, VMEM, VMEM, VMEM],
        (info, tokens_in, data_table, n_qkv, near_bias, near_picks),
        [],
        24,
        9 * US,
        6e6,
    )

    def away_body(*refs):
        attend_far(windows, length, scale, *refs)

    q1, k1, v1, ctx1, att1, picked1, wq1, picks1 = call(
        away_body,
        seen + [((pick_rows, slots), f32, VMEM)],
        [SMEM, VMEM, HBM, HBM],
        (info, emb, qkv_y, qkv_c),
        [
            pltpu.VMEM((extra_rows, cols), bf16),
            pltpu.VMEM((3, cols), f32),
            pltpu.SemaphoreType.DMA((7,)),
        ],
        24,
        9 * US,
        6e6,
    )

    block = 2 * length
    buf_rows = 2 * hid + cols

    def ff_body(*refs):
        feed_forward(length, block, *refs)

    output_rows, gp1, ga, keep_one, send_one, sums, wo = call(
        ff_body,
        [
            ((rows, width), f32, VMEM),
            ((rows, width), f32, VMEM),
            ((rows, width), bf16, VMEM),
            ((2, buf_rows // 2, width), bf16, HBM),
            ((2, buf_rows // 2, width), bf16, HBM),
            ((16, width), f32, VMEM),
            ((2, cols, width), bf16, VMEM),
        ],
        [SMEM, VMEM, VMEM, VMEM, VMEM, VMEM, HBM, HBM] + [VMEM] * 6,
        (info, tokens_in, data_table, ctx0, ctx1, n_out, rest_y, rest_c, n_up, n_down,
         n_ff[None], norm_gains, shifts, cotangent),
        [
            pltpu.VMEM((2, width, hid), bf16),
            pltpu.VMEM((2, hid, width), bf16),
            pltpu.VMEM((rows, 2 * hid), bf16),
            pltpu.VMEM((rows, 2 * hid), bf16),
            pltpu.VMEM((block, 2 * hid), bf16),
            pltpu.VMEM((rows, width), bf16),
            pltpu.VMEM((rows, width), bf16),
            pltpu.VMEM((width, rows), bf16),
            pltpu.VMEM((width, rows), bf16),
            pltpu.VMEM((block, width), f32),
            pltpu.VMEM((2, hid), f32),
            pltpu.VMEM((16, width), bf16),
            pltpu.VMEM((2, buf_rows, width), bf16),
            pltpu.SemaphoreType.DMA((9,)),
        ],
        56,
        32 * US,
        20e6,
    )

    def back_body(*refs):
        attend_back(windows, length, scale, *refs)

    half = width // 2
    keep_two_rows = 3 * half // 2 + 16
    gq, gk, gv, keep_two, send_two = call(
        back_body,
        [
            ((rows, width), bf16, VMEM),
            ((rows, width), bf16, VMEM),
            ((rows, width), bf16, VMEM),
            ((2, keep_two_rows, width), bf16, HBM),
            ((2, keep_two_rows, width), bf16, HBM),
        ],
        [SMEM] + [VMEM] * 16,
        (info, ga, emb, wo, sums, k0, v0, att0, picked0, picks0, wq0,
         k1, v1, att1, picked1, picks1, wq1),
        [
            pltpu.VMEM((rows, width), bf16),
            pltpu.VMEM((width, rows), bf16),
            pltpu.VMEM((16, width), f32),
            pltpu.VMEM((2, 3 * half + 16, width), bf16),
            pltpu.VMEM((2, 16, width), f32),
            pltpu.SemaphoreType.DMA((8,)),
        ],
        40,
        14 * US,
        10e6,
    )
    (grad_rows,) = call(
        input_grad,
        [((rows, width), f32, VMEM)],
        [VMEM] * 6,
        (gq, gk, gv, wq0, wq1, gp1),
        [],
        24,
        4 * US,
        8e6,
    )

    shards = head_count // 2
    mine = head % shards

    def shard(x, dim):
        n = x.shape[dim] // shards
        return x if shards == 1 else lax.dynamic_slice_in_dim(x, mine * n, n, dim)

    blanks = []
    for like in (first_qkv, first_qkv, first_qkv, first_qkv):
        blanks.append((like.shape[0] * like.shape[1], like.shape[2]))
    blanks += [first_out.shape, (2 * first_out.shape[0], width), first_out.shape]
    blanks += [first_up.shape] * 4 + [first_down.shape] * 4
    kinds = [f32, f32, f32, bf16, f32, f32, bf16, f32, f32, f32, bf16, f32, f32, f32, bf16]
    widths = sorted({s[1] for s in blanks})
    blanks = call(
        wipe,
        [(s, k, HBM) for s, k in zip(blanks, kinds)],
        [VMEM],
        (sums,),
        [pltpu.VMEM((256, n), k) for n in widths for k in (f32, bf16)]
        + [pltpu.SemaphoreType.DMA((len(blanks),))],
        8,
        8 * US,
        20e6,
    )
    shapes = [(3, width, first_qkv.shape[2])] * 4
    shapes += [first_out.shape, (2,) + first_out.shape, first_out.shape]
    shapes += [first_up.shape] * 4 + [first_down.shape] * 4
    blanks = [x.reshape(s) for x, s in zip(blanks, shapes)]
    owned = (owner_list == my_rank).astype(jnp.int32)

    sum_one = total_early(keep_one, send_one, bits, far, core_bit)
    g_up = shard(jnp.concatenate([sum_one[:width], sum_one[width : 2 * width]], 1), 1)
    g_down_t = shard(
        jnp.concatenate([sum_one[2 * width : 3 * width], sum_one[3 * width : 4 * width]], 1), 1
    )
    g_out = shard(sum_one[4 * width :], 0)
    rate_wide = width ** (-0.5)
    rate_out = max(width // head_dim, 1) ** (-0.5)
    rate_down = (n_down.shape[0] * 2) ** (-0.5)

    def rest_body(*refs):
        update_rest(rate_out, rate_wide, rate_down, *refs)

    tall, wide, low = first_out.shape, first_up.shape, first_down.shape
    rest_outs = call(
        rest_body,
        [(tall, f32, VMEM), (wide, f32, VMEM), (low, f32, VMEM)]
        + [(x.shape, x.dtype, HBM) for x in blanks[4:]],
        [SMEM, VMEM, VMEM, VMEM] + [HBM] * (15 + 11),
        (owned, g_out, g_up, g_down_t,
         weight_out, first_out, second_out, basis_out_left, basis_out_right,
         weight_up, first_up, second_up, basis_up_left, basis_up_right,
         weight_down, first_down, second_down, basis_down_left, basis_down_right, *blanks[4:]),
        [pltpu.VMEM(tall, f32)] * 3
        + [
            pltpu.VMEM(tall, bf16),
            pltpu.VMEM(basis_out_left.shape, f32),
            pltpu.VMEM(basis_out_right.shape, f32),
            pltpu.VMEM(basis_out_right.shape, bf16),
            pltpu.VMEM(tall, bf16),
            pltpu.VMEM(tall, bf16),
        ]
        + [pltpu.VMEM(wide, f32)] * 3
        + [
            pltpu.VMEM(wide, bf16),
            pltpu.VMEM(basis_up_left.shape, f32),
            pltpu.VMEM(basis_up_right.shape, f32),
            pltpu.VMEM(basis_up_left.shape, bf16),
            pltpu.VMEM(basis_up_right.shape, bf16),
            pltpu.VMEM(wide, bf16),
            pltpu.VMEM(wide, bf16),
        ]
        + [pltpu.VMEM(low, f32)] * 3
        + [pltpu.VMEM(low, bf16)] * 3
        + [pltpu.SemaphoreType.DMA((5,))],
        48,
        12 * US,
        20e6,
        {4 + 15 + i: 3 + i for i in range(11)},
    )
    grad_out_all, grad_up_all, grad_down_all = rest_outs[:3]

    sum_two, small = total_late(keep_two, send_two, 16, bits, far, core_bit)
    pairs = sum_two.reshape(3, half, width)
    g_qkv = shard(jnp.concatenate([pairs[:, :, :cols], pairs[:, :, cols:]], 1), 2)
    small = small.astype(f32)
    grad_table_all = small[0:2]
    grad_gains_all = small[2:4]
    grad_shifts_all = small[4:8]
    grad_ff_all = shard(small[8:10].reshape(-1), 0)
    grad_bias_all = shard(small[10].reshape(2, cols), 1)

    def qkv_body(*refs):
        update_qkv(rate_wide, *refs)

    one = first_qkv.shape[1:]
    qkv_outs = call(
        qkv_body,
        [(first_qkv.shape, f32, VMEM)] + [(x.shape, x.dtype, HBM) for x in blanks[:4]],
        [SMEM, VMEM] + [HBM] * 9,
        (owned, g_qkv, weight_qkv, first_qkv, second_qkv, basis_qkv_left, basis_qkv_right, *blanks[:4]),
        [pltpu.VMEM(one, f32)] * 3
        + [
            pltpu.VMEM(one, bf16),
            pltpu.VMEM(basis_qkv_left.shape[1:], f32),
            pltpu.VMEM(basis_qkv_right.shape[1:], f32),
            pltpu.VMEM(basis_qkv_left.shape[1:], bf16),
            pltpu.VMEM(basis_qkv_right.shape[1:], bf16),
            pltpu.VMEM(one, bf16),
            pltpu.VMEM(one, bf16),
            pltpu.SemaphoreType.DMA((5,)),
        ],
        24,
        6 * US,
        8e6,
        {7 + i: 1 + i for i in range(4)},
    )
    return (
        output_rows,
        grad_rows,
        grad_table_all,
        grad_gains_all,
        grad_shifts_all,
        grad_bias_all,
        grad_ff_all,
        qkv_outs[0],
        grad_out_all,
        grad_up_all,
        grad_down_all,
        *(x[None] for x in qkv_outs[1:]),
        *(x[None] for x in rest_outs[3:]),
    )


def solution(mesh):
    in_specs = (
        P(("dp", "head"), None),
        P(("dp", "head"), None),
        P(),
        P("dp"),
        P("dp", "head", None),
        P(),
        P(None, None, "head"),
        P(None, "head"),
        P("head", None),
        P(None, "head"),
        P("head"),
        P("head", None),
        P(),
        P(),
        P(None, None, "head"),
        P(None, None, "head"),
        P("head", None),
        P("head", None),
        P(None, "head"),
        P(None, "head"),
        P("head", None),
        P("head", None),
        P(),
        P(None, "head", None, None),
        P("head", None, None),
        P(),
        P(),
        P("head", None, None),
        P("head", None, None),
        P(),
    )
    out_specs = (
        P(("dp", "head"), None),
        P(("dp", "head"), None),
        P(),
        P(),
        P(),
        P(None, "head"),
        P("head"),
        P(None, None, "head"),
        P("head", None),
        P(None, "head"),
        P("head", None),
        P("dp", None, None, "head"),
        P("dp", None, None, "head"),
        P("dp", None, None, "head"),
        P("dp", None, None, "head"),
        P("dp", "head", None),
        P("dp", None, "head", None),
        P("dp", "head", None),
        P("dp", None, "head"),
        P("dp", None, "head"),
        P("dp", None, "head"),
        P("dp", None, "head"),
        P("dp", "head", None),
        P("dp", "head", None),
        P("dp", "head", None),
        P("dp", "head", None),
    )
    return jax.shard_map(
        per_device, mesh=mesh, in_specs=in_specs, out_specs=out_specs, check_vma=False
    )
```

```python
import math

import jax
import jax.numpy as jnp
from jax import lax
from jax.experimental import pallas as pl
from jax.experimental.pallas import tpu as pltpu
from jax.sharding import PartitionSpec as P

f32 = jnp.float32
bf16 = jnp.bfloat16

NDATA = 2
EPS_NORM = 1e-05
EPS_ADAM = 1e-08
BETA_ONE = 0.5
BETA_TWO = 0.5

GROUP = 4
SLOTS = 32
MB = 1 << 20


def nn(a, b):
    return jnp.dot(a, b, preferred_element_type=f32)


def nt(a, b):
    return lax.dot_general(a, b, (((1,), (1,)), ((), ())), preferred_element_type=f32)


def col_sum(x):
    return jnp.sum(x, axis=0, keepdims=True)


def row_mean(x):
    return jnp.mean(x, axis=-1, keepdims=True)


VMEM = pl.BlockSpec(memory_space=pltpu.VMEM)
SMEM = pl.BlockSpec(memory_space=pltpu.SMEM)
HBM = pl.BlockSpec(memory_space=pl.ANY)
FAR = pl.BlockSpec(memory_space=pl.ANY)


def whole(*shape):
    return pl.BlockSpec(shape, lambda i: (0,) * len(shape))


def cut(*shape):
    return pl.BlockSpec(shape, lambda i: (i,) + (0,) * (len(shape) - 1))


US = 1_000_000_000


def in_hbm(x, spec):
    if spec is SMEM or spec is HBM or x.size * x.dtype.itemsize < 1 << 16:
        return x
    return pltpu.with_memory_space_constraint(x, pltpu.HBM)


def call(body, outs, ins, args, scratch, limit, flops, nbytes, aliases={}, grid=(), hbm_in=True, hbm_out=True):
    if hbm_in:
        args = [in_hbm(x, spec) for x, spec in zip(args, ins)]
    kind = pltpu.HBM if hbm_out else jax.ShapeDtypeStruct
    return pl.pallas_call(
        body,
        grid=grid,
        out_shape=tuple(kind(s, d) for s, d, _ in outs),
        in_specs=ins,
        out_specs=tuple(spec for _, _, spec in outs),
        scratch_shapes=scratch,
        input_output_aliases=aliases,
        compiler_params=pltpu.CompilerParams(vmem_limit_bytes=limit * MB),
        cost_estimate=pl.CostEstimate(
            flops=int(flops), bytes_accessed=int(nbytes), transcendentals=0
        ),
    )(*args)


def head_mask(cols):
    width = cols // GROUP
    shape = (GROUP * SLOTS, cols)
    return (
        lax.broadcasted_iota(jnp.int32, shape, 0) // SLOTS
        == lax.broadcasted_iota(jnp.int32, shape, 1) // width
    )


def one_hot(picks, w, length):
    row = picks[pl.ds(w, 1), :]
    spots = lax.broadcasted_iota(jnp.int32, (length, GROUP * SLOTS), 0).astype(f32)
    columns = (spots == row).astype(f32)
    return columns.astype(bf16), columns.T.astype(bf16)


def copy_all(pairs, sems):
    copies = [pltpu.make_async_copy(a, b, sems.at[i]) for i, (a, b) in enumerate(pairs)]
    for copy in copies:
        copy.start()
    return copies


def split_sum(parts, at):
    return parts[at : at + 1] + parts[at + 1 : at + 2] + parts[at + 2 : at + 3]


def put_parts(extra, at, row):
    for i in range(3):
        part = row.astype(bf16).astype(f32)
        extra[at + i : at + i + 1, :] = part
        row = row - part


def pack_qkv(windows, info, w, bias, picks, piece, low, extra):
    core = info[0]
    half = w.shape[1] // 2
    for j in range(3):
        low[j] = w[j].astype(bf16)
        piece[j * half : (j + 1) * half, :] = w[j, pl.ds(pl.multiple_of(core * half, half), half), :].astype(bf16)
    extra[...] = jnp.zeros_like(extra)
    for i in range(windows):
        extra[i : i + 1, : GROUP * SLOTS] = picks[pl.ds(info[2] + i, 1), :]
    put_parts(extra, windows, bias[0:1, :])
    put_parts(extra, windows + 3, bias[1:2, :])
    piece[3 * half :, :] = extra[...].astype(bf16)


def pack_rest(info, w_out, w_up, w_down, bias, piece, down_piece, low, down_low, extra):
    hid = w_up.shape[1] // 2
    n_out, n_up, n_down = w_out.shape[0] // 2, w_up.shape[0] // 2, w_down.shape[0] // 2
    extra[...] = jnp.zeros_like(extra)
    put_parts(extra, 0, bias[:, :hid])
    put_parts(extra, 3, bias[:, hid:])
    for m in range(2):
        low[m, :n_out, :] = w_out[m * n_out : (m + 1) * n_out, :].astype(bf16)
        for h in range(2):
            at = n_out + h * n_up
            low[m, at : at + n_up, :] = w_up[
                m * n_up : (m + 1) * n_up, h * hid : (h + 1) * hid
            ].astype(bf16)
        low[m, low.shape[1] - 16 :, :] = extra[...].astype(bf16)
    down_low[...] = w_down[...].astype(bf16)
    piece[...] = low[info[0]]
    down_piece[...] = down_low[pl.ds(pl.multiple_of(info[0] * n_down, n_down), n_down), :]


def attend(wq, bias, picks, start, emb, q_out, k_out, v_out, ctx, att, picked, length, scale):
    cols = wq.shape[2]
    e = emb[...]
    for j, out in enumerate((q_out, k_out, v_out)):
        out[...] = (nn(e, wq[j]) + bias[j]).astype(bf16)
    mask = head_mask(cols)
    mask_low = mask.astype(f32).astype(bf16)
    for i in range(emb.shape[0] // length):
        here = slice(i * length, (i + 1) * length)
        up, down = one_hot(picks, start + i, length)
        q, k, v = q_out[here, :], k_out[here, :], v_out[here, :]
        sel = jnp.where(mask, nn(down, q), 0.0).astype(bf16)
        scores = nt(sel, k) * scale
        exponent = jnp.exp(scores - jnp.max(scores, axis=-1, keepdims=True))
        probs = exponent / jnp.sum(exponent, axis=-1, keepdims=True)
        mixed = jnp.where(mask, nn(probs.astype(bf16), v), 0.0).astype(bf16)
        mean = col_sum(v.astype(f32)) * (1.0 / length)
        active = nn(up, mask_low)
        ctx[here, :] = (nn(up, mixed) + (1.0 - active) * mean).astype(bf16)
        att[i] = probs
        picked[i] = sel


def attend_own(length, scale, info, groups, tokens, table, wq, bias, picks,
               q, k, v, ctx, att, picked, emb):
    per = tokens.shape[0] // length
    first = pl.program_id(0) * per
    for i in range(per):
        here = slice(i * length, (i + 1) * length)
        row = table[pl.ds(groups[info[3] + first + i], 1), :]
        emb[here, :] = (tokens[here, :].astype(f32) + row).astype(bf16)
    rows = (bias[0:1, :], jnp.zeros_like(bias[0:1, :]), bias[1:2, :])
    attend(wq, rows, picks, info[1] + first, emb, q, k, v, ctx, att, picked, length, scale)


def attend_far(length, scale, info, emb, y_piece, c_piece,
               q, k, v, ctx, att, picked, wq, picks, extra, bias, sems):
    core = info[0]
    half = wq.shape[1] // 2
    windows = picks.shape[0]

    @pl.when(pl.program_id(0) == 0)
    def _():
        pairs = [(y_piece.at[pl.ds(3 * half, extra.shape[0]), :], extra)]
        for j in range(3):
            for piece, spot in ((y_piece, core), (c_piece, 1 - core)):
                pairs.append(
                    (
                        piece.at[pl.ds(j * half, half), :],
                        wq.at[j, pl.ds(pl.multiple_of(spot * half, half), half), :],
                    )
                )
        for copy in copy_all(pairs, sems):
            copy.wait()
        rest = extra[...].astype(f32)
        picks[...] = rest[:windows, : GROUP * SLOTS]
        bias[0:1, :] = split_sum(rest, windows)
        bias[1:2, :] = split_sum(rest, windows + 3)

    rows = (bias[0:1, :], jnp.zeros_like(bias[0:1, :]), bias[1:2, :])
    first = pl.program_id(0) * (emb.shape[0] // length)
    attend(wq, rows, picks, first, emb, q, k, v, ctx, att, picked, length, scale)


def gelu_pair(x):
    bell = jnp.exp(-0.5 * (x * x))
    t = 1.0 / (1.0 + (0.3275911 * math.sqrt(0.5)) * jnp.abs(x))
    poly = t * (
        0.5 * 0.254829592
        + t * (0.5 * -0.284496736 + t * (0.5 * 1.421413741 + t * (0.5 * -1.453152027 + t * (0.5 * 1.061405429))))
    )
    tail = poly * bell
    phi = jnp.where(x >= 0.0, 1.0 - tail, tail)
    return x * phi, phi + x * bell * (1.0 / math.sqrt(2.0 * math.pi))


def ff_in(length, info, groups, tokens, table, ctx0, ctx1, near, y_piece, c_piece, ff_bias, gains, shifts,
          resid, act, slope, wo, up, pre, ffb, extra, sems):
    core = info[0]
    step = pl.program_id(0)
    block, width = tokens.shape
    cols = wo.shape[1]
    half = up.shape[2] // 2
    per = block // length

    @pl.when(step == 0)
    def _():
        pairs = [(y_piece.at[pl.ds(y_piece.shape[0] - 16, 16), :], extra)]
        for g, piece, spot in (
            (0, near.at[0], 0), (0, near.at[1], 1), (1, y_piece, core), (1, c_piece, 1 - core)
        ):
            n = cols // 2
            pairs.append(
                (piece.at[pl.ds(0, n), :], wo.at[g, pl.ds(pl.multiple_of(spot * n, n), n), :])
            )
            at, n = n, width // 2
            for h in range(2):
                pairs.append(
                    (
                        piece.at[pl.ds(at + h * n, n), :],
                        up.at[g, pl.ds(pl.multiple_of(spot * n, n), n), pl.ds(h * half, half)],
                    )
                )
        copies = copy_all(pairs, sems)
        ffb[0:1, :] = ff_bias[...]
        for copy in copies:
            copy.wait()
        rest = extra[...].astype(f32)
        ffb[1:2, :half] = split_sum(rest, 0)
        ffb[1:2, half:] = split_sum(rest, 3)

    for i in range(per):
        part = slice(i * length, (i + 1) * length)
        pre[part, :] = tokens[part, :].astype(f32) + table[pl.ds(groups[info[3] + step * per + i], 1), :]
    x = pre[...] + (nn(ctx0[...], wo[0]) + nn(ctx1[...], wo[1]) + shifts[0:1, :])
    resid[...] = x
    center = x - row_mean(x)
    unit = center * lax.rsqrt(row_mean(center * center) + EPS_NORM)
    low = (unit * gains[0:1, :] + shifts[2:3, :]).astype(bf16)
    for ch in range(4):
        g, o = ch // 2, (ch % 2) * half
        z = nn(low, up[g, :, o : o + half]) + ffb[g : g + 1, o : o + half]
        a, d = gelu_pair(z)
        act[:, ch * half : (ch + 1) * half] = a.astype(bf16)
        slope[:, ch * half : (ch + 1) * half] = d.astype(bf16)


def ff_back(length, info, groups, resid, act_in, slope, up, near, y_piece, c_piece, gains, shifts, cot, ctx0, ctx1,
            out, gp1, ga, keep, send, sums,
            dn, act, gpre, nl, gb, ga_all, nl_t, gb_t, buf, sems, act_sems):
    core = info[0]
    step = pl.program_id(0)
    block, width = resid.shape
    rows = nl.shape[0]
    cols = ctx0.shape[1]
    hid = up.shape[2]
    half = hid // 2
    per = block // length
    blocks = rows // block
    act_copies = [
        pltpu.make_async_copy(
            act_in.at[pl.ds(i * block, block), :], act.at[pl.ds(i * block, block), :], act_sems.at[i]
        )
        for i in range(blocks)
    ]

    @pl.when(step == 0)
    def _():
        n = hid // 2
        pairs = [
            (near, dn.at[0]),
            (y_piece, dn.at[1, pl.ds(pl.multiple_of(core * n, n), n), :]),
            (c_piece, dn.at[1, pl.ds(pl.multiple_of((1 - core) * n, n), n), :]),
        ]
        copies = copy_all(pairs, sems)
        for copy in act_copies:
            copy.start()
        sums[...] = jnp.zeros_like(sums)
        for copy in copies:
            copy.wait()

    for i, copy in enumerate(act_copies):

        @pl.when(step == i)
        def _(copy=copy):
            copy.wait()

    here = pl.ds(pl.multiple_of(step * block, 32), block)
    x = resid[...]
    center = x - row_mean(x)
    inv_one = lax.rsqrt(row_mean(center * center) + EPS_NORM)
    unit_one = center * inv_one
    normed = unit_one * gains[0:1, :] + shifts[2:3, :]
    nl[here, :] = normed.astype(bf16)
    branch = shifts[1:2, :]
    for g in range(2):
        branch = branch + nn(act[here, g * hid : (g + 1) * hid], dn[g])
    y = normed + branch
    center = y - row_mean(y)
    inv_two = lax.rsqrt(row_mean(center * center) + EPS_NORM)
    unit_two = center * inv_two
    out[...] = unit_two * gains[1:2, :] + shifts[3:4, :]
    c = cot[...]
    sums[1:2, :] += col_sum(c * unit_two)
    sums[5:6, :] += col_sum(c)
    g2 = c * gains[1:2, :]
    gp2 = (g2 - row_mean(g2) - unit_two * row_mean(g2 * unit_two)) * inv_two
    low = gp2.astype(bf16)
    gb[here, :] = low
    sums[3:4, :] += col_sum(low.astype(f32))
    total = gp2
    for ch in range(4):
        g, o = ch // 2, (ch % 2) * half
        p = nt(low, dn[g, o : o + half, :]) * slope[:, ch * half : (ch + 1) * half].astype(f32)
        p = p.astype(bf16)
        gpre[here, ch * half : (ch + 1) * half] = p
        sums[6 + ch : 7 + ch, :] += col_sum(p.astype(f32))
        total = total + nt(p, up[g, :, o : o + half])
    sums[0:1, :] += col_sum(total * unit_one)
    sums[4:5, :] += col_sum(total)
    g1 = total * gains[0:1, :]
    gp = (g1 - row_mean(g1) - unit_one * row_mean(g1 * unit_one)) * inv_one
    gp1[...] = gp
    low = gp.astype(bf16)
    ga[...] = low
    ga_all[here, :] = low
    sums[2:3, :] += col_sum(low.astype(f32))
    for i in range(per):
        spot = pl.ds(10 + groups[info[3] + step * per + i], 1)
        sums[spot, :] += col_sum(gp[i * length : (i + 1) * length, :])

    @pl.when(step == blocks - 1)
    def _():
        nl_t[...] = nl[...].astype(f32).T.astype(bf16)
        gb_t[...] = gb[...].astype(f32).T.astype(bf16)
        for ch in range(4):
            g, o = ch // 2, (ch % 2) * half
            at = slice(ch * half, (ch + 1) * half)
            buf[g, o : o + half, :] = nn(nl_t[...], gpre[:, at]).astype(bf16)
            buf[g, hid + o : hid + o + half, :] = nn(gb_t[...], act[:, at]).astype(bf16)
        for g, ctx in enumerate((ctx0, ctx1)):
            buf[g, 2 * hid : 2 * hid + cols, :] = nn(
                ctx[...].astype(f32).T.astype(bf16), ga_all[...]
            ).astype(bf16)
        n = buf.shape[1] // 2
        pairs = []
        for g in range(2):
            for dst, spot in ((keep, core), (send, 1 - core)):
                pairs.append((buf.at[g, pl.ds(pl.multiple_of(spot * n, 32), n), :], dst.at[g]))
        for copy in copy_all(pairs, sems):
            copy.wait()


def attend_back(length, scale, info, groups, ga, emb, wo, sums, picks0, picks1, wq0, wq1,
                k0, v0, att0, picked0, k1, v1, att1, picked1,
                gq, gk, gv, keep, send,
                gq_all, gk_all, gv_all, emb_all, wq0_all, wq1_all, emb_t, tsum, buf, small, sems):
    core = info[0]
    step = pl.program_id(0)
    rows, width = emb.shape
    block = ga.shape[0]
    per = block // length
    cols = wq0.shape[2]
    mask = head_mask(cols)
    mask_low = mask.astype(f32).astype(bf16)

    late = [
        pltpu.make_async_copy(a, b, sems.at[8 + i])
        for i, (a, b) in enumerate(((emb, emb_all), (wq0, wq0_all), (wq1, wq1_all)))
    ]

    @pl.when(step == 0)
    def _():
        for copy in late:
            copy.start()
        tsum[...] = jnp.zeros_like(tsum)

    e = ga[...]
    sides = ((k0, v0, att0, picked0, picks0, info[1]), (k1, v1, att1, picked1, picks1, 0))
    for g, (k_in, v_in, att, picked, picks, start) in enumerate(sides):
        at = slice(g * cols, (g + 1) * cols)
        g_ctx = nt(e, wo[g]).astype(bf16)
        for i in range(per):
            here = slice(i * length, (i + 1) * length)
            up, down = one_hot(picks, start + step * per + i, length)
            k, v = k_in[here, :], v_in[here, :]
            gc = g_ctx[here, :]
            ge = jnp.where(mask, nn(down, gc), 0.0).astype(bf16)
            active = nn(up, mask_low)
            gmean = col_sum((1.0 - active) * gc.astype(f32)) * (1.0 / length)
            probs = att[i]
            gprobs = nt(ge, v)
            low_t = probs.T.astype(bf16)
            g_value = (nn(low_t, ge) + gmean).astype(bf16)
            weighted = probs * gprobs
            graw = (weighted - probs * jnp.sum(weighted, axis=-1, keepdims=True)) * scale
            g_key = nn(graw.T.astype(bf16), picked[i]).astype(bf16)
            gpick = jnp.where(mask, nn(graw.astype(bf16), k), 0.0).astype(bf16)
            g_query = nn(up, gpick).astype(bf16)
            rows_here = pl.ds(pl.multiple_of(step * block + i * length, 32), length)
            group = groups[info[3] + step * per + i]
            for j, (x, dst, dst_all) in enumerate(
                ((g_query, gq, gq_all), (g_key, gk, gk_all), (g_value, gv, gv_all))
            ):
                dst[here, at] = x
                dst_all[rows_here, at] = x
                tsum[pl.ds(2 * j + group, 1), at] += col_sum(x.astype(f32))

    @pl.when(step == rows // block - 1)
    def _():
        for copy in late:
            copy.wait()
        emb_t[...] = emb_all[...].astype(f32).T.astype(bf16)
        half = width // 2
        for g in range(2):
            at = slice(g * cols, (g + 1) * cols)
            for j, x in enumerate((gq_all, gk_all, gv_all)):
                r = nn(emb_t[...], x[:, at]).astype(bf16)
                buf[g, j * half : (j + 1) * half, :cols] = r[:half]
                buf[g, j * half : (j + 1) * half, cols:] = r[half:]
        total = jnp.zeros((8, width), f32)
        for j in range(3):
            for g, wq in enumerate((wq0_all, wq1_all)):
                x = tsum[2 * j : 2 * j + 8, g * cols : (g + 1) * cols]
                hi = x.astype(bf16)
                lo = (x - hi.astype(f32)).astype(bf16)
                total = total + nt(hi, wq[j]) + nt(lo, wq[j])
        for g in range(2):
            at = slice(g * cols, (g + 1) * cols)
            small[g] = jnp.zeros_like(small[g])
            small[g, 0:2, :] = total[0:2] + sums[10:12, :]
            small[g, 2:8, :] = sums[0:6, :]
            small[g, 8:10, :] = sums[6 + 2 * g : 8 + 2 * g, :]
            small[g, 10:11, :cols] = tsum[0:1, at] + tsum[1:2, at]
            small[g, 10:11, cols:] = tsum[4:5, at] + tsum[5:6, at]
            buf[g, 3 * half : 3 * half + 16, :] = small[g].astype(bf16)
        n = 3 * half // 2
        pairs = []
        for g in range(2):
            for dst, spot in ((keep, core), (send, 1 - core)):
                pairs.append((buf.at[g, pl.ds(pl.multiple_of(spot * n, 32), n), :], dst.at[g, pl.ds(0, n), :]))
                pairs.append((buf.at[g, pl.ds(2 * n, 16), :], dst.at[g, pl.ds(n, 16), :]))
        for copy in copy_all(pairs, sems):
            copy.wait()


def input_grad(gq, gk, gv, wq0, wq1, gp1, out):
    cols = wq0.shape[2]
    total = gp1[...]
    for j, x in enumerate((gq, gk, gv)):
        for g, wq in enumerate((wq0, wq1)):
            total = total + nt(x[:, g * cols : (g + 1) * cols], wq[j])
    out[...] = total


def hop(x, *bits):
    heads = lax.axis_size("head")
    flip = sum((1 << k) * (heads if axis == "dp" else 1) for axis, k in bits)
    count = lax.axis_size("dp") * heads
    return lax.ppermute(x, ("dp", "head"), [(i, i ^ flip) for i in range(count)])


def side(bit):
    axis, k = bit
    return (lax.axis_index(axis) >> k) & 1


def subsets(bits):
    return [[b for i, b in enumerate(bits) if (r >> i) & 1] for r in range(1 << len(bits))]


def pair_sum(terms):
    while len(terms) > 1:
        terms = [terms[i] + terms[i + 1] for i in range(0, len(terms), 2)]
    return terms[0]


def pick(x, bits, far, flips):
    for bit in bits:
        flipped = bit in flips
        if bit == far:
            x = x[1:] if flipped else x[:1]
        else:
            n = x.shape[1] // 2
            x = lax.dynamic_slice_in_dim(x, (side(bit) ^ int(flipped)) * n, n, 1)
    return x


def scatter_sum(x, bits, far, small=None):
    terms, rest = [], []
    for flips in subsets(bits):
        part = pick(x, bits, far, flips)
        if small is not None:
            part = jnp.concatenate([part, pick(small, [far] if far in bits else [], far, flips)], 1)
        if flips:
            part = hop(part, *flips)
        terms.append(part.astype(f32))
    total = pair_sum(terms).astype(bf16)
    if small is None:
        return total
    n = total.shape[1] - small.shape[1]
    return total[:, :n], total[:, n:]


def gather(x, bits):
    parts = {}
    for r, flips in enumerate(subsets(bits)):
        parts[r] = hop(x, *flips) if flips else x
    for i, bit in enumerate(bits):
        m = side(bit) == 0
        parts = {
            r: jnp.where(m, parts[r], parts[r ^ (1 << i)]) for r in parts
        }
    order = sorted(parts, key=lambda r: [(r >> i) & 1 for i in range(len(bits))])
    return jnp.concatenate([parts[r] for r in order], axis=0)


def plus(a, b):
    return (a.astype(f32) + b.astype(f32)).astype(bf16)


def late_steps(small_rows, bits, far, core):
    stages = [[far, bits[0]]] + [bits[i : i + 2] for i in range(1, len(bits), 2)]

    def cores(state):
        x = plus(state[0], hop(state[1], core))
        return x[:, :-small_rows], x[:, -small_rows:]

    def down(stage):
        return lambda state: scatter_sum(state[0], stage, far, state[1])

    def up(stage):
        wanted = [b for b in stage if b != far]

        def step(state):
            x = state[0] if state[0].ndim == 2 else state[0][0]
            return gather(x, wanted), state[1]

        return step

    return [cores] + [down(s) for s in stages] + [up(s) for s in reversed(stages)] + [up([core])]


def early_steps(bits, far, core):
    first, second, rest = bits[0], bits[1], bits[2:]
    orders = ((far, first, second), (first, second, far), (second, far, first))

    def start(x):
        part = x.shape[1] // 3
        return down(0)([x[:, i * part : (i + 1) * part] for i in range(3)])

    def down(stage):
        return lambda chunks: [scatter_sum(c, [order[stage]], far) for c, order in zip(chunks, orders)]

    def swap(chunks):
        x = jnp.concatenate(chunks, axis=2)[0]
        for bit in rest:
            x = plus(x, hop(x, bit))
        width = x.shape[1] // 3
        return [x[:, : 2 * width], x[:, 2 * width :]]

    def up_one(parts):
        return [gather(parts[0], [second]), gather(parts[1], [first])]

    def up_two(parts):
        two, one = gather(parts[0], [first]), gather(parts[1], [second])
        width = one.shape[1]
        return jnp.concatenate([two[:, :width], two[:, width:], one], axis=0)

    return [start, down(1), down(2), swap, up_one, up_two, lambda x: gather(x, [core])]


def add(a, b):
    return a.astype(f32) + b.astype(f32)


def at_row(start, n):
    return pl.ds(pl.multiple_of(start, 16), n)


def merge_cores(info, keep, got, stay0, far0, stay1, first1, stay2, second2):
    n = keep.shape[1] // 3
    h = n // 2
    a, b = info[4], info[5]
    stay0[...] = add(keep[0, :n], got[0, :n]).astype(bf16)
    far0[...] = add(keep[1, :n], got[1, :n]).astype(bf16)
    for base, bit, stay, send in ((n, a, stay1, first1), (2 * n, b, stay2, second2)):
        for dst, m in ((stay, bit), (send, 1 - bit)):
            here = at_row(base + m * h, h)
            for g in range(2):
                dst[g] = add(keep[g, here], got[g, here]).astype(bf16)


def merge_two(info, stay0, got0, stay1, got1, stay2, got2, keep0, first0, keep1, second1, keep2, far2):
    a, b = info[4], info[5]
    h = stay0.shape[0] // 2
    for dst, m in ((keep0, a), (first0, 1 - a)):
        here = at_row(m * h, h)
        dst[...] = add(stay0[here], got0[here]).astype(bf16)
    q = stay1.shape[1] // 2
    for dst, m in ((keep1, b), (second1, 1 - b)):
        here = at_row(m * q, q)
        for g in range(2):
            dst[g] = add(stay1[g, here], got1[g, here]).astype(bf16)
    keep2[...] = add(stay2[0], got2[0]).astype(bf16)
    far2[...] = add(stay2[1], got2[1]).astype(bf16)


def merge_three(info, in0, got0, in1, got1, in2, got2, keep, got, stay, mine, to_second, to_far, to_first, to_both):
    a, b = info[4], info[5]
    q = in0.shape[0] // 2
    stay[:q] = add(in0[at_row(b * q, q)], got0[at_row(b * q, q)]).astype(bf16)
    to_second[...] = add(in0[at_row((1 - b) * q, q)], got0[at_row((1 - b) * q, q)]).astype(bf16)
    stay[q : 2 * q] = add(in1[0], got1[0]).astype(bf16)
    to_far[:q] = add(in1[1], got1[1]).astype(bf16)
    stay[2 * q :] = add(in2[at_row(a * q, q)], got2[at_row(a * q, q)]).astype(bf16)
    to_first[:q] = add(in2[at_row((1 - a) * q, q)], got2[at_row((1 - a) * q, q)]).astype(bf16)
    n = mine.shape[0]
    h = n - 16
    for dst, base, g, m in (
        (mine, 0, 0, a), (to_first, q, 0, 1 - a), (to_far, q, 1, a), (to_both, 0, 1, 1 - a)
    ):
        here = at_row(m * h, h)
        dst[base : base + h] = add(keep[g, here], got[g, here]).astype(bf16)
        dst[base + h : base + n] = add(keep[g, 2 * h :], got[g, 2 * h :]).astype(bf16)


def merge_four(info, stay, mine, second, far, first, both, part, own, to_second, to_third, to_both, total):
    q = second.shape[0]
    e = part
    e[:q] = add(stay[:q], second[...]).astype(bf16)
    e[q : 2 * q] = add(stay[q : 2 * q], far[:q]).astype(bf16)
    e[2 * q :] = add(stay[2 * q :], first[:q]).astype(bf16)
    to_third[: 3 * q] = e[...]
    total[...] = (add(mine[...], first[q:]) + add(far[q:], both[...])).astype(bf16)
    n = own.shape[0] - 16
    spot = 2 * info[5] + info[6]
    for dst, base, flip in ((own, 0, 0), (to_second, 0, 2), (to_third, 3 * q, 1), (to_both, 0, 3)):
        dst[base : base + n] = total[at_row((spot ^ flip) * n, n)]
        dst[base + n : base + n + 16] = total[4 * n :]


def merge_five(part, own, second, third, both, to_second, to_first, table, gains, shifts, ff, bias):
    n = part.shape[0]
    total = add(part[...], third[:n]).astype(bf16)
    q = n // 3
    to_second[...] = total[: 2 * q]
    to_first[:q] = total[2 * q :]
    s = add(own[...], second[...]) + add(third[n:], both[...])
    h = own.shape[0] - 16
    to_first[q:] = s[:h].astype(bf16)
    s = s[h:]
    width = s.shape[1]
    table[...] = s[0:2]
    gains[...] = s[2:4]
    shifts[...] = s[4:8]
    ff[:, :width] = s[8:9]
    ff[:, width:] = s[9:10]
    bias[0:1] = s[10:11, : width // 2]
    bias[1:2] = s[10:11, width // 2 :]


def merge_six(info, near2, got2, near1, got1, to_first, to_second, to_third):
    a, b = info[4], info[5]
    q = near2.shape[0] // 2
    for c in range(2):
        to_first[at_row(2 * c * q + b * q, q)] = near2[c * q : (c + 1) * q]
        to_first[at_row(2 * c * q + (1 - b) * q, q)] = got2[c * q : (c + 1) * q]
    to_second[at_row(a * q, q)] = near1[:q]
    to_second[at_row((1 - a) * q, q)] = got1[:q]
    h = near1.shape[0] - q
    to_third[at_row(a * h, h)] = near1[q:]
    to_third[at_row((1 - a) * h, h)] = got1[q:]
    to_second[2 * q :] = to_third[...]


def merge_seven(info, near1, got1, near2, got2, near3, got3, both, out):
    a, b = info[4], info[5]
    h = near1.shape[0] // 2
    for c in range(2):
        out[at_row(2 * c * h + a * h, h)] = near1[c * h : (c + 1) * h]
        out[at_row(2 * c * h + (1 - a) * h, h)] = got1[c * h : (c + 1) * h]
    out[at_row(4 * h + b * h, h)] = near2[:h]
    out[at_row(4 * h + (1 - b) * h, h)] = got2[:h]
    spot = 2 * b + info[6]
    n = near3.shape[0] // 2
    for src, base, flip in ((near3, 0, 0), (got2, h, 2), (got3, 0, 1), (both, 0, 3)):
        for m in range(2):
            out[at_row(6 * h + m * 4 * n + (spot ^ flip) * n, n)] = src[base + m * n : base + (m + 1) * n]


def merge(body, info, ins, outs, width, with_info=True):
    shapes = [(s if isinstance(s, tuple) else (s, width), bf16, VMEM) for s in outs]
    return call(
        body,
        shapes,
        [SMEM] * with_info + [VMEM] * len(ins),
        ((info,) if with_info else ()) + tuple(ins),
        [],
        24,
        2 * US,
        2e6,
        hbm_in=False,
        hbm_out=False,
    )


def sum_start(info, keep, send, bits, far, core):
    first, second, _ = bits
    width = keep.shape[2]
    n = keep.shape[1] // 3
    two = (2, n // 2, width)
    stay0, far0, stay1, first1, stay2, second2 = merge(
        merge_cores, info, (keep, hop(send, core)), (n, n, two, two, two, two), width
    )
    return (stay0, hop(far0, far), stay1, hop(first1, first), stay2, hop(second2, second))


def sum_finish(info, state, keep, send, bits, far, core, beside):
    first, second, third = bits
    width = keep.shape[2]
    n = state[0].shape[0]
    q = n // 4
    keep0, first0, keep1, second1, keep2, far2 = merge(
        merge_two, info, state, (n // 2, n // 2, (2, q, width), (2, q, width), n // 2, n // 2), width
    )
    keep0, send = lax.optimization_barrier((keep0, send))
    got = hop(send, core)
    h = (keep.shape[1] - 16) // 2 + 16
    stay, mine, to_second, to_far, to_first, to_both = merge(
        merge_three,
        info,
        (keep0, hop(first0, first), keep1, hop(second1, second), keep2, hop(far2, far), keep, got),
        (3 * q, h, q, q + h, q + h, h),
        width,
    )
    m = (h - 16) // 4
    part, own, to_second, to_third, to_both, _ = merge(
        merge_four,
        info,
        (stay, mine, hop(to_second, second), hop(to_far, far), hop(to_first, first), hop(to_both, first, far)),
        (3 * q, m + 16, m + 16, 3 * q + m + 16, m + 16, h),
        width,
    )
    many = beside[0](part)
    part, many[0] = lax.optimization_barrier((part, many[0]))
    c = width // 2
    to_second, to_first, *small = call(
        merge_five,
        [((2 * q, width), bf16, VMEM), ((q + m, width), bf16, VMEM)]
        + [(shape, f32, VMEM) for shape in ((2, width), (2, width), (4, width), (1, 2 * width), (2, c))],
        [VMEM] * 5,
        (part, own, hop(to_second, second), hop(to_third, third), hop(to_both, second, third)),
        [],
        24,
        2 * US,
        2e6,
        hbm_in=False,
        hbm_out=False,
    )
    got2, got1 = hop(to_second, second), hop(to_first, first)
    to_first, to_second, to_third = merge(
        merge_six, info, (to_second, got2, to_first, got1), (4 * q, 2 * q + 2 * m, 2 * m), width
    )
    rows = beside[1](to_third)
    got1, got2 = hop(to_first, first), hop(to_second, second)
    got3, both = hop(to_third, third), hop(to_third, second, third)
    to_first, rows = lax.optimization_barrier((to_first, rows))
    (mine,) = merge(
        merge_seven, info, (to_first, got1, to_second, got2, to_third, got3, both), (12 * q + 8 * m,), width
    )
    few = beside[2](mine)
    return mine, hop(mine, core), small, (many, rows, few)


def wipe(*refs):
    sems = refs[-1]
    count = sems.shape[0]
    outs, zeros = refs[1 : 1 + count], refs[1 + count : -1]
    for zero in zeros:
        zero[...] = jnp.zeros_like(zero)
    copies = []
    for i, out in enumerate(outs):
        src = next(z for z in zeros if z.dtype == out.dtype and z.shape[1] == out.shape[1])
        rows = out.shape[0]
        n = next(c for c in (256, 192, 128, 64, 32, 16) if rows % c == 0)
        for at in range(0, rows, n):
            copies.append(
                pltpu.make_async_copy(
                    src.at[pl.ds(0, n), :], out.at[pl.ds(at, n), :], sems.at[i]
                )
            )
    for copy in copies:
        copy.start()
    for copy in copies:
        copy.wait()


def blanks_for(gate, likes):
    flat = [(math.prod(x.shape[:-1]), x.shape[-1]) for x in likes]
    widths = sorted({n for _, n in flat})
    outs = call(
        wipe,
        [(s, x.dtype, HBM) for s, x in zip(flat, likes)],
        [HBM],
        (gate,),
        [pltpu.VMEM((256, n), k) for n in widths for k in (f32, bf16)]
        + [pltpu.SemaphoreType.DMA((len(likes),))],
        8,
        5 * US,
        14e6,
        hbm_in=False,
    )
    return [x.reshape(like.shape) for x, like in zip(outs, likes)]


def moments(turned, m, v):
    first = BETA_ONE * m[...] + (1.0 - BETA_ONE) * turned
    second = BETA_TWO * v[...] + (1.0 - BETA_TWO) * (turned * turned)
    m[...] = first
    v[...] = second
    return (first / (jnp.sqrt(second) + EPS_ADAM)).astype(bf16)


def fetch(pairs, sems):
    for copy in copy_all(pairs, sems):
        copy.wait()


def step_wide(g, w, m, v, ql, qr, rate, scratch):
    low_l, low_r, mid, back = scratch
    low_l[...] = ql[...].astype(bf16)
    low_r[...] = qr[...].astype(bf16)
    blocks, size = qr.shape[0], qr.shape[1]
    mid[...] = nn(ql[...].T.astype(bf16), g).astype(bf16)
    for b in range(blocks):
        at = slice(b * size, (b + 1) * size)
        u = moments(nn(mid[:, at], low_r[b]), m.at[:, at], v.at[:, at])
        back[:, at] = nt(u, low_r[b]).astype(bf16)
    w[...] = w[...] - rate * nn(low_l[...], back[...])


def step_tall(g, w, m, v, ql, qr, rate, scratch):
    low_r, mid, back = scratch
    low_r[...] = qr[...].astype(bf16)
    blocks, size = ql.shape[0], ql.shape[1]
    for b in range(blocks):
        at = slice(b * size, (b + 1) * size)
        mid[at, :] = nn(ql[b].T.astype(bf16), g[at, :]).astype(bf16)
    u = moments(nn(mid[...], low_r[...]), m, v)
    back[...] = nt(u, low_r[...]).astype(bf16)
    for b in range(blocks):
        at = slice(b * size, (b + 1) * size)
        w[at, :] = w[at, :] - rate * nn(ql[b].astype(bf16), back[at, :])


def update_qkv(rate, mine, g, w_in, m_in, v_in, ql_in, qr_in, *refs):
    outs, (grad, new, mom, var, copy) = refs[:4], refs[4:9]
    w, m, v, c, ql, qr, low_l, low_r, mid, back, sems = refs[9:]
    for j in range(3):
        grad[j] = g[j].astype(f32)

        @pl.when(mine[j] == 1)
        def _():
            fetch(
                [(w_in.at[j], w), (m_in.at[j], m), (v_in.at[j], v), (ql_in.at[j], ql), (qr_in.at[j], qr)], sems
            )
            step_wide(g[j], w, m, v, ql, qr, rate, (low_l, low_r, mid, back))
            c[...] = w[...].astype(bf16)
            fetch([(w, new.at[j]), (m, mom.at[j]), (v, var.at[j]), (c, copy.at[j])], sems)


def update_rest(rate_out, rate_up, rate_down, mine, g_out, g_up, g_down_t, *refs):
    (wo_in, mo_in, vo_in, lo_in, ro_in, wu_in, mu_in, vu_in, lu_in, ru_in,
     wd_in, md_in, vd_in, ld_in, rd_in) = refs[:15]
    refs = refs[15 + 11 :]
    grad_o, grad_u, grad_d = refs[:3]
    new_o, moments_o, copy_o, new_u, mom_u, var_u, copy_u, new_d, mom_d, var_d, copy_d = refs[3:14]
    (wo, mo, vo, co, lo, ro, low_ro, mid_o, back_o,
     wu, mu, vu, cu, lu, ru, low_lu, low_ru, mid_u, back_u,
     wd, md, vd, cd, mid_d, back_d, sems) = refs[14:]
    grad_o[...] = g_out[...].astype(f32)
    grad_u[...] = g_up[...].astype(f32)
    grad_d[...] = g_down_t[...].astype(f32).T

    @pl.when(mine[3] == 1)
    def _():
        fetch([(wo_in, wo), (mo_in, mo), (vo_in, vo), (lo_in, lo), (ro_in, ro)], sems)
        step_tall(g_out[...], wo, mo, vo, lo, ro, rate_out, (low_ro, mid_o, back_o))
        co[...] = wo[...].astype(bf16)
        fetch([(wo, new_o), (mo, moments_o.at[0]), (vo, moments_o.at[1]), (co, copy_o)], sems)

    @pl.when(mine[4] == 1)
    def _():
        fetch([(wu_in, wu), (mu_in, mu), (vu_in, vu), (lu_in, lu), (ru_in, ru)], sems)
        step_wide(g_up[...], wu, mu, vu, lu, ru, rate_up, (low_lu, low_ru, mid_u, back_u))
        cu[...] = wu[...].astype(bf16)
        fetch([(wu, new_u), (mu, mom_u), (vu, var_u), (cu, copy_u)], sems)

    @pl.when(mine[5] == 1)
    def _():
        fetch([(wd_in, wd), (md_in, md), (vd_in, vd), (ld_in, ru), (rd_in, lu)], sems)
        step_tall(grad_d[...].astype(bf16), wd, md, vd, ru, lu, rate_down, (low_lu, mid_d, back_d))
        cd[...] = wd[...].astype(bf16)
        fetch([(wd, new_d), (md, mom_d), (vd, var_d), (cd, copy_d)], sems)


def owned_step(flag, ins, outs, bufs, in_sems, out_sems):
    loads = [pltpu.make_async_copy(a, b, in_sems.at[i]) for i, (a, b) in enumerate(zip(ins, bufs[:5]))]
    stores = [
        pltpu.make_async_copy(b, a, out_sems.at[i])
        for i, (a, b) in enumerate(zip(outs, (bufs[0], bufs[1], bufs[2], bufs[5])))
    ]

    @pl.when(flag)
    def _():
        for copy in loads:
            copy.start()

    return loads, stores


def update_all(rate_out, rate_wide, rate_down, cols, hid, owned, info, mine, other, *refs):
    wq, mq, vq, lq, rq, wo, mo, vo, lo, ro, wu, mu, vu, lu, ru, wd, md, vd, ld, rd = refs[:20]
    refs = refs[20 + 15 :]
    grad_q, grad_o, grad_u, grad_d = refs[:4]
    new_q, mom_q, var_q, copy_q, new_o, mom_o, copy_o, new_u, mom_u, var_u, copy_u, new_d, mom_d, var_d, copy_d = refs[4:19]
    refs = refs[19:]
    buf, gq, go, gu, gd = refs[:5]
    bufs_q, bufs_o, bufs_u, bufs_d = refs[5:11], refs[11:17], refs[17:23], refs[23:29]
    low_l, low_r64, low_r256, mid_q, mid_o, mid_u, mid_d, back_q, back_o, back_u, back_d = refs[29:40]
    sems, in_sems, out_sems = refs[40:]
    core = info[0]
    width = buf.shape[1]
    half = width // 2
    one = mine.shape[0] // 4 * 3
    two = mine.shape[0] - one
    pairs = []
    for piece, spot in ((mine, core), (other, 1 - core)):
        pairs.append((piece.at[pl.ds(0, one)], buf.at[at_row(spot * one, one)]))
        pairs.append((piece.at[pl.ds(one, two)], buf.at[at_row(2 * one + spot * two, two)]))
    fills = copy_all(pairs, sems)
    jobs = []
    for j in range(3):
        jobs.append(
            owned_step(
                owned[j] == 1,
                [x.at[j] for x in (wq, mq, vq, lq, rq)],
                [x.at[j] for x in (new_q, mom_q, var_q, copy_q)],
                [x.at[j] for x in bufs_q],
                in_sems.at[j],
                out_sems.at[j],
            )
        )
    jobs.append(
        owned_step(owned[3] == 1, (wo, mo, vo, lo, ro), (new_o, mom_o.at[0], mom_o.at[1], copy_o), bufs_o,
                   in_sems.at[3], out_sems.at[3])
    )
    jobs.append(
        owned_step(owned[4] == 1, (wu, mu, vu, lu, ru), (new_u, mom_u, var_u, copy_u), bufs_u,
                   in_sems.at[4], out_sems.at[4])
    )
    jobs.append(
        owned_step(owned[5] == 1, (wd, md, vd, ld, rd), (new_d, mom_d, var_d, copy_d), bufs_d,
                   in_sems.at[5], out_sems.at[5])
    )
    for copy in fills:
        copy.wait()
    grads = []

    def give(scratch, out):
        copy = pltpu.make_async_copy(scratch, out, sems.at[4 + len(grads)])
        copy.start()
        grads.append(copy)

    n = hid // 2
    for h in range(2):
        gu[:, h * n : (h + 1) * n] = buf[h * width : (h + 1) * width, :].astype(f32)
    give(gu, grad_u)
    go[...] = buf[2 * hid : 2 * hid + cols, :].astype(f32)
    give(go, grad_o)
    base = 2 * hid + cols
    for j in range(3):
        x = buf[base + j * half : base + (j + 1) * half, :].astype(f32)
        gq[j, :half, :] = x[:, :cols]
        gq[j, half:, :] = x[:, cols:]
    give(gq, grad_q)
    for h in range(2):
        gd[h * n : (h + 1) * n, :] = buf[hid + h * width : hid + (h + 1) * width, :].astype(f32).T
    give(gd, grad_d)

    def finish(k, bufs, run):
        loads, stores = jobs[k]

        @pl.when(owned[k] == 1)
        def _():
            for copy in loads:
                copy.wait()
            run()
            bufs[5][...] = bufs[0][...].astype(bf16)
            for copy in stores:
                copy.start()

    w, m, v, l, r, _ = bufs_u
    finish(4, bufs_u, lambda: step_wide(gu[...].astype(bf16), w, m, v, l, r, rate_wide,
                                        (low_l, low_r256, mid_u, back_u)))
    wt, mt, vt, lt, rt, _ = bufs_d
    finish(5, bufs_d, lambda: step_tall(gd[...].astype(bf16), wt, mt, vt, lt, rt, rate_down,
                                        (low_l, mid_d, back_d)))
    ws, ms, vs, ls, rs, _ = bufs_o
    finish(3, bufs_o, lambda: step_tall(go[...].astype(bf16), ws, ms, vs, ls, rs, rate_out,
                                        (low_l, mid_o, back_o)))
    for j in range(3):
        here = [x.at[j] for x in bufs_q]
        finish(j, here, lambda here=here, j=j: step_wide(gq[j].astype(bf16), *here[:5], rate_wide,
                                                         (low_l, low_r64, mid_q, back_q)))
    for k in range(6):

        @pl.when(owned[k] == 1)
        def _(k=k):
            for copy in jobs[k][1]:
                copy.wait()

    for copy in grads:
        copy.wait()


def pad_picks(picks):
    windows, heads, slots = picks.shape
    return jnp.pad(picks, ((0, 0), (0, 0), (0, SLOTS - slots)), constant_values=-1).reshape(
        windows, heads * SLOTS
    )


def per_device(
    tokens_in,
    cotangent,
    data_table,
    window_group,
    query_picks,
    owner_list,
    weight_qkv,
    head_bias,
    weight_out,
    weight_up,
    ff_bias,
    weight_down,
    norm_gains,
    shifts,
    first_qkv,
    second_qkv,
    first_out,
    second_out,
    first_up,
    second_up,
    first_down,
    second_down,
    basis_qkv_left,
    basis_qkv_right,
    basis_out_left,
    basis_out_right,
    basis_up_left,
    basis_up_right,
    basis_down_left,
    basis_down_right,
):
    head_count = lax.axis_size("head")
    head = lax.axis_index("head")
    my_rank = lax.axis_index("dp")
    rows, width = tokens_in.shape
    length = rows * head_count // window_group.shape[0]
    windows = rows // length
    head_dim = basis_qkv_right.shape[-1]
    cols = GROUP * head_dim
    scale = 1.0 / math.sqrt(head_dim)
    head_bits = head_count.bit_length() - 1
    far = ("head", head_bits - 1)
    core_bit = ("dp", 0)
    dp_bits = lax.axis_size("dp").bit_length() - 1
    bits = [("dp", k) for k in range(1, dp_bits)] + [("head", k) for k in range(head_bits - 1)]
    core = my_rank & 1
    slots = GROUP * SLOTS
    half = width // 2

    if head_count == 2:
        n_qkv, n_bias, n_out, n_up, n_ff, n_down = (
            weight_qkv, head_bias, weight_out, weight_up, ff_bias, weight_down
        )
        picks = pad_picks(query_picks).astype(f32)
        near_at, far_at = head * windows, (1 - head) * windows
    else:
        def whole_of(x, dim):
            return lax.all_gather(x, "head", axis=dim, tiled=True)

        def pick_group(x, dim, g):
            n = x.shape[dim] // 2
            return lax.dynamic_slice_in_dim(x, (side(far) ^ g) * n, n, dim)

        both = [
            (whole_of(weight_qkv.astype(bf16), 2).astype(f32), 2),
            (whole_of(head_bias, 1), 1),
            (whole_of(weight_out.astype(bf16), 0).astype(f32), 0),
            (whole_of(weight_up.astype(bf16), 1).astype(f32), 1),
            (whole_of(ff_bias, 0), 0),
            (whole_of(weight_down.astype(bf16), 0).astype(f32), 0),
        ]
        n_qkv, n_bias, n_out, n_up, n_ff, n_down = (pick_group(x, d, 0) for x, d in both)
        away = [pick_group(x, d, 1) for x, d in both]
        picks = lax.dynamic_slice_in_dim(whole_of(query_picks, 1), head * windows, windows, 0)
        picks = jnp.concatenate([pad_picks(pick_group(picks, 1, g)) for g in range(2)]).astype(f32)
        near_at, far_at = jnp.int32(0), jnp.int32(windows)
    info = jnp.stack([core, near_at, far_at, head * windows] + [side(b) for b in bits]).astype(jnp.int32)
    quick = head_count == 2 and len(bits) == 3
    hid = n_up.shape[1]
    extra_rows = -(-(windows + 6) // 16) * 16
    buf_rows = 2 * hid + cols
    rest_rows = cols // 2 + width + 16

    def send_qkv(info, w, bias):
        return call(
            lambda *refs: pack_qkv(windows, *refs),
            [((3 * half + extra_rows, cols), bf16, VMEM), ((3, width, cols), bf16, VMEM)],
            [SMEM, VMEM, VMEM, VMEM],
            (info, w, bias, picks),
            [pltpu.VMEM((extra_rows, cols), f32)],
            12,
            2 * US,
            3e6,
            hbm_in=False,
            hbm_out=False,
        )

    def send_rest(info, w_out, w_up, w_down, bias):
        return call(
            pack_rest,
            [
                ((rest_rows, width), bf16, VMEM),
                ((hid // 2, width), bf16, VMEM),
                ((2, rest_rows, width), bf16, VMEM),
                ((hid, width), bf16, VMEM),
            ],
            [SMEM, VMEM, VMEM, VMEM, VMEM],
            (info, w_out, w_up, w_down, bias[None]),
            [pltpu.VMEM((16, width), f32)],
            24,
            4 * US,
            8e6,
            hbm_in=False,
            hbm_out=False,
        )

    qkv_piece, wq0 = send_qkv(info, n_qkv, n_bias)
    if head_count == 2:
        qkv_y = hop(qkv_piece, far)
        rest_piece, down_piece, rest0, down0 = send_rest(info, n_out, n_up, n_down, n_ff)
        rest_piece, qkv_y = lax.optimization_barrier((rest_piece, qkv_y))
        rest_y = hop(rest_piece, far)
        down_piece, rest_y = lax.optimization_barrier((down_piece, rest_y))
        down_y = hop(down_piece, far)
    else:
        other = info.at[0].set(1 - core)
        rest0, down0 = send_rest(info, n_out, n_up, n_down, n_ff)[2:]
        qkv_y, qkv_c = (send_qkv(m, away[0], away[1])[0] for m in (info, other))
        (rest_y, down_y), (rest_c, down_c) = (
            send_rest(m, away[2], away[3], away[5], away[4])[:2] for m in (info, other)
        )

    block = 2 * length
    steps = (rows // block,)
    seen = [
        ((rows, cols), bf16, cut(block, cols)),
        ((rows, cols), bf16, cut(block, cols)),
        ((rows, cols), bf16, cut(block, cols)),
        ((rows, cols), bf16, cut(block, cols)),
        ((windows, slots, length), f32, cut(2, slots, length)),
        ((windows, slots, cols), bf16, cut(2, slots, cols)),
    ]
    q0, k0, v0, ctx0, att0, picked0, emb = call(
        lambda *refs: attend_own(length, scale, *refs),
        seen + [((rows, width), bf16, cut(block, width))],
        [SMEM, SMEM, cut(block, width), whole(NDATA, width), whole(3, width, cols),
         whole(2, cols), whole(*picks.shape)],
        (info, window_group, tokens_in, data_table, wq0, n_bias, picks),
        [],
        24,
        9 * US,
        6e6,
        grid=steps,
        hbm_in=False,
    )
    if head_count == 2:
        qkv_y, ctx0 = lax.optimization_barrier((qkv_y, ctx0))
        qkv_c = hop(qkv_y, core_bit)
    q1, k1, v1, ctx1, att1, picked1, wq1, picks1 = call(
        lambda *refs: attend_far(length, scale, *refs),
        seen + [((3, width, cols), bf16, whole(3, width, cols)), ((windows, slots), f32, whole(windows, slots))],
        [SMEM, cut(block, width), HBM, HBM],
        (info, emb, qkv_y, qkv_c),
        [
            pltpu.VMEM((extra_rows, cols), bf16),
            pltpu.VMEM((2, cols), f32),
            pltpu.SemaphoreType.DMA((7,)),
        ],
        24,
        9 * US,
        6e6,
        grid=steps,
    )
    if head_count == 2:
        rest_y, ctx1 = lax.optimization_barrier((rest_y, ctx1))
        rest_c = hop(rest_y, core_bit)

    def kinds(x):
        return [jax.ShapeDtypeStruct(x.shape, k) for k in (f32, f32, f32, bf16)]

    few = kinds(first_qkv) + [
        jax.ShapeDtypeStruct(first_out.shape, f32),
        jax.ShapeDtypeStruct((2,) + first_out.shape, f32),
        jax.ShapeDtypeStruct(first_out.shape, bf16),
    ]
    many = kinds(first_up) + kinds(first_down)

    def make_few(gate):
        return blanks_for(gate, few)

    def make_many(gate):
        return blanks_for(gate, many)

    def make_input_grad(gq, gp1):
        return call(
            input_grad,
            [((rows, width), f32, cut(block, width))],
            [cut(block, width)] * 3 + [whole(3, width, cols)] * 2 + [cut(block, width)],
            (gq, gk, gv, wq0, wq1, gp1),
            [],
            24,
            4 * US,
            8e6,
            grid=steps,
        )[0]

    big = rows // 2 if rows // 2 % block == 0 else block
    resid, act, slope, wo, up = call(
        lambda *refs: ff_in(length, *refs),
        [
            ((rows, width), f32, cut(big, width)),
            ((rows, 2 * hid), bf16, cut(big, 2 * hid)),
            ((rows, 2 * hid), bf16, cut(big, 2 * hid)),
            ((2, cols, width), bf16, whole(2, cols, width)),
            ((2, width, hid), bf16, whole(2, width, hid)),
        ],
        [SMEM, SMEM, cut(big, width), whole(NDATA, width), cut(big, cols), cut(big, cols), FAR, HBM, HBM,
         whole(1, hid), whole(2, width), whole(4, width)],
        (info, window_group, tokens_in, data_table, ctx0, ctx1, rest0, rest_y, rest_c,
         n_ff[None], norm_gains, shifts),
        [
            pltpu.VMEM((big, width), f32),
            pltpu.VMEM((2, hid), f32),
            pltpu.VMEM((16, width), bf16),
            pltpu.SemaphoreType.DMA((13,)),
        ],
        40,
        10 * US,
        14e6,
        grid=(rows // big,),
    )
    if head_count == 2:
        down_y, resid = lax.optimization_barrier((down_y, resid))
        down_c = hop(down_y, core_bit)
    output_rows, gp1, ga, keep_one, send_one, sums = call(
        lambda *refs: ff_back(length, *refs),
        [
            ((rows, width), f32, cut(big, width)),
            ((rows, width), f32, cut(big, width)),
            ((rows, width), bf16, cut(big, width)),
            ((2, buf_rows // 2, width), bf16, HBM),
            ((2, buf_rows // 2, width), bf16, HBM),
            ((16, width), f32, whole(16, width)),
        ],
        [SMEM, SMEM, cut(big, width), FAR, cut(big, 2 * hid), whole(2, width, hid), FAR, HBM, HBM,
         whole(2, width), whole(4, width), cut(big, width), whole(rows, cols), whole(rows, cols)],
        (info, window_group, resid, act, slope, up, down0, down_y, down_c,
         norm_gains, shifts, cotangent, ctx0, ctx1),
        [
            pltpu.VMEM((2, hid, width), bf16),
            pltpu.VMEM((rows, 2 * hid), bf16),
            pltpu.VMEM((rows, 2 * hid), bf16),
            pltpu.VMEM((rows, width), bf16),
            pltpu.VMEM((rows, width), bf16),
            pltpu.VMEM((rows, width), bf16),
            pltpu.VMEM((width, rows), bf16),
            pltpu.VMEM((width, rows), bf16),
            pltpu.VMEM((2, buf_rows, width), bf16),
            pltpu.SemaphoreType.DMA((4,)),
            pltpu.SemaphoreType.DMA((rows // big,)),
        ],
        56,
        20 * US,
        20e6,
        grid=(rows // big,),
    )
    if quick:
        state_one = sum_start(info, keep_one, send_one, bits, far, core_bit)
        ga, held = lax.optimization_barrier((ga, state_one[0]))
        state_one = (held, *state_one[1:])
    else:
        sum_one = plus(keep_one, hop(send_one, core_bit))
        sum_one, ga = lax.optimization_barrier((sum_one, ga))
    piece_two = 3 * half // 2 + 16
    gq, gk, gv, keep_two, send_two = call(
        lambda *refs: attend_back(length, scale, *refs),
        [
            ((rows, width), bf16, cut(block, width)),
            ((rows, width), bf16, cut(block, width)),
            ((rows, width), bf16, cut(block, width)),
            ((2, piece_two, width), bf16, HBM),
            ((2, piece_two, width), bf16, HBM),
        ],
        [SMEM, SMEM, cut(block, width), FAR, whole(2, cols, width), whole(16, width),
         whole(*picks.shape), whole(windows, slots), FAR, FAR]
        + [cut(block, cols), cut(block, cols), cut(2, slots, length), cut(2, slots, cols)] * 2,
        (info, window_group, ga, emb, wo, sums, picks, picks1, wq0, wq1,
         k0, v0, att0, picked0, k1, v1, att1, picked1),
        [pltpu.VMEM((rows, width), bf16)] * 4
        + [pltpu.VMEM((3, width, cols), bf16)] * 2
        + [
            pltpu.VMEM((width, rows), bf16),
            pltpu.VMEM((16, width), f32),
            pltpu.VMEM((2, 3 * half + 16, width), bf16),
            pltpu.VMEM((2, 16, width), f32),
            pltpu.SemaphoreType.DMA((11,)),
        ],
        40,
        14 * US,
        10e6,
        grid=steps,
    )
    shards = head_count // 2
    mine = head % shards

    def shard(x, dim):
        n = x.shape[dim] // shards
        return x if shards == 1 else lax.dynamic_slice_in_dim(x, mine * n, n, dim)

    owned = (owner_list == my_rank).astype(jnp.int32)

    rate_wide = width ** (-0.5)
    rate_out = max(width // head_dim, 1) ** (-0.5)
    rate_down = (n_down.shape[0] * 2) ** (-0.5)
    moments_in = (
        weight_qkv, first_qkv, second_qkv, basis_qkv_left, basis_qkv_right,
        weight_out, first_out, second_out, basis_out_left, basis_out_right,
        weight_up, first_up, second_up, basis_up_left, basis_up_right,
        weight_down, first_down, second_down, basis_down_left, basis_down_right,
    )
    if quick:
        held, keep_two, send_two = lax.optimization_barrier((state_one[0], keep_two, send_two))
        beside = (make_many, lambda gate: make_input_grad(lax.optimization_barrier((gq, gate))[0], gp1), make_few)
        mine, other, small, (many, grad_rows, few) = sum_finish(
            info, (held, *state_one[1:]), keep_two, send_two, bits, far, core_bit, beside
        )
        blanks = few + many
        grads = [first_qkv, first_out, first_up, first_down]
        sets = [moments_in[5 * i : 5 * i + 5] for i in range(4)]
        scratch = [pltpu.VMEM((buf_rows + 3 * half, width), bf16)] + [pltpu.VMEM(x.shape, f32) for x in grads]
        for group in sets:
            scratch += [pltpu.VMEM(x.shape, f32) for x in group] + [pltpu.VMEM(group[0].shape, bf16)]
        scratch += [
            pltpu.VMEM((width, width), bf16),
            pltpu.VMEM(basis_qkv_right.shape[1:], bf16),
            pltpu.VMEM(basis_up_right.shape, bf16),
        ]
        temps = [first_qkv.shape[1:], first_out.shape, first_up.shape, first_down.shape]
        scratch += [pltpu.VMEM(x, bf16) for x in temps * 2]
        scratch += [
            pltpu.SemaphoreType.DMA((8,)),
            pltpu.SemaphoreType.DMA((6, 5)),
            pltpu.SemaphoreType.DMA((6, 4)),
        ]
        outs = call(
            lambda *refs: update_all(rate_out, rate_wide, rate_down, cols, hid, *refs),
            [(x.shape, f32, HBM) for x in grads] + [(x.shape, x.dtype, HBM) for x in blanks],
            [SMEM, SMEM] + [HBM] * 2 + [FAR] * (20 + 15),
            (owned, info, mine, other, *moments_in, *blanks),
            scratch,
            60,
            12 * US,
            30e6,
            {24 + i: 4 + i for i in range(15)},
        )
        grad_qkv_all, grad_out_all, grad_up_all, grad_down_all = outs[:4]
        qkv_outs, rest_outs = outs[3:8], outs[5:]
        grad_table_all, grad_gains_all, grad_shifts_all, grad_ff_all, grad_bias_all = small
        grad_ff_all = grad_ff_all.reshape(-1)
    else:
        grad_rows = make_input_grad(gq, gp1)
        blanks = make_few(sums) + make_many(sums)
        early, late = early_steps(bits, far, core_bit), late_steps(16, bits, far, core_bit)
        state_one, state_two = early[0](sum_one), (keep_two, send_two)
        for i in range(1, max(len(early), len(late) + 1)):
            state_one, state_two = lax.optimization_barrier((state_one, state_two))
            if i < len(early):
                state_one = early[i](state_one)
            if i <= len(late):
                state_two = late[i - 1](state_two)
        sum_one, (sum_two, small) = state_one, state_two
        small = small[0]
        g_up = shard(jnp.concatenate([sum_one[:width], sum_one[width : 2 * width]], 1), 1)
        g_down_t = shard(
            jnp.concatenate([sum_one[2 * width : 3 * width], sum_one[3 * width : 4 * width]], 1), 1
        )
        g_out = shard(sum_one[4 * width :], 0)

        def rest_body(*refs):
            update_rest(rate_out, rate_wide, rate_down, *refs)

        tall, wide, low = first_out.shape, first_up.shape, first_down.shape
        rest_outs = call(
            rest_body,
            [(tall, f32, VMEM), (wide, f32, VMEM), (low, f32, VMEM)]
            + [(x.shape, x.dtype, HBM) for x in blanks[4:]],
            [SMEM, VMEM, VMEM, VMEM] + [HBM] * (15 + 11),
            (owned, g_out, g_up, g_down_t,
             weight_out, first_out, second_out, basis_out_left, basis_out_right,
             weight_up, first_up, second_up, basis_up_left, basis_up_right,
             weight_down, first_down, second_down, basis_down_left, basis_down_right, *blanks[4:]),
            [pltpu.VMEM(tall, f32)] * 3
            + [
                pltpu.VMEM(tall, bf16),
                pltpu.VMEM(basis_out_left.shape, f32),
                pltpu.VMEM(basis_out_right.shape, f32),
                pltpu.VMEM(basis_out_right.shape, bf16),
                pltpu.VMEM(tall, bf16),
                pltpu.VMEM(tall, bf16),
            ]
            + [pltpu.VMEM(wide, f32)] * 3
            + [
                pltpu.VMEM(wide, bf16),
                pltpu.VMEM(basis_up_left.shape, f32),
                pltpu.VMEM(basis_up_right.shape, f32),
                pltpu.VMEM(basis_up_left.shape, bf16),
                pltpu.VMEM(basis_up_right.shape, bf16),
                pltpu.VMEM(wide, bf16),
                pltpu.VMEM(wide, bf16),
            ]
            + [pltpu.VMEM(low, f32)] * 3
            + [pltpu.VMEM(low, bf16)] * 3
            + [pltpu.SemaphoreType.DMA((5,))],
            48,
            12 * US,
            20e6,
            {4 + 15 + i: 3 + i for i in range(11)},
        )
        grad_out_all, grad_up_all, grad_down_all = rest_outs[:3]

        pairs = sum_two.reshape(3, half, width)
        g_qkv = shard(jnp.concatenate([pairs[:, :, :cols], pairs[:, :, cols:]], 1), 2)
        small = small.astype(f32)

        def qkv_body(*refs):
            update_qkv(rate_wide, *refs)

        one = first_qkv.shape[1:]
        qkv_outs = call(
            qkv_body,
            [(first_qkv.shape, f32, VMEM)] + [(x.shape, x.dtype, HBM) for x in blanks[:4]],
            [SMEM, VMEM] + [HBM] * 9,
            (owned, g_qkv, weight_qkv, first_qkv, second_qkv, basis_qkv_left, basis_qkv_right, *blanks[:4]),
            [pltpu.VMEM(one, f32)] * 3
            + [
                pltpu.VMEM(one, bf16),
                pltpu.VMEM(basis_qkv_left.shape[1:], f32),
                pltpu.VMEM(basis_qkv_right.shape[1:], f32),
                pltpu.VMEM(basis_qkv_left.shape[1:], bf16),
                pltpu.VMEM(basis_qkv_right.shape[1:], bf16),
                pltpu.VMEM(one, bf16),
                pltpu.VMEM(one, bf16),
                pltpu.SemaphoreType.DMA((5,)),
            ],
            24,
            6 * US,
            8e6,
            {7 + i: 1 + i for i in range(4)},
        )
        grad_qkv_all = qkv_outs[0]
        grad_table_all = small[0:2]
        grad_gains_all = small[2:4]
        grad_shifts_all = small[4:8]
        grad_ff_all = shard(small[8:10].reshape(-1), 0)
        grad_bias_all = shard(small[10].reshape(2, cols), 1)
    return (
        output_rows,
        grad_rows,
        grad_table_all,
        grad_gains_all,
        grad_shifts_all,
        grad_bias_all,
        grad_ff_all,
        grad_qkv_all,
        grad_out_all,
        grad_up_all,
        grad_down_all,
        *(x[None] for x in qkv_outs[1:]),
        *(x[None] for x in rest_outs[3:]),
    )


def solution(mesh):
    in_specs = (
        P(("dp", "head"), None),
        P(("dp", "head"), None),
        P(),
        P("dp"),
        P("dp", "head", None),
        P(),
        P(None, None, "head"),
        P(None, "head"),
        P("head", None),
        P(None, "head"),
        P("head"),
        P("head", None),
        P(),
        P(),
        P(None, None, "head"),
        P(None, None, "head"),
        P("head", None),
        P("head", None),
        P(None, "head"),
        P(None, "head"),
        P("head", None),
        P("head", None),
        P(),
        P(None, "head", None, None),
        P("head", None, None),
        P(),
        P(),
        P("head", None, None),
        P("head", None, None),
        P(),
    )
    out_specs = (
        P(("dp", "head"), None),
        P(("dp", "head"), None),
        P(),
        P(),
        P(),
        P(None, "head"),
        P("head"),
        P(None, None, "head"),
        P("head", None),
        P(None, "head"),
        P("head", None),
        P("dp", None, None, "head"),
        P("dp", None, None, "head"),
        P("dp", None, None, "head"),
        P("dp", None, None, "head"),
        P("dp", "head", None),
        P("dp", None, "head", None),
        P("dp", "head", None),
        P("dp", None, "head"),
        P("dp", None, "head"),
        P("dp", None, "head"),
        P("dp", None, "head"),
        P("dp", "head", None),
        P("dp", "head", None),
        P("dp", "head", None),
        P("dp", "head", None),
    )
    return jax.shard_map(
        per_device, mesh=mesh, in_specs=in_specs, out_specs=out_specs, check_vma=False
    )
```

```python
import math

import jax
import jax.numpy as jnp
from jax import lax
from jax.experimental import pallas as pl
from jax.experimental.pallas import tpu as pltpu
from jax.sharding import PartitionSpec as P

f32 = jnp.float32
bf16 = jnp.bfloat16

NDATA = 2
EPS_NORM = 1e-05
EPS_ADAM = 1e-08
BETA_ONE = 0.5
BETA_TWO = 0.5

GROUP = 4
SLOTS = 32
MB = 1 << 20


def nn(a, b):
    return jnp.dot(a, b, preferred_element_type=f32)


def nt(a, b):
    return lax.dot_general(a, b, (((1,), (1,)), ((), ())), preferred_element_type=f32)


def col_sum(x):
    return jnp.sum(x, axis=0, keepdims=True)


def row_mean(x):
    return jnp.mean(x, axis=-1, keepdims=True)


VMEM = pl.BlockSpec(memory_space=pltpu.VMEM)
SMEM = pl.BlockSpec(memory_space=pltpu.SMEM)
HBM = pl.BlockSpec(memory_space=pl.ANY)
FAR = pl.BlockSpec(memory_space=pl.ANY)


def whole(*shape):
    return pl.BlockSpec(shape, lambda i: (0,) * len(shape))


def cut(*shape):
    return pl.BlockSpec(shape, lambda i: (i,) + (0,) * (len(shape) - 1))


US = 1_000_000_000


def in_hbm(x, spec):
    if spec is SMEM or spec is HBM or x.size * x.dtype.itemsize < 1 << 16:
        return x
    return pltpu.with_memory_space_constraint(x, pltpu.HBM)


def call(body, outs, ins, args, scratch, limit, flops, nbytes, aliases={}, grid=(), hbm_in=True, hbm_out=True):
    if hbm_in:
        args = [in_hbm(x, spec) for x, spec in zip(args, ins)]
    kind = pltpu.HBM if hbm_out else jax.ShapeDtypeStruct
    return pl.pallas_call(
        body,
        grid=grid,
        out_shape=tuple(kind(s, d) for s, d, _ in outs),
        in_specs=ins,
        out_specs=tuple(spec for _, _, spec in outs),
        scratch_shapes=scratch,
        input_output_aliases=aliases,
        compiler_params=pltpu.CompilerParams(vmem_limit_bytes=limit * MB),
        cost_estimate=pl.CostEstimate(
            flops=int(flops), bytes_accessed=int(nbytes), transcendentals=0
        ),
    )(*args)


def head_mask(cols):
    width = cols // GROUP
    shape = (GROUP * SLOTS, cols)
    return (
        lax.broadcasted_iota(jnp.int32, shape, 0) // SLOTS
        == lax.broadcasted_iota(jnp.int32, shape, 1) // width
    )


def one_hot(picks, w, length):
    row = picks[pl.ds(w, 1), :]
    spots = lax.broadcasted_iota(jnp.int32, (length, GROUP * SLOTS), 0).astype(f32)
    columns = (spots == row).astype(f32)
    return columns.astype(bf16), columns.T.astype(bf16)


def copy_all(pairs, sems):
    copies = [pltpu.make_async_copy(a, b, sems.at[i]) for i, (a, b) in enumerate(pairs)]
    for copy in copies:
        copy.start()
    return copies


def split_sum(parts, at):
    return parts[at : at + 1] + parts[at + 1 : at + 2] + parts[at + 2 : at + 3]


def put_parts(extra, at, row):
    for i in range(3):
        part = row.astype(bf16).astype(f32)
        extra[at + i : at + i + 1, :] = part
        row = row - part


def pack_qkv(windows, info, w, bias, picks, piece, part, extra, sems):
    n = part.shape[1]
    rows = pl.ds(pl.multiple_of(info[7] * n, n), n)
    copies = copy_all([(w.at[j, rows, :], part.at[j]) for j in range(3)], sems)
    extra[...] = jnp.zeros_like(extra)
    for i in range(windows):
        extra[i : i + 1, : GROUP * SLOTS] = picks[pl.ds(info[2] + i, 1), :]
    put_parts(extra, windows, bias[0:1, :])
    put_parts(extra, windows + 3, bias[1:2, :])
    piece[3 * n :, :] = extra[...].astype(bf16)
    for j, copy in enumerate(copies):
        copy.wait()
        piece[j * n : (j + 1) * n, :] = part[j].astype(bf16)


def pack_rest(info, w_out, w_up, w_down, bias, piece, down_piece, out_low, up_low, down_low, extra):
    hid = w_up.shape[1] // 2
    n_out, n_up, n_down = w_out.shape[0] // 4, w_up.shape[0] // 4, w_down.shape[0] // 4
    out_low[...] = w_out[...].astype(bf16)
    up_low[...] = w_up[...].astype(bf16)
    down_low[...] = w_down[...].astype(bf16)
    extra[...] = jnp.zeros_like(extra)
    put_parts(extra, 0, bias[:, :hid])
    put_parts(extra, 3, bias[:, hid:])
    piece[:n_out, :] = out_low[pl.ds(pl.multiple_of(info[7] * n_out, n_out), n_out), :]
    rows = pl.ds(pl.multiple_of(info[7] * n_up, n_up), n_up)
    for h in range(2):
        piece[n_out + h * n_up : n_out + (h + 1) * n_up, :] = up_low[rows, h * hid : (h + 1) * hid]
    piece[n_out + 2 * n_up :, :] = extra[...].astype(bf16)
    down_piece[...] = down_low[pl.ds(pl.multiple_of(info[7] * n_down, n_down), n_down), :]


def attend(wq, bias, picks, start, emb, q_out, k_out, v_out, ctx, att, picked, length, scale):
    cols = wq.shape[2]
    e = emb[...]
    for j, out in enumerate((q_out, k_out, v_out)):
        out[...] = (nn(e, wq[j]) + bias[j]).astype(bf16)
    mask = head_mask(cols)
    mask_low = mask.astype(f32).astype(bf16)
    spots = [slice(i * length, (i + 1) * length) for i in range(emb.shape[0] // length)]
    hots = [one_hot(picks, start + i, length) for i in range(len(spots))]
    sel = [nn(down, q_out[here, :]) for (_, down), here in zip(hots, spots)]
    sel = [jnp.where(mask, x, 0.0).astype(bf16) for x in sel]
    for i, x in enumerate(sel):
        picked[i] = x
    scores = [nt(x, k_out[here, :]) * scale for x, here in zip(sel, spots)]
    active = [nn(up, mask_low) for up, _ in hots]
    exponent = [jnp.exp(x - jnp.max(x, axis=-1, keepdims=True)) for x in scores]
    probs = [x * (1.0 / jnp.sum(x, axis=-1, keepdims=True)) for x in exponent]
    for i, x in enumerate(probs):
        att[i] = x
    mixed = [nn(x.astype(bf16), v_out[here, :]) for x, here in zip(probs, spots)]
    mixed = [jnp.where(mask, x, 0.0).astype(bf16) for x in mixed]
    mean = [col_sum(v_out[here, :].astype(f32)) * (1.0 / length) for here in spots]
    mixed = [nn(up, x) for (up, _), x in zip(hots, mixed)]
    for here, x, act, m in zip(spots, mixed, active, mean):
        ctx[here, :] = (x + (1.0 - act) * m).astype(bf16)


def attend_own(length, scale, info, groups, tokens, table, w, bias, picks,
               q, k, v, ctx, att, picked, emb, emb_t, wq):
    @pl.when(pl.program_id(0) == 0)
    def _():
        for j in range(3):
            wq[j] = w[j].astype(bf16)

    per = tokens.shape[0] // length
    first = pl.program_id(0) * per
    for i in range(per):
        here = slice(i * length, (i + 1) * length)
        row = table[pl.ds(groups[info[3] + first + i], 1), :]
        emb[here, :] = (tokens[here, :].astype(f32) + row).astype(bf16)
    emb_t[...] = emb[...].astype(f32).T.astype(bf16)
    rows = (bias[0:1, :], jnp.zeros_like(bias[0:1, :]), bias[1:2, :])
    attend(wq, rows, picks, info[1] + first, emb, q, k, v, ctx, att, picked, length, scale)


def attend_far(length, scale, info, emb, p0, p1, p2, p3,
               q, k, v, ctx, att, picked, wq, picks, extra, bias, sems):
    n = wq.shape[1] // 4
    windows = picks.shape[0]

    @pl.when(pl.program_id(0) == 0)
    def _():
        pairs = [(p0.at[pl.ds(3 * n, extra.shape[0]), :], extra)]
        for i, piece in enumerate((p0, p1, p2, p3)):
            for j in range(3):
                pairs.append(
                    (
                        piece.at[pl.ds(j * n, n), :],
                        wq.at[j, pl.ds(pl.multiple_of((info[7] ^ i) * n, n), n), :],
                    )
                )
        for copy in copy_all(pairs, sems):
            copy.wait()
        rest = extra[...].astype(f32)
        picks[...] = rest[:windows, : GROUP * SLOTS]
        bias[0:1, :] = split_sum(rest, windows)
        bias[1:2, :] = split_sum(rest, windows + 3)

    rows = (bias[0:1, :], jnp.zeros_like(bias[0:1, :]), bias[1:2, :])
    first = pl.program_id(0) * (emb.shape[0] // length)
    attend(wq, rows, picks, first, emb, q, k, v, ctx, att, picked, length, scale)


def gelu_pair(x):
    bell = jnp.exp2((x * x) * (-0.5 * math.log2(math.e)))
    y = 1.0 + (0.3275911 * math.sqrt(0.5)) * jnp.abs(x)
    t = pl.reciprocal(y, approx=True)
    t = t * (2.0 - y * t)
    poly = t * (
        0.5 * 0.254829592
        + t * (0.5 * -0.284496736 + t * (0.5 * 1.421413741 + t * (0.5 * -1.453152027 + t * (0.5 * 1.061405429))))
    )
    tail = poly * bell
    phi = jnp.where(x >= 0.0, 1.0 - tail, tail)
    return x * phi, phi + (x * (1.0 / math.sqrt(2.0 * math.pi))) * bell


def feed_forward(length, parts, info, groups, tokens, table, ctx0, ctx1, near_out, near_up, near_down,
                 p0, p1, p2, p3, d0, d1, d2, d3, ff_bias, gains, shifts, cot_in,
                 out_far, gp1_far, ga_far, keep, send, sums, wo_far,
                 wo, up, dn, act, gpre, slope, nl, gb, ga, out, gp1, pre, cot, nl_t, gb_t, ffb, extra, buf,
                 sems, row_sems, end_sems):
    core, quarter = info[0], info[7]
    rows, width = tokens.shape
    block = rows // parts
    cols = wo.shape[1]
    hid = up.shape[2]
    half = hid // 2

    def rows_of(x, i, n, *rest):
        return x.at[(1, pl.ds(pl.multiple_of((quarter ^ i) * n, n), n)) + rest]

    n_out, n_up, n_down = cols // 4, width // 4, hid // 4
    pairs = [[(near_out, wo.at[0])], [(near_up, up.at[0])], [(near_down, dn.at[0])], [(cot_in, cot)]]
    pairs[1].append((p0.at[pl.ds(n_out + 2 * n_up, 16), :], extra))
    for i, (p, d) in enumerate(((p0, d0), (p1, d1), (p2, d2), (p3, d3))):
        pairs[0].append((p.at[pl.ds(0, n_out), :], rows_of(wo, i, n_out)))
        for h in range(2):
            pairs[1].append(
                (p.at[pl.ds(n_out + h * n_up, n_up), :], rows_of(up, i, n_up, pl.ds(h * half, half)))
            )
        pairs[2].append((d, rows_of(dn, i, n_down)))
    loads, at = [], 0
    for some in pairs:
        loads.append([pltpu.make_async_copy(a, b, sems.at[at + i]) for i, (a, b) in enumerate(some)])
        at += len(some)
    for some in loads:
        for copy in some:
            copy.start()
    wo_copy = pltpu.make_async_copy(wo, wo_far, end_sems.at[4])
    ffb[0:1, :] = ff_bias[...]
    for i in range(rows // length):
        here = slice(i * length, (i + 1) * length)
        pre[here, :] = tokens[here, :].astype(f32) + table[pl.ds(groups[info[3] + i], 1), :]
    for copy in loads[0]:
        copy.wait()
    wo_copy.start()

    spans = [slice(i * block, (i + 1) * block) for i in range(parts)]
    inv_one = []
    xs = [nn(ctx0[here, :], wo[0]) + nn(ctx1[here, :], wo[1]) for here in spans]
    for here, x in zip(spans, xs):
        x = pre[here, :] + (x + shifts[0:1, :])
        center = x - row_mean(x)
        inv_one.append(lax.rsqrt(row_mean(center * center) + EPS_NORM))
        unit = center * inv_one[-1]
        pre[here, :] = unit
        nl[here, :] = (unit * gains[0:1, :] + shifts[2:3, :]).astype(bf16)
    for some in loads[1:]:
        for copy in some:
            copy.wait()
    rest = extra[...].astype(f32)
    ffb[1:2, :half] = split_sum(rest, 0)
    ffb[1:2, half:] = split_sum(rest, 3)

    order = [(i, ch) for ch in range(4) for i in range(parts)]

    def lift(i, ch):
        g, o = ch // 2, (ch % 2) * half
        return nn(nl[spans[i], :], up[g, :, o : o + half])

    later = lift(*order[0])
    branch = [shifts[1:2, :]] * parts
    for k, (i, ch) in enumerate(order):
        g, o = ch // 2, (ch % 2) * half
        z = later + ffb[g : g + 1, o : o + half]
        if k + 1 < len(order):
            later = lift(*order[k + 1])
        a, d = gelu_pair(z)
        a = a.astype(bf16)
        act[spans[i], ch * half : (ch + 1) * half] = a
        slope[spans[i], ch * half : (ch + 1) * half] = d.astype(bf16)
        branch[i] = branch[i] + nn(a, dn[g, o : o + half, :])
    total = []
    tops = [0.0] * 3
    for here, x in zip(spans, branch):
        y = pre[here, :] * gains[0:1, :] + shifts[2:3, :] + x
        center = y - row_mean(y)
        inv_two = lax.rsqrt(row_mean(center * center) + EPS_NORM)
        unit_two = center * inv_two
        out[here, :] = unit_two * gains[1:2, :] + shifts[3:4, :]
        c = cot[here, :]
        g2 = c * gains[1:2, :]
        gp2 = (g2 - row_mean(g2) - unit_two * row_mean(g2 * unit_two)) * inv_two
        low = gp2.astype(bf16)
        gb[here, :] = low
        tops = [t + col_sum(x) for t, x in zip(tops, (c * unit_two, c, low.astype(f32)))]
        total.append(gp2)
    sums[...] = jnp.zeros_like(sums)
    sums[1:2, :] = tops[0]
    sums[5:6, :] = tops[1]
    sums[3:4, :] = tops[2]

    def lower(i, ch):
        g, o = ch // 2, (ch % 2) * half
        return nt(gb[spans[i], :], dn[g, o : o + half, :])

    later = lower(*order[0])
    for k, (i, ch) in enumerate(order):
        g, o = ch // 2, (ch % 2) * half
        p = later * slope[spans[i], ch * half : (ch + 1) * half].astype(f32)
        if k + 1 < len(order):
            later = lower(*order[k + 1])
        p = p.astype(bf16)
        gpre[spans[i], ch * half : (ch + 1) * half] = p
        sums[6 + ch : 7 + ch, :] += col_sum(p.astype(f32))
        total[i] = total[i] + nt(p, up[g, :, o : o + half])
    tops = [0.0] * 3
    for here, x, inv in zip(spans, total, inv_one):
        unit_one = pre[here, :]
        g1 = x * gains[0:1, :]
        gp = (g1 - row_mean(g1) - unit_one * row_mean(g1 * unit_one)) * inv
        gp1[here, :] = gp
        low_one = gp.astype(bf16)
        ga[here, :] = low_one
        tops = [t + col_sum(v) for t, v in zip(tops, (x * unit_one, x, low_one.astype(f32)))]
    sums[0:1, :] = tops[0]
    sums[4:5, :] = tops[1]
    sums[2:3, :] = tops[2]
    ends = [
        pltpu.make_async_copy(a, b, row_sems.at[j])
        for j, (a, b) in enumerate(((ga, ga_far), (gp1, gp1_far), (out, out_far)))
    ] + [wo_copy]
    for copy in ends[:3]:
        copy.start()
    for i in range(rows // length):
        spot = pl.ds(10 + groups[info[3] + i], 1)
        sums[spot, :] += col_sum(gp1[i * length : (i + 1) * length, :])
    nl_t[...] = nl[...].astype(f32).T.astype(bf16)
    gb_t[...] = gb[...].astype(f32).T.astype(bf16)
    n = buf.shape[1] // 2
    for g, ctx in ((1, ctx1), (0, ctx0)):
        buf[g, 2 * hid : 2 * hid + cols, :] = nn(ctx[...].astype(f32).T.astype(bf16), ga[...]).astype(bf16)
        for ch in (2 * g, 2 * g + 1):
            o = (ch % 2) * half
            at = slice(ch * half, (ch + 1) * half)
            buf[g, o : o + half, :] = nn(nl_t[...], gpre[:, at]).astype(bf16)
            buf[g, hid + o : hid + o + half, :] = nn(gb_t[...], act[:, at]).astype(bf16)
        for dst, spot in ((send, 1 - core), (keep, core)):
            copy = pltpu.make_async_copy(
                buf.at[g, pl.ds(pl.multiple_of(spot * n, 32), n), :], dst.at[g], end_sems.at[2 * g + (dst is keep)]
            )
            copy.start()
            ends.append(copy)
    for copy in ends:
        copy.wait()


def attend_back(length, scale, g, info, groups, ga, emb_in, wo, picks, wq_in, k_in, v_in, att, picked, *refs):
    last = g == 0
    if last:
        sums, tsum_far, total_far, *refs = refs
    gq, gk, gv, keep, send, *refs = refs
    if not last:
        tsum, total_out, *refs = refs
    gq_all, gk_all, gv_all, emb_t, wq, buf, *refs = refs
    if last:
        tsum, small, *refs = refs
    (sems,) = refs
    core = info[0]
    step = pl.program_id(0)
    width, rows = emb_t.shape
    block = ga.shape[0]
    per = block // length
    cols = wq.shape[2]
    half = width // 2
    mask = head_mask(cols)
    mask_low = mask.astype(f32).astype(bf16)
    late = [
        pltpu.make_async_copy(a, b, sems.at[8 + i]) for i, (a, b) in enumerate(((emb_in, emb_t), (wq_in, wq)))
    ]

    @pl.when(step == 0)
    def _():
        for copy in late:
            copy.start()
        tsum[...] = jnp.zeros_like(tsum)

    start = (info[1] if last else 0) + step * per
    spots = [slice(i * length, (i + 1) * length) for i in range(per)]
    g_ctx = nt(ga[...], wo[g]).astype(bf16)
    hots = [one_hot(picks, start + i, length) for i in range(per)]
    ge = [nn(down, g_ctx[here, :]) for here, (_, down) in zip(spots, hots)]
    ge = [jnp.where(mask, x, 0.0).astype(bf16) for x in ge]
    active = [nn(up, mask_low) for up, _ in hots]
    gprobs = [nt(x, v_in[here, :]) for here, x in zip(spots, ge)]
    low_t = [att[i].T.astype(bf16) for i in range(per)]
    gmean = [
        col_sum((1.0 - x) * g_ctx[here, :].astype(f32)) * (1.0 / length) for here, x in zip(spots, active)
    ]
    g_value = [nn(x, y) for x, y in zip(low_t, ge)]
    weighted = [att[i] * x for i, x in enumerate(gprobs)]
    graw = [(x - att[i] * jnp.sum(x, axis=-1, keepdims=True)) * scale for i, x in enumerate(weighted)]
    gpick = [nn(x.astype(bf16), k_in[here, :]) for here, x in zip(spots, graw)]
    graw_t = [x.T.astype(bf16) for x in graw]
    g_value = [(x + m).astype(bf16) for x, m in zip(g_value, gmean)]
    gpick = [jnp.where(mask, x, 0.0).astype(bf16) for x in gpick]
    g_key = [nn(x, picked[i]).astype(bf16) for i, x in enumerate(graw_t)]
    g_query = [nn(up, x).astype(bf16) for (up, _), x in zip(hots, gpick)]
    for i, three in enumerate(zip(g_query, g_key, g_value)):
        rows_here = pl.ds(pl.multiple_of(step * block + i * length, 32), length)
        group = groups[info[3] + step * per + i]
        for j, (x, dst, dst_all) in enumerate(zip(three, (gq, gk, gv), (gq_all, gk_all, gv_all))):
            dst[spots[i], :] = x
            dst_all[rows_here, :] = x
            tsum[pl.ds(2 * j + group, 1), :] += col_sum(x.astype(f32))

    @pl.when(step == rows // block - 1)
    def _():
        for copy in late:
            copy.wait()
        n = 3 * half // 2
        pairs = []
        for j, x in enumerate((gq_all, gk_all, gv_all)):
            r = nn(emb_t[...], x[...]).astype(bf16)
            buf[j * half : (j + 1) * half, :cols] = r[:half]
            buf[j * half : (j + 1) * half, cols:] = r[half:]
        for dst, spot in ((send, 1 - core), (keep, core)):
            pairs.append((buf.at[at_row(spot * n, n), :], dst.at[pl.ds(0, n), :]))
        copies = copy_all(pairs, sems)
        total = jnp.zeros((8, width), f32)
        for j in range(3):
            x = tsum[2 * j : 2 * j + 8, :]
            hi = x.astype(bf16)
            lo = (x - hi.astype(f32)).astype(bf16)
            total = total + nt(hi, wq[j]) + nt(lo, wq[j])
        if last:
            total = total + total_far[...]
            small[...] = jnp.zeros_like(small)
            for m, t in enumerate((tsum, tsum_far)):
                at = 16 * m
                small[at : at + 2, :] = total[0:2] + sums[10:12, :]
                small[at + 2 : at + 8, :] = sums[0:6, :]
                small[at + 8 : at + 10, :] = sums[6 + 2 * m : 8 + 2 * m, :]
                small[at + 10 : at + 11, :cols] = t[0:1, :] + t[1:2, :]
                small[at + 10 : at + 11, cols:] = t[4:5, :] + t[5:6, :]
            buf[2 * n :, :] = small[...].astype(bf16)
            more = [
                pltpu.make_async_copy(buf.at[pl.ds(2 * n, 32), :], dst.at[pl.ds(n, 32), :], sems.at[2 + i])
                for i, dst in enumerate((send, keep))
            ]
            for copy in more:
                copy.start()
            copies += more
        else:
            total_out[...] = total
        for copy in copies:
            copy.wait()


def input_grad(*refs):
    (*grads, wq0, wq1, gp1, out) = refs
    total = gp1[...]
    for i, x in enumerate(grads):
        total = total + nt(x[...], (wq0, wq1)[i // 3][i % 3])
    out[...] = total


def hop(x, *bits):
    heads = lax.axis_size("head")
    flip = sum((1 << k) * (heads if axis == "dp" else 1) for axis, k in bits)
    count = lax.axis_size("dp") * heads
    return lax.ppermute(x, ("dp", "head"), [(i, i ^ flip) for i in range(count)])


def side(bit):
    axis, k = bit
    return (lax.axis_index(axis) >> k) & 1


def subsets(bits):
    return [[b for i, b in enumerate(bits) if (r >> i) & 1] for r in range(1 << len(bits))]


def pair_sum(terms):
    while len(terms) > 1:
        terms = [terms[i] + terms[i + 1] for i in range(0, len(terms), 2)]
    return terms[0]


def pick(x, bits, far, flips):
    for bit in bits:
        flipped = bit in flips
        if bit == far:
            x = x[1:] if flipped else x[:1]
        else:
            n = x.shape[1] // 2
            x = lax.dynamic_slice_in_dim(x, (side(bit) ^ int(flipped)) * n, n, 1)
    return x


def scatter_sum(x, bits, far, small=None):
    terms, rest = [], []
    for flips in subsets(bits):
        part = pick(x, bits, far, flips)
        if small is not None:
            part = jnp.concatenate([part, pick(small, [far] if far in bits else [], far, flips)], 1)
        if flips:
            part = hop(part, *flips)
        terms.append(part.astype(f32))
    total = pair_sum(terms).astype(bf16)
    if small is None:
        return total
    n = total.shape[1] - small.shape[1]
    return total[:, :n], total[:, n:]


def gather(x, bits):
    parts = {}
    for r, flips in enumerate(subsets(bits)):
        parts[r] = hop(x, *flips) if flips else x
    for i, bit in enumerate(bits):
        m = side(bit) == 0
        parts = {
            r: jnp.where(m, parts[r], parts[r ^ (1 << i)]) for r in parts
        }
    order = sorted(parts, key=lambda r: [(r >> i) & 1 for i in range(len(bits))])
    return jnp.concatenate([parts[r] for r in order], axis=0)


def plus(a, b):
    return (a.astype(f32) + b.astype(f32)).astype(bf16)


def late_steps(small_rows, bits, far, core):
    stages = [[far, bits[0]]] + [bits[i : i + 2] for i in range(1, len(bits), 2)]

    def cores(state):
        x = plus(state[0], hop(state[1], core))
        return x[:, :-small_rows], x[:, -small_rows:]

    def down(stage):
        return lambda state: scatter_sum(state[0], stage, far, state[1])

    def up(stage):
        wanted = [b for b in stage if b != far]

        def step(state):
            x = state[0] if state[0].ndim == 2 else state[0][0]
            return gather(x, wanted), state[1]

        return step

    return [cores] + [down(s) for s in stages] + [up(s) for s in reversed(stages)] + [up([core])]


def early_steps(bits, far, core):
    first, second, rest = bits[0], bits[1], bits[2:]
    orders = ((far, first, second), (first, second, far), (second, far, first))

    def start(x):
        part = x.shape[1] // 3
        return down(0)([x[:, i * part : (i + 1) * part] for i in range(3)])

    def down(stage):
        return lambda chunks: [scatter_sum(c, [order[stage]], far) for c, order in zip(chunks, orders)]

    def swap(chunks):
        x = jnp.concatenate(chunks, axis=2)[0]
        for bit in rest:
            x = plus(x, hop(x, bit))
        width = x.shape[1] // 3
        return [x[:, : 2 * width], x[:, 2 * width :]]

    def up_one(parts):
        return [gather(parts[0], [second]), gather(parts[1], [first])]

    def up_two(parts):
        two, one = gather(parts[0], [first]), gather(parts[1], [second])
        width = one.shape[1]
        return jnp.concatenate([two[:, :width], two[:, width:], one], axis=0)

    return [start, down(1), down(2), swap, up_one, up_two, lambda x: gather(x, [core])]


def add(a, b):
    return a.astype(f32) + b.astype(f32)


def at_row(start, n):
    return pl.ds(pl.multiple_of(start, 16), n)


def merge_cores(info, keep, got, stay0, far0, stay1, first1, stay2, second2):
    n = keep.shape[1] // 3
    h = n // 2
    a, b = info[4], info[5]
    stay0[...] = add(keep[0, :n], got[0, :n]).astype(bf16)
    far0[...] = add(keep[1, :n], got[1, :n]).astype(bf16)
    for base, bit, stay, send in ((n, a, stay1, first1), (2 * n, b, stay2, second2)):
        for dst, m in ((stay, bit), (send, 1 - bit)):
            here = at_row(base + m * h, h)
            for g in range(2):
                dst[g] = add(keep[g, here], got[g, here]).astype(bf16)


def merge_two(info, stay0, got0, stay1, got1, stay2, got2, keep0, first0, keep1, second1, keep2, far2):
    a, b = info[4], info[5]
    h = stay0.shape[0] // 2
    for dst, m in ((keep0, a), (first0, 1 - a)):
        here = at_row(m * h, h)
        dst[...] = add(stay0[here], got0[here]).astype(bf16)
    q = stay1.shape[1] // 2
    for dst, m in ((keep1, b), (second1, 1 - b)):
        here = at_row(m * q, q)
        for g in range(2):
            dst[g] = add(stay1[g, here], got1[g, here]).astype(bf16)
    keep2[...] = add(stay2[0], got2[0]).astype(bf16)
    far2[...] = add(stay2[1], got2[1]).astype(bf16)


def merge_three(info, in0, got0, in1, got1, in2, got2, stay, to_second, to_far, to_first):
    a, b = info[4], info[5]
    q = to_far.shape[0]
    stay[:q] = add(in0[at_row(b * q, q)], got0[at_row(b * q, q)]).astype(bf16)
    to_second[...] = add(in0[at_row((1 - b) * q, q)], got0[at_row((1 - b) * q, q)]).astype(bf16)
    stay[q : 2 * q] = add(in1[0], got1[0]).astype(bf16)
    to_far[...] = add(in1[1], got1[1]).astype(bf16)
    stay[2 * q :] = add(in2[at_row(a * q, q)], got2[at_row(a * q, q)]).astype(bf16)
    to_first[...] = add(in2[at_row((1 - a) * q, q)], got2[at_row((1 - a) * q, q)]).astype(bf16)


def merge_four(info, stay, second, far, first, keep0, got0, keep1, got1, part, mine, to_first, to_far, to_both):
    q = second.shape[0]
    for i, x in enumerate((second, far, first)):
        part[i * q : (i + 1) * q] = add(stay[i * q : (i + 1) * q], x[...]).astype(bf16)
    a = info[4]
    h = mine.shape[0] - 16
    for dst, keep, got, g, m in (
        (mine, keep0, got0, 0, a), (to_first, keep0, got0, 0, 1 - a),
        (to_far, keep1, got1, 1, a), (to_both, keep1, got1, 1, 1 - a),
    ):
        here = at_row(m * h, h)
        tail = slice(2 * h + 16 * g, 2 * h + 16 * g + 16)
        dst[:h] = add(keep[here], got[here]).astype(bf16)
        dst[h:] = add(keep0[tail], got0[tail]).astype(bf16)


def merge_five(info, part, third, mine, first, far, both, own, to_second, to_first, to_third, to_both, total):
    q = part.shape[0] // 3
    to_second[: 2 * q] = add(part[: 2 * q], third[: 2 * q]).astype(bf16)
    to_first[...] = add(part[2 * q :], third[2 * q :]).astype(bf16)
    total[...] = (add(mine[...], first[...]) + add(far[...], both[...])).astype(bf16)
    n = own.shape[0] - 16
    spot = 2 * info[5] + info[6]
    for dst, base, flip in ((own, 0, 0), (to_second, 2 * q, 2), (to_third, 0, 1), (to_both, 0, 3)):
        dst[base : base + n] = total[at_row((spot ^ flip) * n, n)]
        dst[base + n : base + n + 16] = total[4 * n :]


def merge_six(info, near2, got2, near1, got1, own, third, both,
              to_first, to_second, to_third, table, gains, shifts, ff, bias):
    a, b = info[4], info[5]
    q = near1.shape[0]
    for c in range(2):
        to_first[at_row(2 * c * q + b * q, q)] = near2[c * q : (c + 1) * q]
        to_first[at_row(2 * c * q + (1 - b) * q, q)] = got2[c * q : (c + 1) * q]
    to_second[at_row(a * q, q)] = near1[...]
    to_second[at_row((1 - a) * q, q)] = got1[...]
    s = add(own[...], got2[2 * q :]) + add(third[...], both[...])
    h = own.shape[0] - 16
    to_third[...] = s[:h].astype(bf16)
    to_second[2 * q :] = to_third[...]
    s = s[h:]
    width = s.shape[1]
    table[...] = s[0:2]
    gains[...] = s[2:4]
    shifts[...] = s[4:8]
    ff[:, :width] = s[8:9]
    ff[:, width:] = s[9:10]
    bias[0:1] = s[10:11, : width // 2]
    bias[1:2] = s[10:11, width // 2 :]


def merge_seven(info, near1, got1, near2, got2, near3, got3, both, out, two):
    a, b = info[4], info[5]
    h = near1.shape[0] // 2
    for c in range(2):
        out[at_row(2 * c * h + a * h, h)] = near1[c * h : (c + 1) * h]
        out[at_row(2 * c * h + (1 - a) * h, h)] = got1[c * h : (c + 1) * h]
    out[at_row(4 * h + b * h, h)] = near2[:h]
    out[at_row(4 * h + (1 - b) * h, h)] = got2[:h]
    spot = 2 * b + info[6]
    n = near3.shape[0]
    for src, base, flip in ((near3, 0, 0), (got2, h, 2), (got3, 0, 1), (both, 0, 3)):
        two[at_row((spot ^ flip) * n, n)] = src[base : base + n]


def merge_eight(info, near, got, out):
    n = near.shape[0]
    out[at_row(info[4] * n, n)] = near[...]
    out[at_row((1 - info[4]) * n, n)] = got[...]


def merge(body, info, ins, outs, width, with_info=True):
    shapes = [(s if isinstance(s, tuple) else (s, width), bf16, VMEM) for s in outs]
    return call(
        body,
        shapes,
        [SMEM] * with_info + [VMEM] * len(ins),
        ((info,) if with_info else ()) + tuple(ins),
        [],
        24,
        2 * US,
        2e6,
        hbm_in=False,
        hbm_out=False,
    )


def sum_start(info, keep, send, bits, far, core):
    first, second, _ = bits
    width = keep.shape[2]
    n = keep.shape[1] // 3
    two = (2, n // 2, width)
    stay0, far0, stay1, first1, stay2, second2 = merge(
        merge_cores, info, (keep, hop(send, core)), (n, n, two, two, two, two), width
    )
    return (stay0, hop(far0, far), stay1, hop(first1, first), stay2, hop(second2, second))


def sum_middle(info, state, bits, far, width):
    first, second, _ = bits
    n = state[0].shape[0]
    q = n // 4
    keep0, first0, keep1, second1, keep2, far2 = merge(
        merge_two, info, state, (n // 2, n // 2, (2, q, width), (2, q, width), n // 2, n // 2), width
    )
    return (keep0, hop(first0, first), keep1, hop(second1, second), keep2, hop(far2, far))


def sum_finish(info, state, late, bits, far, core, beside):
    first, second, third = bits
    width = state[0].shape[1]
    q = state[0].shape[0] // 2
    keep0, send0, keep1, got1 = late
    stay, to_second, to_far, to_first = merge(merge_three, info, state, (3 * q, q, q, q), width)
    send0, stay = lax.optimization_barrier((send0, stay))
    got0 = hop(send0, core)
    h = keep1.shape[0] // 2
    part, mine, to_first, to_far, to_both = merge(
        merge_four,
        info,
        (stay, hop(to_second, second), hop(to_far, far), hop(to_first, first), keep0, got0, keep1, got1),
        (3 * q, h + 16, h + 16, h + 16, h + 16),
        width,
    )
    many = beside[0](part)
    got = hop(part, third), hop(to_first, first), hop(to_far, far), hop(to_both, first, far)
    part, many[0] = lax.optimization_barrier((part, many[0]))
    m = h // 4
    own, to_second, to_first, to_third, to_both, _ = merge(
        merge_five,
        info,
        (part, got[0], mine, *got[1:]),
        (m + 16, 2 * q + m + 16, q, m + 16, m + 16, h + 16),
        width,
    )
    few = beside[2](own)
    got = hop(to_second, second), hop(to_first, first), hop(to_third, third), hop(to_both, second, third)
    own, few[0] = lax.optimization_barrier((own, few[0]))
    to_first, to_second, to_third, *small = call(
        merge_six,
        [((4 * q, width), bf16, VMEM), ((2 * q + m, width), bf16, VMEM), ((m, width), bf16, VMEM)]
        + [(shape, f32, VMEM) for shape in ((2, width), (2, width), (4, width), (1, 2 * width), (2, width // 2))],
        [SMEM] + [VMEM] * 7,
        (info, to_second, got[0], to_first, got[1], own, got[2], got[3]),
        [],
        24,
        2 * US,
        2e6,
        hbm_in=False,
        hbm_out=False,
    )
    rows = beside[1](to_third)
    got = hop(to_first, first), hop(to_second, second), hop(to_third, third), hop(to_third, second, third)
    to_first, rows = lax.optimization_barrier((to_first, rows))
    one, two = merge(
        merge_seven, info, (to_first, got[0], to_second, got[1], to_third, got[2], got[3]), (12 * q, 4 * m), width
    )
    other = hop(one, core)
    got = hop(two, first)
    (two,) = merge(merge_eight, info, (two, got), (8 * m,), width)
    return (one, other), (two, hop(two, core)), small, (many, rows, few)


def wipe(*refs):
    sems = refs[-1]
    count = sems.shape[0]
    outs, zeros = refs[1 : 1 + count], refs[1 + count : -1]
    for zero in zeros:
        zero[...] = jnp.zeros_like(zero)
    copies = []
    for i, out in enumerate(outs):
        src = next(z for z in zeros if z.dtype == out.dtype and z.shape[1] == out.shape[1])
        rows = out.shape[0]
        n = next(c for c in (256, 192, 128, 64, 32, 16) if rows % c == 0)
        for at in range(0, rows, n):
            copies.append(
                pltpu.make_async_copy(
                    src.at[pl.ds(0, n), :], out.at[pl.ds(at, n), :], sems.at[i]
                )
            )
    for copy in copies:
        copy.start()
    for copy in copies:
        copy.wait()


def blanks_for(gate, likes):
    flat = [(math.prod(x.shape[:-1]), x.shape[-1]) for x in likes]
    widths = sorted({n for _, n in flat})
    outs = call(
        wipe,
        [(s, x.dtype, HBM) for s, x in zip(flat, likes)],
        [HBM],
        (gate,),
        [pltpu.VMEM((256, n), k) for n in widths for k in (f32, bf16)]
        + [pltpu.SemaphoreType.DMA((len(likes),))],
        8,
        US // 2,
        1e6,
        hbm_in=False,
    )
    return [x.reshape(like.shape) for x, like in zip(outs, likes)]


def moments(turned, m, v):
    first = BETA_ONE * m[...] + (1.0 - BETA_ONE) * turned
    second = BETA_TWO * v[...] + (1.0 - BETA_TWO) * (turned * turned)
    m[...] = first
    v[...] = second
    return (first / (jnp.sqrt(second) + EPS_ADAM)).astype(bf16)


def fetch(pairs, sems):
    for copy in copy_all(pairs, sems):
        copy.wait()


def step_wide(g, w, m, v, ql, qr, rate, scratch, ready):
    low_l, low_r, mid, back = scratch
    low_l[...] = ql[...].astype(bf16)
    low_r[...] = qr[...].astype(bf16)
    blocks, size = qr.shape[0], qr.shape[1]
    mid[...] = nn(ql[...].T.astype(bf16), g).astype(bf16)
    for b in range(blocks):
        at = slice(b * size, (b + 1) * size)
        u = moments(nn(mid[:, at], low_r[b]), m.at[:, at], v.at[:, at])
        back[:, at] = nt(u, low_r[b]).astype(bf16)
    ready()
    w[...] = w[...] - rate * nn(low_l[...], back[...])


def step_tall(g, w, m, v, ql, qr, rate, scratch, ready):
    low_r, mid, back = scratch
    low_r[...] = qr[...].astype(bf16)
    blocks, size = ql.shape[0], ql.shape[1]
    for b in range(blocks):
        at = slice(b * size, (b + 1) * size)
        mid[at, :] = nn(ql[b].T.astype(bf16), g[at, :]).astype(bf16)
    u = moments(nn(mid[...], low_r[...]), m, v)
    ready()
    back[...] = nt(u, low_r[...]).astype(bf16)
    for b in range(blocks):
        at = slice(b * size, (b + 1) * size)
        w[at, :] = w[at, :] - rate * nn(ql[b].astype(bf16), back[at, :])


def update_qkv(rate, mine, g, w_in, m_in, v_in, ql_in, qr_in, *refs):
    outs, (grad, new, mom, var, copy) = refs[:4], refs[4:9]
    w, m, v, c, ql, qr, low_l, low_r, mid, back, sems = refs[9:]
    for j in range(3):
        grad[j] = g[j].astype(f32)

        @pl.when(mine[j] == 1)
        def _():
            fetch(
                [(w_in.at[j], w), (m_in.at[j], m), (v_in.at[j], v), (ql_in.at[j], ql), (qr_in.at[j], qr)], sems
            )
            step_wide(g[j], w, m, v, ql, qr, rate, (low_l, low_r, mid, back), lambda: None)
            c[...] = w[...].astype(bf16)
            fetch([(w, new.at[j]), (m, mom.at[j]), (v, var.at[j]), (c, copy.at[j])], sems)


def update_rest(rate_out, rate_up, rate_down, mine, g_out, g_up, g_down_t, *refs):
    (wo_in, mo_in, vo_in, lo_in, ro_in, wu_in, mu_in, vu_in, lu_in, ru_in,
     wd_in, md_in, vd_in, ld_in, rd_in) = refs[:15]
    refs = refs[15 + 11 :]
    grad_o, grad_u, grad_d = refs[:3]
    new_o, moments_o, copy_o, new_u, mom_u, var_u, copy_u, new_d, mom_d, var_d, copy_d = refs[3:14]
    (wo, mo, vo, co, lo, ro, low_ro, mid_o, back_o,
     wu, mu, vu, cu, lu, ru, low_lu, low_ru, mid_u, back_u,
     wd, md, vd, cd, mid_d, back_d, sems) = refs[14:]
    grad_o[...] = g_out[...].astype(f32)
    grad_u[...] = g_up[...].astype(f32)
    grad_d[...] = g_down_t[...].astype(f32).T

    @pl.when(mine[3] == 1)
    def _():
        fetch([(wo_in, wo), (mo_in, mo), (vo_in, vo), (lo_in, lo), (ro_in, ro)], sems)
        step_tall(g_out[...], wo, mo, vo, lo, ro, rate_out, (low_ro, mid_o, back_o), lambda: None)
        co[...] = wo[...].astype(bf16)
        fetch([(wo, new_o), (mo, moments_o.at[0]), (vo, moments_o.at[1]), (co, copy_o)], sems)

    @pl.when(mine[4] == 1)
    def _():
        fetch([(wu_in, wu), (mu_in, mu), (vu_in, vu), (lu_in, lu), (ru_in, ru)], sems)
        step_wide(g_up[...], wu, mu, vu, lu, ru, rate_up, (low_lu, low_ru, mid_u, back_u), lambda: None)
        cu[...] = wu[...].astype(bf16)
        fetch([(wu, new_u), (mu, mom_u), (vu, var_u), (cu, copy_u)], sems)

    @pl.when(mine[5] == 1)
    def _():
        fetch([(wd_in, wd), (md_in, md), (vd_in, vd), (ld_in, ru), (rd_in, lu)], sems)
        step_tall(grad_d[...].astype(bf16), wd, md, vd, ru, lu, rate_down, (low_lu, mid_d, back_d), lambda: None)
        cd[...] = wd[...].astype(bf16)
        fetch([(wd, new_d), (md, mom_d), (vd, var_d), (cd, copy_d)], sems)


def update_all(rate_out, rate_wide, rate_down, cols, hid, owned, info, mine, other, mine_q, other_q, *refs):
    ins, refs = refs[:20], refs[20 + 15 :]
    grad_q, grad_o, grad_u, grad_d = refs[:4]
    outs, held, refs = refs[4:19], refs[19:39], refs[39:]
    wq, mq, vq, lq, rq, wo, mo, vo, lo, ro, wu, mu, vu, lu, ru, wd, md, vd, ld, rd = held
    new_q, mom_q, var_q, copy_q, new_o, mom_o, copy_o, new_u, mom_u, var_u, copy_u, new_d, mom_d, var_d, copy_d = outs
    buf, buf_q, gq, go, gu, gd, cq, co, cu, cd = refs[:10]
    low_l, low_r64, low_r256, mid_q, mid_o, mid_u, mid_d, back_q, back_o, back_u, back_d = refs[10:21]
    sems, in_sems, out_sems = refs[21:]
    core = info[0]
    loads = []
    for k in (4, 5, 3, 0, 1, 2):
        base = 5 * max(k - 2, 0)
        some = [(a.at[k], b.at[k]) if k < 3 else (a, b) for a, b in zip(ins[base : base + 5], held[base : base + 5])]
        some = [pltpu.make_async_copy(a, b, in_sems.at[k, i]) for i, (a, b) in enumerate(some)]
        loads.append((k, some))

        @pl.when(owned[k] == 1)
        def _(some=some):
            for copy in some:
                copy.start()

    loads = dict(loads)
    width = buf.shape[1]
    half = width // 2
    n = mine.shape[0]
    n_q = mine_q.shape[0]
    fills = copy_all(
        [(mine, buf.at[at_row(core * n, n)]), (other, buf.at[at_row((1 - core) * n, n)]),
         (mine_q, buf_q.at[at_row(core * n_q, n_q)]), (other_q, buf_q.at[at_row((1 - core) * n_q, n_q)])],
        sems,
    )
    pending = []

    def give(scratch, out, k):
        copy = pltpu.make_async_copy(scratch, out, sems.at[4 + k])
        copy.start()
        pending.append((None, copy))

    def finish(k, w, m, v, c, outs, run):
        stores = [
            pltpu.make_async_copy(a, b, out_sems.at[k, i]) for i, (a, b) in enumerate(zip((w, m, v, c), outs))
        ]

        @pl.when(owned[k] == 1)
        def _():
            for copy in loads[k]:
                copy.wait()

            def ready():
                stores[1].start()
                stores[2].start()

            run(ready)
            stores[0].start()
            c[...] = w[...].astype(bf16)
            stores[3].start()

        pending.extend((owned[k] == 1, copy) for copy in stores)

    fills[0].wait()
    fills[1].wait()
    h = hid // 2
    for i in range(2):
        gu[:, i * h : (i + 1) * h] = buf[i * width : (i + 1) * width, :].astype(f32)
    give(gu, grad_u, 0)
    finish(4, wu, mu, vu, cu, (new_u, mom_u, var_u, copy_u),
           lambda ready: step_wide(gu[...].astype(bf16), wu, mu, vu, lu, ru, rate_wide,
                                   (low_l, low_r256, mid_u, back_u), ready))
    for i in range(2):
        gd[i * h : (i + 1) * h, :] = buf[hid + i * width : hid + (i + 1) * width, :].astype(f32).T
    give(gd, grad_d, 1)
    finish(5, wd, md, vd, cd, (new_d, mom_d, var_d, copy_d),
           lambda ready: step_tall(gd[...].astype(bf16), wd, md, vd, ld, rd, rate_down,
                                   (low_l, mid_d, back_d), ready))
    go[...] = buf[2 * hid : 2 * hid + cols, :].astype(f32)
    give(go, grad_o, 2)
    finish(3, wo, mo, vo, co, (new_o, mom_o.at[0], mom_o.at[1], copy_o),
           lambda ready: step_tall(go[...].astype(bf16), wo, mo, vo, lo, ro, rate_out,
                                   (low_l, mid_o, back_o), ready))
    fills[2].wait()
    fills[3].wait()
    for j in range(3):
        x = buf_q[j * half : (j + 1) * half, :].astype(f32)
        gq[j, :half, :] = x[:, :cols]
        gq[j, half:, :] = x[:, cols:]
        give(gq.at[j], grad_q.at[j], 3 + j)
        finish(j, wq.at[j], mq.at[j], vq.at[j], cq.at[j], [x.at[j] for x in (new_q, mom_q, var_q, copy_q)],
               lambda ready, j=j: step_wide(gq[j].astype(bf16), wq.at[j], mq.at[j], vq.at[j], lq.at[j], rq.at[j],
                                            rate_wide, (low_l, low_r64, mid_q, back_q), ready))
    for flag, copy in pending:
        if flag is None:
            copy.wait()
        else:

            @pl.when(flag)
            def _(copy=copy):
                copy.wait()


def pad_picks(picks):
    windows, heads, slots = picks.shape
    return jnp.pad(picks, ((0, 0), (0, 0), (0, SLOTS - slots)), constant_values=-1).reshape(
        windows, heads * SLOTS
    )


def per_device(
    tokens_in,
    cotangent,
    data_table,
    window_group,
    query_picks,
    owner_list,
    weight_qkv,
    head_bias,
    weight_out,
    weight_up,
    ff_bias,
    weight_down,
    norm_gains,
    shifts,
    first_qkv,
    second_qkv,
    first_out,
    second_out,
    first_up,
    second_up,
    first_down,
    second_down,
    basis_qkv_left,
    basis_qkv_right,
    basis_out_left,
    basis_out_right,
    basis_up_left,
    basis_up_right,
    basis_down_left,
    basis_down_right,
):
    head_count = lax.axis_size("head")
    head = lax.axis_index("head")
    my_rank = lax.axis_index("dp")
    rows, width = tokens_in.shape
    length = rows * head_count // window_group.shape[0]
    windows = rows // length
    head_dim = basis_qkv_right.shape[-1]
    cols = GROUP * head_dim
    scale = 1.0 / math.sqrt(head_dim)
    head_bits = head_count.bit_length() - 1
    far = ("head", head_bits - 1)
    core_bit = ("dp", 0)
    dp_bits = lax.axis_size("dp").bit_length() - 1
    bits = [("dp", k) for k in range(1, dp_bits)] + [("head", k) for k in range(head_bits - 1)]
    core = my_rank & 1
    quarter = my_rank & 3
    second_bit = ("dp", 1)
    slots = GROUP * SLOTS
    half = width // 2

    if head_count == 2:
        n_qkv, n_bias, n_out, n_up, n_ff, n_down = (
            weight_qkv, head_bias, weight_out, weight_up, ff_bias, weight_down
        )
        picks = pad_picks(query_picks).astype(f32)
        near_at, far_at = head * windows, (1 - head) * windows
    else:
        def whole_of(x, dim):
            return lax.all_gather(x, "head", axis=dim, tiled=True)

        def pick_group(x, dim, g):
            n = x.shape[dim] // 2
            return lax.dynamic_slice_in_dim(x, (side(far) ^ g) * n, n, dim)

        both = [
            (whole_of(weight_qkv.astype(bf16), 2).astype(f32), 2),
            (whole_of(head_bias, 1), 1),
            (whole_of(weight_out.astype(bf16), 0).astype(f32), 0),
            (whole_of(weight_up.astype(bf16), 1).astype(f32), 1),
            (whole_of(ff_bias, 0), 0),
            (whole_of(weight_down.astype(bf16), 0).astype(f32), 0),
        ]
        n_qkv, n_bias, n_out, n_up, n_ff, n_down = (pick_group(x, d, 0) for x, d in both)
        away = [pick_group(x, d, 1) for x, d in both]
        picks = lax.dynamic_slice_in_dim(whole_of(query_picks, 1), head * windows, windows, 0)
        picks = jnp.concatenate([pad_picks(pick_group(picks, 1, g)) for g in range(2)]).astype(f32)
        near_at, far_at = jnp.int32(0), jnp.int32(windows)
    info = jnp.stack([core, near_at, far_at, head * windows] + [side(b) for b in bits[:3]] + [quarter]).astype(jnp.int32)
    quick = head_count == 2 and len(bits) == 3
    hid = n_up.shape[1]
    extra_rows = -(-(windows + 6) // 16) * 16
    buf_rows = 2 * hid + cols
    rest_rows = cols // 4 + width // 2 + 16

    def send_qkv(info, w, bias):
        return call(
            lambda *refs: pack_qkv(windows, *refs),
            [((3 * width // 4 + extra_rows, cols), bf16, VMEM)],
            [SMEM, HBM, VMEM, VMEM],
            (info, w, bias, picks),
            [
                pltpu.VMEM((3, width // 4, cols), f32),
                pltpu.VMEM((extra_rows, cols), f32),
                pltpu.SemaphoreType.DMA((3,)),
            ],
            12,
            2 * US,
            3e6,
            hbm_in=False,
            hbm_out=False,
        )

    def send_rest(info, w_out, w_up, w_down, bias):
        return call(
            pack_rest,
            [
                ((rest_rows, width), bf16, VMEM),
                ((hid // 4, width), bf16, VMEM),
                ((cols, width), bf16, VMEM),
                ((width, hid), bf16, VMEM),
                ((hid, width), bf16, VMEM),
            ],
            [SMEM, VMEM, VMEM, VMEM, VMEM],
            (info, w_out, w_up, w_down, bias[None]),
            [pltpu.VMEM((16, width), f32)],
            24,
            4 * US,
            8e6,
            hbm_in=False,
            hbm_out=False,
        )

    (qkv_piece,) = send_qkv(info, n_qkv, n_bias)
    if head_count == 2:
        qkv_y = hop(qkv_piece, far)
        rest_piece, down_piece, *near_low = send_rest(info, n_out, n_up, n_down, n_ff)
    else:
        near_low = send_rest(info, n_out, n_up, n_down, n_ff)[2:]
        others = [info.at[7].set(quarter ^ i) for i in range(4)]
        qkv_all = [send_qkv(m, away[0], away[1])[0] for m in others]
        rest_all, down_all = zip(*(send_rest(m, away[2], away[3], away[5], away[4])[:2] for m in others))

    block = 2 * length
    steps = (rows // block,)
    wide = 4 if windows % 4 == 0 else 2
    wide_block, wide_steps = wide * length, (windows // wide,)
    seen = [
        ((rows, cols), bf16, cut(wide_block, cols)),
        ((rows, cols), bf16, cut(wide_block, cols)),
        ((rows, cols), bf16, cut(wide_block, cols)),
        ((rows, cols), bf16, cut(wide_block, cols)),
        ((windows, slots, length), f32, cut(wide, slots, length)),
        ((windows, slots, cols), bf16, cut(wide, slots, cols)),
    ]
    q0, k0, v0, ctx0, att0, picked0, emb, emb_t, wq0 = call(
        lambda *refs: attend_own(length, scale, *refs),
        seen
        + [
            ((rows, width), bf16, cut(wide_block, width)),
            ((width, rows), bf16, pl.BlockSpec((width, wide_block), lambda i: (0, i))),
            ((3, width, cols), bf16, whole(3, width, cols)),
        ],
        [SMEM, SMEM, cut(wide_block, width), whole(NDATA, width), whole(3, width, cols),
         whole(2, cols), whole(*picks.shape)],
        (info, window_group, tokens_in, data_table, n_qkv, n_bias, picks),
        [],
        24,
        9 * US,
        6e6,
        grid=wide_steps,
        hbm_in=False,
    )
    if head_count == 2:

        def spread(x):
            across = hop(x, second_bit)
            return [x, hop(x, core_bit), across, hop(across, core_bit)]

        qkv_y, ctx0, rest_piece = lax.optimization_barrier((qkv_y, ctx0, rest_piece))
        rest_y = hop(rest_piece, far)
        qkv_all = spread(qkv_y)
        rest_y, emb, down_piece = lax.optimization_barrier((rest_y, emb, down_piece))
        down_y = hop(down_piece, far)
        rest_all = spread(rest_y)
    q1, k1, v1, ctx1, att1, picked1, wq1, picks1 = call(
        lambda *refs: attend_far(length, scale, *refs),
        seen + [((3, width, cols), bf16, whole(3, width, cols)), ((windows, slots), f32, whole(windows, slots))],
        [SMEM, cut(wide_block, width)] + [HBM] * 4,
        (info, emb, *qkv_all),
        [
            pltpu.VMEM((extra_rows, cols), bf16),
            pltpu.VMEM((2, cols), f32),
            pltpu.SemaphoreType.DMA((13,)),
        ],
        24,
        9 * US,
        6e6,
        grid=wide_steps,
        hbm_in=False,
    )
    if head_count == 2:
        down_y, ctx1 = lax.optimization_barrier((down_y, ctx1))
        down_all = spread(down_y)

    def kinds(x):
        return [jax.ShapeDtypeStruct(x.shape, k) for k in (f32, f32, f32, bf16)]

    few = kinds(first_qkv) + [
        jax.ShapeDtypeStruct(first_out.shape, f32),
        jax.ShapeDtypeStruct((2,) + first_out.shape, f32),
        jax.ShapeDtypeStruct(first_out.shape, bf16),
    ]
    many = kinds(first_up) + kinds(first_down)

    def make_few(gate):
        return blanks_for(gate, few)

    def make_many(gate):
        return blanks_for(gate, many)

    def make_input_grad(gp1):
        return call(
            input_grad,
            [((rows, width), f32, cut(block, width))],
            [cut(block, cols)] * 6 + [whole(3, width, cols)] * 2 + [cut(block, width)],
            (gq0, gk0, gv0, gq1, gk1, gv1, wq0, wq1, gp1),
            [],
            24,
            US // 2,
            1e6,
            grid=steps,
        )[0]

    parts = 2 if windows % 4 == 0 else 1
    output_rows, gp1, ga, keep_one, send_one, sums, wo = call(
        lambda *refs: feed_forward(length, parts, *refs),
        [
            ((rows, width), f32, HBM),
            ((rows, width), f32, HBM),
            ((rows, width), bf16, HBM),
            ((2, buf_rows // 2, width), bf16, HBM),
            ((2, buf_rows // 2, width), bf16, HBM),
            ((16, width), f32, VMEM),
            ((2, cols, width), bf16, HBM),
        ],
        [SMEM, SMEM, VMEM, VMEM, VMEM, VMEM] + [HBM] * 11 + [VMEM, VMEM, VMEM, HBM],
        (info, window_group, tokens_in, data_table, ctx0, ctx1, *near_low, *rest_all, *down_all,
         n_ff[None], norm_gains, shifts, cotangent),
        [
            pltpu.VMEM((2, cols, width), bf16),
            pltpu.VMEM((2, width, hid), bf16),
            pltpu.VMEM((2, hid, width), bf16),
            pltpu.VMEM((rows, 2 * hid), bf16),
            pltpu.VMEM((rows, 2 * hid), bf16),
            pltpu.VMEM((rows, 2 * hid), bf16),
            pltpu.VMEM((rows, width), bf16),
            pltpu.VMEM((rows, width), bf16),
            pltpu.VMEM((rows, width), bf16),
            pltpu.VMEM((rows, width), f32),
            pltpu.VMEM((rows, width), f32),
            pltpu.VMEM((rows, width), f32),
            pltpu.VMEM((rows, width), f32),
            pltpu.VMEM((width, rows), bf16),
            pltpu.VMEM((width, rows), bf16),
            pltpu.VMEM((2, hid), f32),
            pltpu.VMEM((16, width), bf16),
            pltpu.VMEM((2, buf_rows, width), bf16),
            pltpu.SemaphoreType.DMA((21,)),
            pltpu.SemaphoreType.DMA((3,)),
            pltpu.SemaphoreType.DMA((5,)),
        ],
        56,
        24 * US,
        20e6,
    )
    if quick:
        state_one = sum_start(info, keep_one, send_one, bits, far, core_bit)
        ga, held = lax.optimization_barrier((ga, state_one[0]))
        state_one = (held, *state_one[1:])
    else:
        sum_one = plus(keep_one, hop(send_one, core_bit))
        sum_one, ga = lax.optimization_barrier((sum_one, ga))

    def make_back(g, ga, picks, wq, k, v, att, picked, extra_in):
        last = g == 0
        n = 3 * half // 2 + 32 * last
        more = [((16, cols), f32, whole(16, cols)), ((8, width), f32, whole(8, width))]
        return call(
            lambda *refs: attend_back(length, scale, g, *refs),
            [((rows, cols), bf16, cut(wide_block, cols))] * 3
            + [((n, width), bf16, HBM)] * 2
            + ([] if last else more),
            [SMEM, SMEM, cut(wide_block, width), FAR, whole(2, cols, width), whole(*picks.shape), FAR,
             cut(wide_block, cols), cut(wide_block, cols), cut(wide, slots, length), cut(wide, slots, cols)]
            + [whole(*x.shape) for x in extra_in],
            (info, window_group, ga, emb_t, wo, picks, wq, k, v, att, picked, *extra_in),
            [pltpu.VMEM((rows, cols), bf16)] * 3
            + [
                pltpu.VMEM((width, rows), bf16),
                pltpu.VMEM((3, width, cols), bf16),
                pltpu.VMEM((3 * half + 32 * last, width), bf16),
            ]
            + ([pltpu.VMEM((16, cols), f32), pltpu.VMEM((32, width), f32)] if last else [])
            + [pltpu.SemaphoreType.DMA((10,))],
            32,
            6 * US,
            8e6,
            grid=wide_steps,
        )

    gq1, gk1, gv1, keep_far, send_far, tsum, table_far = make_back(
        1, ga, picks1, wq1, k1, v1, att1, picked1, ()
    )
    if quick:
        held, keep_far, send_far = lax.optimization_barrier((state_one[0], keep_far, send_far))
        state_one = sum_middle(info, (held, *state_one[1:]), bits, far, width)
        held, ga, send_far = lax.optimization_barrier((state_one[0], ga, send_far))
        state_one = (held, *state_one[1:])
        got_far = hop(send_far, core_bit)
    gq0, gk0, gv0, keep_near, send_near = make_back(
        0, ga, picks, wq0, k0, v0, att0, picked0, (sums, tsum, table_far)
    )

    shards = head_count // 2
    mine = head % shards

    def shard(x, dim):
        n = x.shape[dim] // shards
        return x if shards == 1 else lax.dynamic_slice_in_dim(x, mine * n, n, dim)

    owned = (owner_list == my_rank).astype(jnp.int32)

    rate_wide = width ** (-0.5)
    rate_out = max(width // head_dim, 1) ** (-0.5)
    rate_down = (n_down.shape[0] * 2) ** (-0.5)
    moments_in = (
        weight_qkv, first_qkv, second_qkv, basis_qkv_left, basis_qkv_right,
        weight_out, first_out, second_out, basis_out_left, basis_out_right,
        weight_up, first_up, second_up, basis_up_left, basis_up_right,
        weight_down, first_down, second_down, basis_down_left, basis_down_right,
    )
    if quick:
        held, keep_near, send_near = lax.optimization_barrier((state_one[0], keep_near, send_near))
        beside = (
            make_many,
            lambda gate: make_input_grad(lax.optimization_barrier((gp1, gate))[0]),
            make_few,
        )
        pieces_one, pieces_two, small, (many, grad_rows, few) = sum_finish(
            info, (held, *state_one[1:]), (keep_near, send_near, keep_far, got_far), bits, far, core_bit, beside
        )
        likes = [first_qkv, first_out, first_up, first_down]
        blanks = [*few, *many]
        temps = [first_qkv.shape[1:], first_out.shape, first_up.shape, first_down.shape]
        outs = call(
            lambda *refs: update_all(rate_out, rate_wide, rate_down, cols, hid, *refs),
            [(x.shape, f32, HBM) for x in likes] + [(x.shape, x.dtype, HBM) for x in blanks],
            [SMEM, SMEM] + [HBM] * 4 + [FAR] * 35,
            (owned, info, *pieces_one, *pieces_two, *moments_in, *blanks),
            [pltpu.VMEM(x.shape, f32) for x in moments_in]
            + [pltpu.VMEM((buf_rows, width), bf16), pltpu.VMEM((3 * half, width), bf16)]
            + [pltpu.VMEM(x.shape, f32) for x in likes]
            + [pltpu.VMEM(x.shape, bf16) for x in likes]
            + [
                pltpu.VMEM((width, width), bf16),
                pltpu.VMEM(basis_qkv_right.shape[1:], bf16),
                pltpu.VMEM(basis_up_right.shape, bf16),
            ]
            + [pltpu.VMEM(x, bf16) for x in temps * 2]
            + [
                pltpu.SemaphoreType.DMA((10,)),
                pltpu.SemaphoreType.DMA((6, 5)),
                pltpu.SemaphoreType.DMA((6, 4)),
            ],
            49,
            12 * US,
            30e6,
            {26 + i: 4 + i for i in range(15)},
        )
        grad_qkv_all, grad_out_all, grad_up_all, grad_down_all = outs[:4]
        qkv_outs, rest_outs = outs[3:8], outs[5:19]
        grad_table_all, grad_gains_all, grad_shifts_all, grad_ff_all, grad_bias_all = small
        grad_ff_all = grad_ff_all.reshape(-1)
    else:
        grad_rows = make_input_grad(gp1)
        n = 3 * half // 2
        keep_two, send_two = (
            jnp.stack([near[: n + 16], jnp.concatenate([away_part, near[n + 16 :]])])
            for near, away_part in ((keep_near, keep_far), (send_near, send_far))
        )
        blanks = make_few(sums) + make_many(sums)
        early, late = early_steps(bits, far, core_bit), late_steps(16, bits, far, core_bit)
        state_one, state_two = early[0](sum_one), (keep_two, send_two)
        for i in range(1, max(len(early), len(late) + 1)):
            state_one, state_two = lax.optimization_barrier((state_one, state_two))
            if i < len(early):
                state_one = early[i](state_one)
            if i <= len(late):
                state_two = late[i - 1](state_two)
        sum_one, (sum_two, small) = state_one, state_two
        small = small[0]
        g_up = shard(jnp.concatenate([sum_one[:width], sum_one[width : 2 * width]], 1), 1)
        g_down_t = shard(
            jnp.concatenate([sum_one[2 * width : 3 * width], sum_one[3 * width : 4 * width]], 1), 1
        )
        g_out = shard(sum_one[4 * width :], 0)

        def rest_body(*refs):
            update_rest(rate_out, rate_wide, rate_down, *refs)

        tall, wide, low = first_out.shape, first_up.shape, first_down.shape
        rest_outs = call(
            rest_body,
            [(tall, f32, VMEM), (wide, f32, VMEM), (low, f32, VMEM)]
            + [(x.shape, x.dtype, HBM) for x in blanks[4:]],
            [SMEM, VMEM, VMEM, VMEM] + [HBM] * (15 + 11),
            (owned, g_out, g_up, g_down_t,
             weight_out, first_out, second_out, basis_out_left, basis_out_right,
             weight_up, first_up, second_up, basis_up_left, basis_up_right,
             weight_down, first_down, second_down, basis_down_left, basis_down_right, *blanks[4:]),
            [pltpu.VMEM(tall, f32)] * 3
            + [
                pltpu.VMEM(tall, bf16),
                pltpu.VMEM(basis_out_left.shape, f32),
                pltpu.VMEM(basis_out_right.shape, f32),
                pltpu.VMEM(basis_out_right.shape, bf16),
                pltpu.VMEM(tall, bf16),
                pltpu.VMEM(tall, bf16),
            ]
            + [pltpu.VMEM(wide, f32)] * 3
            + [
                pltpu.VMEM(wide, bf16),
                pltpu.VMEM(basis_up_left.shape, f32),
                pltpu.VMEM(basis_up_right.shape, f32),
                pltpu.VMEM(basis_up_left.shape, bf16),
                pltpu.VMEM(basis_up_right.shape, bf16),
                pltpu.VMEM(wide, bf16),
                pltpu.VMEM(wide, bf16),
            ]
            + [pltpu.VMEM(low, f32)] * 3
            + [pltpu.VMEM(low, bf16)] * 3
            + [pltpu.SemaphoreType.DMA((5,))],
            48,
            12 * US,
            20e6,
            {4 + 15 + i: 3 + i for i in range(11)},
        )
        grad_out_all, grad_up_all, grad_down_all = rest_outs[:3]

        pairs = sum_two.reshape(3, half, width)
        g_qkv = shard(jnp.concatenate([pairs[:, :, :cols], pairs[:, :, cols:]], 1), 2)
        small = small.astype(f32)

        def qkv_body(*refs):
            update_qkv(rate_wide, *refs)

        one = first_qkv.shape[1:]
        qkv_outs = call(
            qkv_body,
            [(first_qkv.shape, f32, VMEM)] + [(x.shape, x.dtype, HBM) for x in blanks[:4]],
            [SMEM, VMEM] + [HBM] * 9,
            (owned, g_qkv, weight_qkv, first_qkv, second_qkv, basis_qkv_left, basis_qkv_right, *blanks[:4]),
            [pltpu.VMEM(one, f32)] * 3
            + [
                pltpu.VMEM(one, bf16),
                pltpu.VMEM(basis_qkv_left.shape[1:], f32),
                pltpu.VMEM(basis_qkv_right.shape[1:], f32),
                pltpu.VMEM(basis_qkv_left.shape[1:], bf16),
                pltpu.VMEM(basis_qkv_right.shape[1:], bf16),
                pltpu.VMEM(one, bf16),
                pltpu.VMEM(one, bf16),
                pltpu.SemaphoreType.DMA((5,)),
            ],
            24,
            6 * US,
            8e6,
            {7 + i: 1 + i for i in range(4)},
        )
        grad_qkv_all = qkv_outs[0]
        grad_table_all = small[0:2]
        grad_gains_all = small[2:4]
        grad_shifts_all = small[4:8]
        grad_ff_all = shard(small[8:10].reshape(-1), 0)
        grad_bias_all = shard(small[10].reshape(2, cols), 1)
    return (
        output_rows,
        grad_rows,
        grad_table_all,
        grad_gains_all,
        grad_shifts_all,
        grad_bias_all,
        grad_ff_all,
        grad_qkv_all,
        grad_out_all,
        grad_up_all,
        grad_down_all,
        *(x[None] for x in qkv_outs[1:]),
        *(x[None] for x in rest_outs[3:]),
    )


def solution(mesh):
    in_specs = (
        P(("dp", "head"), None),
        P(("dp", "head"), None),
        P(),
        P("dp"),
        P("dp", "head", None),
        P(),
        P(None, None, "head"),
        P(None, "head"),
        P("head", None),
        P(None, "head"),
        P("head"),
        P("head", None),
        P(),
        P(),
        P(None, None, "head"),
        P(None, None, "head"),
        P("head", None),
        P("head", None),
        P(None, "head"),
        P(None, "head"),
        P("head", None),
        P("head", None),
        P(),
        P(None, "head", None, None),
        P("head", None, None),
        P(),
        P(),
        P("head", None, None),
        P("head", None, None),
        P(),
    )
    out_specs = (
        P(("dp", "head"), None),
        P(("dp", "head"), None),
        P(),
        P(),
        P(),
        P(None, "head"),
        P("head"),
        P(None, None, "head"),
        P("head", None),
        P(None, "head"),
        P("head", None),
        P("dp", None, None, "head"),
        P("dp", None, None, "head"),
        P("dp", None, None, "head"),
        P("dp", None, None, "head"),
        P("dp", "head", None),
        P("dp", None, "head", None),
        P("dp", "head", None),
        P("dp", None, "head"),
        P("dp", None, "head"),
        P("dp", None, "head"),
        P("dp", None, "head"),
        P("dp", "head", None),
        P("dp", "head", None),
        P("dp", "head", None),
        P("dp", "head", None),
    )
    return jax.shard_map(
        per_device, mesh=mesh, in_specs=in_specs, out_specs=out_specs, check_vma=False
    )
```

```python
import math

import jax
import jax.numpy as jnp
from jax import lax
from jax.experimental import pallas as pl
from jax.experimental.pallas import tpu as pltpu
from jax.sharding import PartitionSpec as P

f32 = jnp.float32
bf16 = jnp.bfloat16

NDATA = 2
EPS_NORM = 1e-05
EPS_ADAM = 1e-08
BETA_ONE = 0.5
BETA_TWO = 0.5

GROUP = 4
SLOTS = 32
MB = 1 << 20


def nn(a, b):
    return jnp.dot(a, b, preferred_element_type=f32)


def nt(a, b):
    return lax.dot_general(a, b, (((1,), (1,)), ((), ())), preferred_element_type=f32)


def col_sum(x):
    return jnp.sum(x, axis=0, keepdims=True)


def row_mean(x):
    return jnp.mean(x, axis=-1, keepdims=True)


VMEM = pl.BlockSpec(memory_space=pltpu.VMEM)
SMEM = pl.BlockSpec(memory_space=pltpu.SMEM)
HBM = pl.BlockSpec(memory_space=pl.ANY)
FAR = pl.BlockSpec(memory_space=pl.ANY)


def whole(*shape):
    return pl.BlockSpec(shape, lambda i: (0,) * len(shape))


def cut(*shape):
    return pl.BlockSpec(shape, lambda i: (i,) + (0,) * (len(shape) - 1))


US = 1_000_000_000


def in_hbm(x, spec):
    small = x.size * x.dtype.itemsize < 1 << 16
    if spec is SMEM or spec is HBM or (small and spec is not FAR):
        return x
    return pltpu.with_memory_space_constraint(x, pltpu.HBM)


def call(body, outs, ins, args, scratch, limit, flops, nbytes, aliases={}, grid=(), hbm_in=True, hbm_out=True):
    if hbm_in:
        args = [in_hbm(x, spec) for x, spec in zip(args, ins)]
    kind = pltpu.HBM if hbm_out else jax.ShapeDtypeStruct
    return pl.pallas_call(
        body,
        grid=grid,
        out_shape=tuple(kind(s, d) for s, d, _ in outs),
        in_specs=ins,
        out_specs=tuple(spec for _, _, spec in outs),
        scratch_shapes=scratch,
        input_output_aliases=aliases,
        compiler_params=pltpu.CompilerParams(vmem_limit_bytes=limit * MB),
        cost_estimate=pl.CostEstimate(
            flops=int(flops), bytes_accessed=int(nbytes), transcendentals=0
        ),
    )(*args)


def head_mask(cols):
    width = cols // GROUP
    shape = (GROUP * SLOTS, cols)
    return (
        lax.broadcasted_iota(jnp.int32, shape, 0) // SLOTS
        == lax.broadcasted_iota(jnp.int32, shape, 1) // width
    )


def one_hot(picks, w, length):
    row = picks[pl.ds(w, 1), :]
    spots = lax.broadcasted_iota(jnp.int32, (length, GROUP * SLOTS), 0).astype(f32)
    columns = (spots == row).astype(f32)
    return columns.astype(bf16), columns.T.astype(bf16)


def copy_all(pairs, sems):
    copies = [pltpu.make_async_copy(a, b, sems.at[i]) for i, (a, b) in enumerate(pairs)]
    for copy in copies:
        copy.start()
    return copies


def split_sum(parts, at):
    return parts[at : at + 1] + parts[at + 1 : at + 2] + parts[at + 2 : at + 3]


def put_parts(extra, at, row):
    for i in range(3):
        part = row.astype(bf16).astype(f32)
        extra[at + i : at + i + 1, :] = part
        row = row - part


def pack_qkv(windows, info, w, bias_in, picks_in, piece, part, extra, bias, picks, sems):
    n = part.shape[1]
    rows = pl.ds(pl.multiple_of(info[7] * n, n), n)
    pairs = [(w.at[j, rows, :], part.at[j]) for j in range(3)] + [(bias_in, bias), (picks_in, picks)]
    copies = copy_all(pairs, sems)
    extra[...] = jnp.zeros_like(extra)
    for copy in copies[3:]:
        copy.wait()
    for i in range(windows):
        extra[i : i + 1, : GROUP * SLOTS] = picks[pl.ds(info[2] + i, 1), :]
    put_parts(extra, windows, bias[0:1, :])
    put_parts(extra, windows + 3, bias[1:2, :])
    piece[3 * n :, :] = extra[...].astype(bf16)
    for j, copy in enumerate(copies[:3]):
        copy.wait()
        piece[j * n : (j + 1) * n, :] = part[j].astype(bf16)


def pack_rest(info, w_out, w_up, w_down, bias, piece, down_piece, out_low, up_low, down_low, extra):
    hid = w_up.shape[1] // 2
    n_out, n_up, n_down = w_out.shape[0] // 4, w_up.shape[0] // 4, w_down.shape[0] // 4
    out_low[...] = w_out[...].astype(bf16)
    up_low[...] = w_up[...].astype(bf16)
    down_low[...] = w_down[...].astype(bf16)
    extra[...] = jnp.zeros_like(extra)
    put_parts(extra, 0, bias[:, :hid])
    put_parts(extra, 3, bias[:, hid:])
    piece[:n_out, :] = out_low[pl.ds(pl.multiple_of(info[7] * n_out, n_out), n_out), :]
    rows = pl.ds(pl.multiple_of(info[7] * n_up, n_up), n_up)
    for h in range(2):
        piece[n_out + h * n_up : n_out + (h + 1) * n_up, :] = up_low[rows, h * hid : (h + 1) * hid]
    piece[n_out + 2 * n_up :, :] = extra[...].astype(bf16)
    down_piece[...] = down_low[pl.ds(pl.multiple_of(info[7] * n_down, n_down), n_down), :]


def attend(wq, bias, picks, start, emb, q_out, k_out, v_out, ctx, att, picked, length, scale):
    cols = wq.shape[2]
    e = emb[...]
    for j, out in enumerate((q_out, k_out, v_out)):
        out[...] = (nn(e, wq[j]) + bias[j]).astype(bf16)
    mask = head_mask(cols)
    mask_low = mask.astype(f32).astype(bf16)
    spots = [slice(i * length, (i + 1) * length) for i in range(emb.shape[0] // length)]
    hots = [one_hot(picks, start + i, length) for i in range(len(spots))]
    sel = [nn(down, q_out[here, :]) for (_, down), here in zip(hots, spots)]
    sel = [jnp.where(mask, x, 0.0).astype(bf16) for x in sel]
    for i, x in enumerate(sel):
        picked[i] = x
    scores = [nt(x, k_out[here, :]) * scale for x, here in zip(sel, spots)]
    active = [nn(up, mask_low) for up, _ in hots]
    exponent = [jnp.exp(x - jnp.max(x, axis=-1, keepdims=True)) for x in scores]
    probs = [x * (1.0 / jnp.sum(x, axis=-1, keepdims=True)) for x in exponent]
    for i, x in enumerate(probs):
        att[i] = x
    mixed = [nn(x.astype(bf16), v_out[here, :]) for x, here in zip(probs, spots)]
    mixed = [jnp.where(mask, x, 0.0).astype(bf16) for x in mixed]
    mean = [col_sum(v_out[here, :].astype(f32)) * (1.0 / length) for here in spots]
    mixed = [nn(up, x) for (up, _), x in zip(hots, mixed)]
    for here, x, act, m in zip(spots, mixed, active, mean):
        ctx[here, :] = (x + (1.0 - act) * m).astype(bf16)


def attend_own(length, scale, info, groups, tokens, table, w, bias, picks,
               q, k, v, ctx, att, picked, emb, emb_t, wq):
    @pl.when(pl.program_id(0) == 0)
    def _():
        for j in range(3):
            wq[j] = w[j].astype(bf16)

    per = tokens.shape[0] // length
    first = pl.program_id(0) * per
    for i in range(per):
        here = slice(i * length, (i + 1) * length)
        row = table[pl.ds(groups[info[3] + first + i], 1), :]
        emb[here, :] = (tokens[here, :].astype(f32) + row).astype(bf16)
    emb_t[...] = emb[...].astype(f32).T.astype(bf16)
    rows = (bias[0:1, :], jnp.zeros_like(bias[0:1, :]), bias[1:2, :])
    attend(wq, rows, picks, info[1] + first, emb, q, k, v, ctx, att, picked, length, scale)


def attend_far(length, scale, info, emb, p0, p1, p2, p3,
               q, k, v, ctx, att, picked, wq, picks, extra, bias, sems):
    n = wq.shape[1] // 4
    windows = picks.shape[0]

    @pl.when(pl.program_id(0) == 0)
    def _():
        pairs = [(p0.at[pl.ds(3 * n, extra.shape[0]), :], extra)]
        for i, piece in enumerate((p0, p1, p2, p3)):
            for j in range(3):
                pairs.append(
                    (
                        piece.at[pl.ds(j * n, n), :],
                        wq.at[j, pl.ds(pl.multiple_of((info[7] ^ i) * n, n), n), :],
                    )
                )
        for copy in copy_all(pairs, sems):
            copy.wait()
        rest = extra[...].astype(f32)
        picks[...] = rest[:windows, : GROUP * SLOTS]
        bias[0:1, :] = split_sum(rest, windows)
        bias[1:2, :] = split_sum(rest, windows + 3)

    rows = (bias[0:1, :], jnp.zeros_like(bias[0:1, :]), bias[1:2, :])
    first = pl.program_id(0) * (emb.shape[0] // length)
    attend(wq, rows, picks, first, emb, q, k, v, ctx, att, picked, length, scale)


def gelu_pair(x):
    bell = jnp.exp2((x * x) * (-0.5 * math.log2(math.e)))
    y = 1.0 + (0.3275911 * math.sqrt(0.5)) * jnp.abs(x)
    t = pl.reciprocal(y, approx=True)
    t = t * (2.0 - y * t)
    poly = t * (
        0.5 * 0.254829592
        + t * (0.5 * -0.284496736 + t * (0.5 * 1.421413741 + t * (0.5 * -1.453152027 + t * (0.5 * 1.061405429))))
    )
    tail = poly * bell
    phi = jnp.where(x >= 0.0, 1.0 - tail, tail)
    return x * phi, phi + (x * (1.0 / math.sqrt(2.0 * math.pi))) * bell


def feed_forward(length, parts, info, groups, tokens, table, ctx0, ctx1, near_out, near_up, near_down,
                 p0, p1, p2, p3, d0, d1, d2, d3, ff_bias, gains, shifts, cot_in,
                 out_far, gp1_far, ga_far, keep, send, sums, wo_far,
                 wo, up, dn, act, gpre, slope, nl, gb, ga, out, gp1, pre, cot, nl_t, gb_t, ffb, extra, buf,
                 sems, row_sems, end_sems):
    core, quarter = info[0], info[7]
    rows, width = tokens.shape
    block = rows // parts
    cols = wo.shape[1]
    hid = up.shape[2]
    half = hid // 2

    def rows_of(x, i, n, *rest):
        return x.at[(1, pl.ds(pl.multiple_of((quarter ^ i) * n, n), n)) + rest]

    n_out, n_up, n_down = cols // 4, width // 4, hid // 4
    pairs = [[(near_out, wo.at[0])], [(near_up, up.at[0])], [(near_down, dn.at[0])], [(cot_in, cot)]]
    pairs[1].append((p0.at[pl.ds(n_out + 2 * n_up, 16), :], extra))
    for i, (p, d) in enumerate(((p0, d0), (p1, d1), (p2, d2), (p3, d3))):
        pairs[0].append((p.at[pl.ds(0, n_out), :], rows_of(wo, i, n_out)))
        for h in range(2):
            pairs[1].append(
                (p.at[pl.ds(n_out + h * n_up, n_up), :], rows_of(up, i, n_up, pl.ds(h * half, half)))
            )
        pairs[2].append((d, rows_of(dn, i, n_down)))
    loads, at = [], 0
    for some in pairs:
        loads.append([pltpu.make_async_copy(a, b, sems.at[at + i]) for i, (a, b) in enumerate(some)])
        at += len(some)
    for some in loads:
        for copy in some:
            copy.start()
    wo_copy = pltpu.make_async_copy(wo, wo_far, end_sems.at[4])
    ffb[0:1, :] = ff_bias[...]
    for i in range(rows // length):
        here = slice(i * length, (i + 1) * length)
        pre[here, :] = tokens[here, :].astype(f32) + table[pl.ds(groups[info[3] + i], 1), :]
    for copy in loads[0]:
        copy.wait()
    wo_copy.start()

    spans = [slice(i * block, (i + 1) * block) for i in range(parts)]
    inv_one = []
    xs = [nn(ctx0[here, :], wo[0]) + nn(ctx1[here, :], wo[1]) for here in spans]
    for here, x in zip(spans, xs):
        x = pre[here, :] + (x + shifts[0:1, :])
        center = x - row_mean(x)
        inv_one.append(lax.rsqrt(row_mean(center * center) + EPS_NORM))
        unit = center * inv_one[-1]
        pre[here, :] = unit
        nl[here, :] = (unit * gains[0:1, :] + shifts[2:3, :]).astype(bf16)
    for some in loads[1:]:
        for copy in some:
            copy.wait()
    rest = extra[...].astype(f32)
    ffb[1:2, :half] = split_sum(rest, 0)
    ffb[1:2, half:] = split_sum(rest, 3)

    order = [(i, ch) for ch in range(4) for i in range(parts)]

    def lift(i, ch):
        g, o = ch // 2, (ch % 2) * half
        return nn(nl[spans[i], :], up[g, :, o : o + half])

    later = lift(*order[0])
    branch = [shifts[1:2, :]] * parts
    for k, (i, ch) in enumerate(order):
        g, o = ch // 2, (ch % 2) * half
        z = later + ffb[g : g + 1, o : o + half]
        if k + 1 < len(order):
            later = lift(*order[k + 1])
        a, d = gelu_pair(z)
        a = a.astype(bf16)
        act[spans[i], ch * half : (ch + 1) * half] = a
        slope[spans[i], ch * half : (ch + 1) * half] = d.astype(bf16)
        branch[i] = branch[i] + nn(a, dn[g, o : o + half, :])
    total = []
    tops = [0.0] * 3
    for here, x in zip(spans, branch):
        y = pre[here, :] * gains[0:1, :] + shifts[2:3, :] + x
        center = y - row_mean(y)
        inv_two = lax.rsqrt(row_mean(center * center) + EPS_NORM)
        unit_two = center * inv_two
        out[here, :] = unit_two * gains[1:2, :] + shifts[3:4, :]
        c = cot[here, :]
        g2 = c * gains[1:2, :]
        gp2 = (g2 - row_mean(g2) - unit_two * row_mean(g2 * unit_two)) * inv_two
        low = gp2.astype(bf16)
        gb[here, :] = low
        tops = [t + col_sum(x) for t, x in zip(tops, (c * unit_two, c, low.astype(f32)))]
        total.append(gp2)
    sums[...] = jnp.zeros_like(sums)
    sums[1:2, :] = tops[0]
    sums[5:6, :] = tops[1]
    sums[3:4, :] = tops[2]

    def lower(i, ch):
        g, o = ch // 2, (ch % 2) * half
        return nt(gb[spans[i], :], dn[g, o : o + half, :])

    later = lower(*order[0])
    for k, (i, ch) in enumerate(order):
        g, o = ch // 2, (ch % 2) * half
        p = later * slope[spans[i], ch * half : (ch + 1) * half].astype(f32)
        if k + 1 < len(order):
            later = lower(*order[k + 1])
        p = p.astype(bf16)
        gpre[spans[i], ch * half : (ch + 1) * half] = p
        sums[6 + ch : 7 + ch, :] += col_sum(p.astype(f32))
        total[i] = total[i] + nt(p, up[g, :, o : o + half])
    tops = [0.0] * 3
    for here, x, inv in zip(spans, total, inv_one):
        unit_one = pre[here, :]
        g1 = x * gains[0:1, :]
        gp = (g1 - row_mean(g1) - unit_one * row_mean(g1 * unit_one)) * inv
        gp1[here, :] = gp
        low_one = gp.astype(bf16)
        ga[here, :] = low_one
        tops = [t + col_sum(v) for t, v in zip(tops, (x * unit_one, x, low_one.astype(f32)))]
    sums[0:1, :] = tops[0]
    sums[4:5, :] = tops[1]
    sums[2:3, :] = tops[2]
    ends = [
        pltpu.make_async_copy(a, b, row_sems.at[j])
        for j, (a, b) in enumerate(((ga, ga_far), (gp1, gp1_far), (out, out_far)))
    ] + [wo_copy]
    for copy in ends[:3]:
        copy.start()
    for i in range(rows // length):
        spot = pl.ds(10 + groups[info[3] + i], 1)
        sums[spot, :] += col_sum(gp1[i * length : (i + 1) * length, :])
    nl_t[...] = nl[...].astype(f32).T.astype(bf16)
    gb_t[...] = gb[...].astype(f32).T.astype(bf16)
    n = buf.shape[1] // 2
    for g, ctx in ((1, ctx1), (0, ctx0)):
        buf[g, 2 * hid : 2 * hid + cols, :] = nn(ctx[...].astype(f32).T.astype(bf16), ga[...]).astype(bf16)
        for ch in (2 * g, 2 * g + 1):
            o = (ch % 2) * half
            at = slice(ch * half, (ch + 1) * half)
            buf[g, o : o + half, :] = nn(nl_t[...], gpre[:, at]).astype(bf16)
            buf[g, hid + o : hid + o + half, :] = nn(gb_t[...], act[:, at]).astype(bf16)
        for dst, spot in ((send, 1 - core), (keep, core)):
            copy = pltpu.make_async_copy(
                buf.at[g, pl.ds(pl.multiple_of(spot * n, 32), n), :], dst.at[g], end_sems.at[2 * g + (dst is keep)]
            )
            copy.start()
            ends.append(copy)
    for copy in ends:
        copy.wait()


def attend_back(length, scale, g, info, groups, ga, emb_in, wo, picks, wq_in, k_in, v_in, att, picked, *refs):
    last = g == 0
    if last:
        sums, tsum_far, total_far, *refs = refs
    gq, gk, gv, keep, send, *refs = refs
    if not last:
        tsum, total_out, *refs = refs
    gq_all, gk_all, gv_all, emb_t, wq, buf, *refs = refs
    if last:
        tsum, small, *refs = refs
    (sems,) = refs
    core = info[0]
    step = pl.program_id(0)
    width, rows = emb_t.shape
    block = ga.shape[0]
    per = block // length
    cols = wq.shape[2]
    half = width // 2
    mask = head_mask(cols)
    mask_low = mask.astype(f32).astype(bf16)
    late = [
        pltpu.make_async_copy(a, b, sems.at[8 + i]) for i, (a, b) in enumerate(((emb_in, emb_t), (wq_in, wq)))
    ]

    @pl.when(step == 0)
    def _():
        for copy in late:
            copy.start()
        tsum[...] = jnp.zeros_like(tsum)

    start = (info[1] if last else 0) + step * per
    spots = [slice(i * length, (i + 1) * length) for i in range(per)]
    g_ctx = nt(ga[...], wo[g]).astype(bf16)
    hots = [one_hot(picks, start + i, length) for i in range(per)]
    ge = [nn(down, g_ctx[here, :]) for here, (_, down) in zip(spots, hots)]
    ge = [jnp.where(mask, x, 0.0).astype(bf16) for x in ge]
    active = [nn(up, mask_low) for up, _ in hots]
    gprobs = [nt(x, v_in[here, :]) for here, x in zip(spots, ge)]
    low_t = [att[i].T.astype(bf16) for i in range(per)]
    gmean = [
        col_sum((1.0 - x) * g_ctx[here, :].astype(f32)) * (1.0 / length) for here, x in zip(spots, active)
    ]
    g_value = [nn(x, y) for x, y in zip(low_t, ge)]
    weighted = [att[i] * x for i, x in enumerate(gprobs)]
    graw = [(x - att[i] * jnp.sum(x, axis=-1, keepdims=True)) * scale for i, x in enumerate(weighted)]
    gpick = [nn(x.astype(bf16), k_in[here, :]) for here, x in zip(spots, graw)]
    graw_t = [x.T.astype(bf16) for x in graw]
    g_value = [(x + m).astype(bf16) for x, m in zip(g_value, gmean)]
    gpick = [jnp.where(mask, x, 0.0).astype(bf16) for x in gpick]
    g_key = [nn(x, picked[i]).astype(bf16) for i, x in enumerate(graw_t)]
    g_query = [nn(up, x).astype(bf16) for (up, _), x in zip(hots, gpick)]
    for i, three in enumerate(zip(g_query, g_key, g_value)):
        rows_here = pl.ds(pl.multiple_of(step * block + i * length, 32), length)
        group = groups[info[3] + step * per + i]
        for j, (x, dst, dst_all) in enumerate(zip(three, (gq, gk, gv), (gq_all, gk_all, gv_all))):
            dst[spots[i], :] = x
            dst_all[rows_here, :] = x
            tsum[pl.ds(2 * j + group, 1), :] += col_sum(x.astype(f32))

    @pl.when(step == rows // block - 1)
    def _():
        for copy in late:
            copy.wait()
        n = 3 * half // 2
        pairs = []
        for j, x in enumerate((gq_all, gk_all, gv_all)):
            r = nn(emb_t[...], x[...]).astype(bf16)
            buf[j * half : (j + 1) * half, :cols] = r[:half]
            buf[j * half : (j + 1) * half, cols:] = r[half:]
        for dst, spot in ((send, 1 - core), (keep, core)):
            pairs.append((buf.at[at_row(spot * n, n), :], dst.at[pl.ds(0, n), :]))
        copies = copy_all(pairs, sems)
        total = jnp.zeros((8, width), f32)
        for j in range(3):
            x = tsum[2 * j : 2 * j + 8, :]
            hi = x.astype(bf16)
            lo = (x - hi.astype(f32)).astype(bf16)
            total = total + nt(hi, wq[j]) + nt(lo, wq[j])
        if last:
            total = total + total_far[...]
            small[...] = jnp.zeros_like(small)
            for m, t in enumerate((tsum, tsum_far)):
                at = 16 * m
                small[at : at + 2, :] = total[0:2] + sums[10:12, :]
                small[at + 2 : at + 8, :] = sums[0:6, :]
                small[at + 8 : at + 10, :] = sums[6 + 2 * m : 8 + 2 * m, :]
                small[at + 10 : at + 11, :cols] = t[0:1, :] + t[1:2, :]
                small[at + 10 : at + 11, cols:] = t[4:5, :] + t[5:6, :]
            buf[2 * n :, :] = small[...].astype(bf16)
            more = [
                pltpu.make_async_copy(buf.at[pl.ds(2 * n, 32), :], dst.at[pl.ds(n, 32), :], sems.at[2 + i])
                for i, dst in enumerate((send, keep))
            ]
            for copy in more:
                copy.start()
            copies += more
        else:
            total_out[...] = total
        for copy in copies:
            copy.wait()


def input_grad(*refs):
    (*grads, wq0, wq1, gp1, out) = refs
    total = gp1[...]
    for i, x in enumerate(grads):
        total = total + nt(x[...], (wq0, wq1)[i // 3][i % 3])
    out[...] = total


def hop(x, *bits):
    heads = lax.axis_size("head")
    flip = sum((1 << k) * (heads if axis == "dp" else 1) for axis, k in bits)
    count = lax.axis_size("dp") * heads
    return lax.ppermute(x, ("dp", "head"), [(i, i ^ flip) for i in range(count)])


def side(bit):
    axis, k = bit
    return (lax.axis_index(axis) >> k) & 1


def subsets(bits):
    return [[b for i, b in enumerate(bits) if (r >> i) & 1] for r in range(1 << len(bits))]


def pair_sum(terms):
    while len(terms) > 1:
        terms = [terms[i] + terms[i + 1] for i in range(0, len(terms), 2)]
    return terms[0]


def pick(x, bits, far, flips):
    for bit in bits:
        flipped = bit in flips
        if bit == far:
            x = x[1:] if flipped else x[:1]
        else:
            n = x.shape[1] // 2
            x = lax.dynamic_slice_in_dim(x, (side(bit) ^ int(flipped)) * n, n, 1)
    return x


def scatter_sum(x, bits, far, small=None):
    terms, rest = [], []
    for flips in subsets(bits):
        part = pick(x, bits, far, flips)
        if small is not None:
            part = jnp.concatenate([part, pick(small, [far] if far in bits else [], far, flips)], 1)
        if flips:
            part = hop(part, *flips)
        terms.append(part.astype(f32))
    total = pair_sum(terms).astype(bf16)
    if small is None:
        return total
    n = total.shape[1] - small.shape[1]
    return total[:, :n], total[:, n:]


def gather(x, bits):
    parts = {}
    for r, flips in enumerate(subsets(bits)):
        parts[r] = hop(x, *flips) if flips else x
    for i, bit in enumerate(bits):
        m = side(bit) == 0
        parts = {
            r: jnp.where(m, parts[r], parts[r ^ (1 << i)]) for r in parts
        }
    order = sorted(parts, key=lambda r: [(r >> i) & 1 for i in range(len(bits))])
    return jnp.concatenate([parts[r] for r in order], axis=0)


def plus(a, b):
    return (a.astype(f32) + b.astype(f32)).astype(bf16)


def late_steps(small_rows, bits, far, core):
    stages = [[far, bits[0]]] + [bits[i : i + 2] for i in range(1, len(bits), 2)]

    def cores(state):
        x = plus(state[0], hop(state[1], core))
        return x[:, :-small_rows], x[:, -small_rows:]

    def down(stage):
        return lambda state: scatter_sum(state[0], stage, far, state[1])

    def up(stage):
        wanted = [b for b in stage if b != far]

        def step(state):
            x = state[0] if state[0].ndim == 2 else state[0][0]
            return gather(x, wanted), state[1]

        return step

    return [cores] + [down(s) for s in stages] + [up(s) for s in reversed(stages)] + [up([core])]


def early_steps(bits, far, core):
    first, second, rest = bits[0], bits[1], bits[2:]
    orders = ((far, first, second), (first, second, far), (second, far, first))

    def start(x):
        part = x.shape[1] // 3
        return down(0)([x[:, i * part : (i + 1) * part] for i in range(3)])

    def down(stage):
        return lambda chunks: [scatter_sum(c, [order[stage]], far) for c, order in zip(chunks, orders)]

    def swap(chunks):
        x = jnp.concatenate(chunks, axis=2)[0]
        for bit in rest:
            x = plus(x, hop(x, bit))
        width = x.shape[1] // 3
        return [x[:, : 2 * width], x[:, 2 * width :]]

    def up_one(parts):
        return [gather(parts[0], [second]), gather(parts[1], [first])]

    def up_two(parts):
        two, one = gather(parts[0], [first]), gather(parts[1], [second])
        width = one.shape[1]
        return jnp.concatenate([two[:, :width], two[:, width:], one], axis=0)

    return [start, down(1), down(2), swap, up_one, up_two, lambda x: gather(x, [core])]


def add(a, b):
    return a.astype(f32) + b.astype(f32)


def at_row(start, n):
    return pl.ds(pl.multiple_of(start, 16), n)


def merge_cores(info, keep_in, got_in, stay0, far0, stay1, first1, stay2, second2, keep, got, sems, more_sems):
    n = keep.shape[1] // 3
    h = n // 2
    a, b = info[4], info[5]
    here = [pl.ds(i * n, n) for i in range(3)]
    loads = copy_all([(got_in.at[:, x, :], got.at[:, x, :]) for x in here], sems)
    more = copy_all([(keep_in.at[:, x, :], keep.at[:, x, :]) for x in here], more_sems)
    loads[0].wait()
    more[0].wait()
    stay0[...] = add(keep[0, :n], got[0, :n]).astype(bf16)
    far0[...] = add(keep[1, :n], got[1, :n]).astype(bf16)
    for base, bit, stay, send in ((n, a, stay1, first1), (2 * n, b, stay2, second2)):
        loads[base // n].wait()
        more[base // n].wait()
        for dst, m in ((stay, bit), (send, 1 - bit)):
            here = at_row(base + m * h, h)
            for g in range(2):
                dst[g] = add(keep[g, here], got[g, here]).astype(bf16)


def merge_two(info, stay0, got0, stay1, got1, stay2, got2, keep0, first0, keep1, second1, keep2, far2):
    a, b = info[4], info[5]
    h = stay0.shape[0] // 2
    for dst, m in ((keep0, a), (first0, 1 - a)):
        here = at_row(m * h, h)
        dst[...] = add(stay0[here], got0[here]).astype(bf16)
    q = stay1.shape[1] // 2
    for dst, m in ((keep1, b), (second1, 1 - b)):
        here = at_row(m * q, q)
        for g in range(2):
            dst[g] = add(stay1[g, here], got1[g, here]).astype(bf16)
    keep2[...] = add(stay2[0], got2[0]).astype(bf16)
    far2[...] = add(stay2[1], got2[1]).astype(bf16)


def merge_three(info, in0, got0, in1, got1, in2, got2, stay, to_second, to_far, to_first):
    a, b = info[4], info[5]
    q = to_far.shape[0]
    stay[:q] = add(in0[at_row(b * q, q)], got0[at_row(b * q, q)]).astype(bf16)
    to_second[...] = add(in0[at_row((1 - b) * q, q)], got0[at_row((1 - b) * q, q)]).astype(bf16)
    stay[q : 2 * q] = add(in1[0], got1[0]).astype(bf16)
    to_far[...] = add(in1[1], got1[1]).astype(bf16)
    stay[2 * q :] = add(in2[at_row(a * q, q)], got2[at_row(a * q, q)]).astype(bf16)
    to_first[...] = add(in2[at_row((1 - a) * q, q)], got2[at_row((1 - a) * q, q)]).astype(bf16)


def merge_four(info, stay, second, far, first, keep0, got0, keep1, got1, part, mine, to_first, to_far, to_both):
    q = second.shape[0]
    for i, x in enumerate((second, far, first)):
        part[i * q : (i + 1) * q] = add(stay[i * q : (i + 1) * q], x[...]).astype(bf16)
    a = info[4]
    h = mine.shape[0] - 16
    for dst, keep, got, g, m in (
        (mine, keep0, got0, 0, a), (to_first, keep0, got0, 0, 1 - a),
        (to_far, keep1, got1, 1, a), (to_both, keep1, got1, 1, 1 - a),
    ):
        here = at_row(m * h, h)
        tail = slice(2 * h + 16 * g, 2 * h + 16 * g + 16)
        dst[:h] = add(keep[here], got[here]).astype(bf16)
        dst[h:] = add(keep0[tail], got0[tail]).astype(bf16)


def merge_five(info, part, third, mine, first, far, both, own, to_second, to_first, total):
    q = part.shape[0] // 3
    to_second[: 2 * q] = add(part[: 2 * q], third[: 2 * q]).astype(bf16)
    to_first[...] = add(part[2 * q :], third[2 * q :]).astype(bf16)
    total[...] = (add(mine[...], first[...]) + add(far[...], both[...])).astype(bf16)
    n = own.shape[0] - 16
    for dst, base, m in ((own, 0, info[5]), (to_second, 2 * q, 1 - info[5])):
        dst[base : base + n] = total[at_row(m * n, n)]
        dst[base + n : base + n + 16] = total[2 * n :]


def merge_six(info, near2, got2, near1, got1, own, to_first, to_second, to_third):
    a, b = info[4], info[5]
    q = near1.shape[0]
    for c in range(2):
        to_first[at_row(2 * c * q + b * q, q)] = near2[c * q : (c + 1) * q]
        to_first[at_row(2 * c * q + (1 - b) * q, q)] = got2[c * q : (c + 1) * q]
    to_second[at_row(a * q, q)] = near1[...]
    to_second[at_row((1 - a) * q, q)] = got1[...]
    to_third[...] = add(own[...], got2[2 * q :]).astype(bf16)


def merge_seven(info, near1, got1, near2, got2, near3, got3, out, two, table, gains, shifts, ff, bias):
    a, b = info[4], info[5]
    h = near1.shape[0] // 2
    for c in range(2):
        out[at_row(2 * c * h + a * h, h)] = near1[c * h : (c + 1) * h]
        out[at_row(2 * c * h + (1 - a) * h, h)] = got1[c * h : (c + 1) * h]
    out[at_row(4 * h + b * h, h)] = near2[...]
    out[at_row(4 * h + (1 - b) * h, h)] = got2[...]
    n = two.shape[0]
    s = add(near3[...], got3[...])
    two[...] = s[:n].astype(bf16)
    s = s[n:]
    width = s.shape[1]
    table[...] = s[0:2]
    gains[...] = s[2:4]
    shifts[...] = s[4:8]
    ff[:, :width] = s[8:9]
    ff[:, width:] = s[9:10]
    bias[0:1] = s[10:11, : width // 2]
    bias[1:2] = s[10:11, width // 2 :]


def merge_eight(info, near, first, second, both, out):
    n = near.shape[0]
    a, b = info[4], info[5]
    for x, i, j in ((near, a, b), (first, 1 - a, b), (second, a, 1 - b), (both, 1 - a, 1 - b)):
        out[at_row(2 * n * i + n * j, n)] = x[...]


def merge(body, info, ins, outs, width, with_info=True):
    shapes = [(s if isinstance(s, tuple) else (s, width), bf16, VMEM) for s in outs]
    return call(
        body,
        shapes,
        [SMEM] * with_info + [VMEM] * len(ins),
        ((info,) if with_info else ()) + tuple(ins),
        [],
        24,
        2 * US,
        2e6,
        hbm_in=False,
        hbm_out=False,
    )


def sum_start(info, keep, send, bits, far, core):
    first, second, _ = bits
    width = keep.shape[2]
    n = keep.shape[1] // 3
    two = (2, n // 2, width)
    stay0, far0, stay1, first1, stay2, second2 = call(
        merge_cores,
        [(x, bf16, VMEM) for x in ((n, width), (n, width), two, two, two, two)],
        [SMEM, FAR, HBM],
        (info, keep, hop(send, core)),
        [pltpu.VMEM(keep.shape, bf16)] * 2 + [pltpu.SemaphoreType.DMA((3,))] * 2,
        24,
        2 * US,
        2e6,
        hbm_out=False,
    )
    return (stay0, hop(far0, far), stay1, hop(first1, first), stay2, hop(second2, second))


def sum_middle(info, state, bits, far, width):
    first, second, _ = bits
    n = state[0].shape[0]
    q = n // 4
    keep0, first0, keep1, second1, keep2, far2 = merge(
        merge_two, info, state, (n // 2, n // 2, (2, q, width), (2, q, width), n // 2, n // 2), width
    )
    return (keep0, hop(first0, first), keep1, hop(second1, second), keep2, hop(far2, far))


def sum_finish(info, state, late, bits, far, core, beside):
    first, second, third = bits
    width = state[0].shape[1]
    q = state[0].shape[0] // 2
    keep0, send0, keep1, got1 = late
    stay, to_second, to_far, to_first = merge(merge_three, info, state, (3 * q, q, q, q), width)
    send0, stay = lax.optimization_barrier((send0, stay))
    got0 = hop(send0, core)
    h = keep1.shape[0] // 2
    part, mine, to_first, to_far, to_both = merge(
        merge_four,
        info,
        (stay, hop(to_second, second), hop(to_far, far), hop(to_first, first), keep0, got0, keep1, got1),
        (3 * q, h + 16, h + 16, h + 16, h + 16),
        width,
    )
    rows = beside[0](part)
    got = hop(part, third), hop(to_first, first), hop(to_far, far), hop(to_both, first, far)
    part, rows = lax.optimization_barrier((part, rows))
    m = h // 2
    own, to_second, to_first, _ = merge(
        merge_five, info, (part, got[0], mine, *got[1:]), (m + 16, 2 * q + m + 16, q, h + 16), width
    )
    blanks_one = beside[1](own)
    got = hop(to_second, second), hop(to_first, first)
    own, blanks_one[0] = lax.optimization_barrier((own, blanks_one[0]))
    to_first, to_second, to_third = merge(
        merge_six, info, (to_second, got[0], to_first, got[1], own), (4 * q, 2 * q, m + 16), width
    )
    blanks_two = beside[2](to_third)
    got = hop(to_first, first), hop(to_second, second), hop(to_third, third)
    to_first, blanks_two[0] = lax.optimization_barrier((to_first, blanks_two[0]))
    one, two, *small = call(
        merge_seven,
        [((12 * q, width), bf16, VMEM), ((m, width), bf16, VMEM)]
        + [(shape, f32, VMEM) for shape in ((2, width), (2, width), (4, width), (1, 2 * width), (2, width // 2))],
        [SMEM] + [VMEM] * 6,
        (info, to_first, got[0], to_second, got[1], to_third, got[2]),
        [],
        24,
        2 * US,
        2e6,
        hbm_in=False,
        hbm_out=False,
    )
    other = hop(one, core)
    got = hop(two, first), hop(two, second), hop(two, first, second)
    blanks_three = beside[3](two)
    two, blanks_three[0] = lax.optimization_barrier((two, blanks_three[0]))
    (two,) = merge(merge_eight, info, (two, *got), (4 * m,), width)
    return (one, other), (two, hop(two, core)), small, (rows, blanks_two + blanks_one + blanks_three)


def wipe(*refs):
    sems = refs[-1]
    count = sems.shape[0]
    outs, zeros = refs[1 : 1 + count], refs[1 + count : -1]
    for zero in zeros:
        zero[...] = jnp.zeros_like(zero)
    copies = []
    for i, out in enumerate(outs):
        src = next(z for z in zeros if z.dtype == out.dtype and z.shape[1] == out.shape[1])
        rows = out.shape[0]
        n = next(c for c in (256, 192, 128, 64, 32, 16) if rows % c == 0)
        for at in range(0, rows, n):
            copies.append(
                pltpu.make_async_copy(
                    src.at[pl.ds(0, n), :], out.at[pl.ds(at, n), :], sems.at[i]
                )
            )
    for copy in copies:
        copy.start()
    for copy in copies:
        copy.wait()


def blanks_for(gate, likes):
    flat = [(math.prod(x.shape[:-1]), x.shape[-1]) for x in likes]
    widths = sorted({n for _, n in flat})
    outs = call(
        wipe,
        [(s, x.dtype, HBM) for s, x in zip(flat, likes)],
        [HBM],
        (gate,),
        [pltpu.VMEM((256, n), k) for n in widths for k in (f32, bf16)]
        + [pltpu.SemaphoreType.DMA((len(likes),))],
        8,
        US // 2,
        1e6,
        hbm_in=False,
    )
    return [x.reshape(like.shape) for x, like in zip(outs, likes)]


def moments(turned, m, v):
    first = BETA_ONE * m[...] + (1.0 - BETA_ONE) * turned
    second = BETA_TWO * v[...] + (1.0 - BETA_TWO) * (turned * turned)
    m[...] = first
    v[...] = second
    return (first / (jnp.sqrt(second) + EPS_ADAM)).astype(bf16)


def fetch(pairs, sems):
    for copy in copy_all(pairs, sems):
        copy.wait()


def step_wide(g, w, m, v, ql, qr, rate, scratch, ready):
    low_l, low_r, mid, back = scratch
    low_l[...] = ql[...].astype(bf16)
    low_r[...] = qr[...].astype(bf16)
    blocks, size = qr.shape[0], qr.shape[1]
    mid[...] = nn(ql[...].T.astype(bf16), g).astype(bf16)
    for b in range(blocks):
        at = slice(b * size, (b + 1) * size)
        u = moments(nn(mid[:, at], low_r[b]), m.at[:, at], v.at[:, at])
        back[:, at] = nt(u, low_r[b]).astype(bf16)
    ready()
    w[...] = w[...] - rate * nn(low_l[...], back[...])


def step_tall(g, w, m, v, ql, qr, rate, scratch, ready):
    low_r, mid, back = scratch
    low_r[...] = qr[...].astype(bf16)
    blocks, size = ql.shape[0], ql.shape[1]
    for b in range(blocks):
        at = slice(b * size, (b + 1) * size)
        mid[at, :] = nn(ql[b].T.astype(bf16), g[at, :]).astype(bf16)
    u = moments(nn(mid[...], low_r[...]), m, v)
    ready()
    back[...] = nt(u, low_r[...]).astype(bf16)
    for b in range(blocks):
        at = slice(b * size, (b + 1) * size)
        w[at, :] = w[at, :] - rate * nn(ql[b].astype(bf16), back[at, :])


def update_qkv(rate, mine, g, w_in, m_in, v_in, ql_in, qr_in, *refs):
    outs, (grad, new, mom, var, copy) = refs[:4], refs[4:9]
    w, m, v, c, ql, qr, low_l, low_r, mid, back, sems = refs[9:]
    for j in range(3):
        grad[j] = g[j].astype(f32)

        @pl.when(mine[j] == 1)
        def _():
            fetch(
                [(w_in.at[j], w), (m_in.at[j], m), (v_in.at[j], v), (ql_in.at[j], ql), (qr_in.at[j], qr)], sems
            )
            step_wide(g[j], w, m, v, ql, qr, rate, (low_l, low_r, mid, back), lambda: None)
            c[...] = w[...].astype(bf16)
            fetch([(w, new.at[j]), (m, mom.at[j]), (v, var.at[j]), (c, copy.at[j])], sems)


def update_rest(rate_out, rate_up, rate_down, mine, g_out, g_up, g_down_t, *refs):
    (wo_in, mo_in, vo_in, lo_in, ro_in, wu_in, mu_in, vu_in, lu_in, ru_in,
     wd_in, md_in, vd_in, ld_in, rd_in) = refs[:15]
    refs = refs[15 + 11 :]
    grad_o, grad_u, grad_d = refs[:3]
    new_o, moments_o, copy_o, new_u, mom_u, var_u, copy_u, new_d, mom_d, var_d, copy_d = refs[3:14]
    (wo, mo, vo, co, lo, ro, low_ro, mid_o, back_o,
     wu, mu, vu, cu, lu, ru, low_lu, low_ru, mid_u, back_u,
     wd, md, vd, cd, mid_d, back_d, sems) = refs[14:]
    grad_o[...] = g_out[...].astype(f32)
    grad_u[...] = g_up[...].astype(f32)
    grad_d[...] = g_down_t[...].astype(f32).T

    @pl.when(mine[3] == 1)
    def _():
        fetch([(wo_in, wo), (mo_in, mo), (vo_in, vo), (lo_in, lo), (ro_in, ro)], sems)
        step_tall(g_out[...], wo, mo, vo, lo, ro, rate_out, (low_ro, mid_o, back_o), lambda: None)
        co[...] = wo[...].astype(bf16)
        fetch([(wo, new_o), (mo, moments_o.at[0]), (vo, moments_o.at[1]), (co, copy_o)], sems)

    @pl.when(mine[4] == 1)
    def _():
        fetch([(wu_in, wu), (mu_in, mu), (vu_in, vu), (lu_in, lu), (ru_in, ru)], sems)
        step_wide(g_up[...], wu, mu, vu, lu, ru, rate_up, (low_lu, low_ru, mid_u, back_u), lambda: None)
        cu[...] = wu[...].astype(bf16)
        fetch([(wu, new_u), (mu, mom_u), (vu, var_u), (cu, copy_u)], sems)

    @pl.when(mine[5] == 1)
    def _():
        fetch([(wd_in, wd), (md_in, md), (vd_in, vd), (ld_in, ru), (rd_in, lu)], sems)
        step_tall(grad_d[...].astype(bf16), wd, md, vd, ru, lu, rate_down, (low_lu, mid_d, back_d), lambda: None)
        cd[...] = wd[...].astype(bf16)
        fetch([(wd, new_d), (md, mom_d), (vd, var_d), (cd, copy_d)], sems)


def update_all(rate_out, rate_wide, rate_down, cols, hid, owned, info, mine, other, mine_q, other_q, *refs):
    ins, refs = refs[:20], refs[20 + 15 :]
    grad_q, grad_o, grad_u, grad_d = refs[:4]
    outs, held, refs = refs[4:19], refs[19:39], refs[39:]
    wq, mq, vq, lq, rq, wo, mo, vo, lo, ro, wu, mu, vu, lu, ru, wd, md, vd, ld, rd = held
    new_q, mom_q, var_q, copy_q, new_o, mom_o, copy_o, new_u, mom_u, var_u, copy_u, new_d, mom_d, var_d, copy_d = outs
    buf, buf_q, gq, go, gu, gd, cq, co, cu, cd = refs[:10]
    low_l, low_r64, low_r256, mid_q, mid_o, mid_u, mid_d, back_q, back_o, back_u, back_d = refs[10:21]
    sems, in_sems, out_sems = refs[21:]
    core = info[0]
    loads = []
    for k in (4, 5, 3, 0, 1, 2):
        base = 5 * max(k - 2, 0)
        some = [(a.at[k], b.at[k]) if k < 3 else (a, b) for a, b in zip(ins[base : base + 5], held[base : base + 5])]
        some = [pltpu.make_async_copy(a, b, in_sems.at[k, i]) for i, (a, b) in enumerate(some)]
        loads.append((k, some))

        @pl.when(owned[k] == 1)
        def _(some=some):
            for copy in some:
                copy.start()

    loads = dict(loads)
    width = buf.shape[1]
    half = width // 2
    n = mine.shape[0]
    n_q = mine_q.shape[0]
    fills = copy_all(
        [(mine, buf.at[at_row(core * n, n)]), (other, buf.at[at_row((1 - core) * n, n)]),
         (mine_q, buf_q.at[at_row(core * n_q, n_q)]), (other_q, buf_q.at[at_row((1 - core) * n_q, n_q)])],
        sems,
    )
    pending = []

    def give(scratch, out, k):
        copy = pltpu.make_async_copy(scratch, out, sems.at[4 + k])
        copy.start()
        pending.append((None, copy))

    def finish(k, w, m, v, c, outs, run):
        stores = [
            pltpu.make_async_copy(a, b, out_sems.at[k, i]) for i, (a, b) in enumerate(zip((w, m, v, c), outs))
        ]

        @pl.when(owned[k] == 1)
        def _():
            for copy in loads[k]:
                copy.wait()

            def ready():
                stores[1].start()
                stores[2].start()

            run(ready)
            stores[0].start()
            c[...] = w[...].astype(bf16)
            stores[3].start()

        pending.extend((owned[k] == 1, copy) for copy in stores)

    fills[0].wait()
    fills[1].wait()
    h = hid // 2
    for i in range(2):
        gu[:, i * h : (i + 1) * h] = buf[i * width : (i + 1) * width, :].astype(f32)
    give(gu, grad_u, 0)
    finish(4, wu, mu, vu, cu, (new_u, mom_u, var_u, copy_u),
           lambda ready: step_wide(gu[...].astype(bf16), wu, mu, vu, lu, ru, rate_wide,
                                   (low_l, low_r256, mid_u, back_u), ready))
    for i in range(2):
        gd[i * h : (i + 1) * h, :] = buf[hid + i * width : hid + (i + 1) * width, :].astype(f32).T
    give(gd, grad_d, 1)
    finish(5, wd, md, vd, cd, (new_d, mom_d, var_d, copy_d),
           lambda ready: step_tall(gd[...].astype(bf16), wd, md, vd, ld, rd, rate_down,
                                   (low_l, mid_d, back_d), ready))
    go[...] = buf[2 * hid : 2 * hid + cols, :].astype(f32)
    give(go, grad_o, 2)
    finish(3, wo, mo, vo, co, (new_o, mom_o.at[0], mom_o.at[1], copy_o),
           lambda ready: step_tall(go[...].astype(bf16), wo, mo, vo, lo, ro, rate_out,
                                   (low_l, mid_o, back_o), ready))
    fills[2].wait()
    fills[3].wait()
    for j in range(3):
        x = buf_q[j * half : (j + 1) * half, :].astype(f32)
        gq[j, :half, :] = x[:, :cols]
        gq[j, half:, :] = x[:, cols:]
        give(gq.at[j], grad_q.at[j], 3 + j)
        finish(j, wq.at[j], mq.at[j], vq.at[j], cq.at[j], [x.at[j] for x in (new_q, mom_q, var_q, copy_q)],
               lambda ready, j=j: step_wide(gq[j].astype(bf16), wq.at[j], mq.at[j], vq.at[j], lq.at[j], rq.at[j],
                                            rate_wide, (low_l, low_r64, mid_q, back_q), ready))
    for flag, copy in pending:
        if flag is None:
            copy.wait()
        else:

            @pl.when(flag)
            def _(copy=copy):
                copy.wait()


def pad_picks(picks):
    windows, heads, slots = picks.shape
    return jnp.pad(picks, ((0, 0), (0, 0), (0, SLOTS - slots)), constant_values=-1).reshape(
        windows, heads * SLOTS
    )


def per_device(
    tokens_in,
    cotangent,
    data_table,
    window_group,
    query_picks,
    owner_list,
    weight_qkv,
    head_bias,
    weight_out,
    weight_up,
    ff_bias,
    weight_down,
    norm_gains,
    shifts,
    first_qkv,
    second_qkv,
    first_out,
    second_out,
    first_up,
    second_up,
    first_down,
    second_down,
    basis_qkv_left,
    basis_qkv_right,
    basis_out_left,
    basis_out_right,
    basis_up_left,
    basis_up_right,
    basis_down_left,
    basis_down_right,
):
    head_count = lax.axis_size("head")
    head = lax.axis_index("head")
    my_rank = lax.axis_index("dp")
    rows, width = tokens_in.shape
    length = rows * head_count // window_group.shape[0]
    windows = rows // length
    head_dim = basis_qkv_right.shape[-1]
    cols = GROUP * head_dim
    scale = 1.0 / math.sqrt(head_dim)
    head_bits = head_count.bit_length() - 1
    far = ("head", head_bits - 1)
    core_bit = ("dp", 0)
    dp_bits = lax.axis_size("dp").bit_length() - 1
    bits = [("dp", k) for k in range(1, dp_bits)] + [("head", k) for k in range(head_bits - 1)]
    core = my_rank & 1
    quarter = my_rank & 3
    second_bit = ("dp", 1)
    slots = GROUP * SLOTS
    half = width // 2

    if head_count == 2:
        n_qkv, n_bias, n_out, n_up, n_ff, n_down = (
            weight_qkv, head_bias, weight_out, weight_up, ff_bias, weight_down
        )
        picks = pad_picks(query_picks).astype(f32)
        near_at, far_at = head * windows, (1 - head) * windows
    else:
        def whole_of(x, dim):
            return lax.all_gather(x, "head", axis=dim, tiled=True)

        def pick_group(x, dim, g):
            n = x.shape[dim] // 2
            return lax.dynamic_slice_in_dim(x, (side(far) ^ g) * n, n, dim)

        both = [
            (whole_of(weight_qkv.astype(bf16), 2).astype(f32), 2),
            (whole_of(head_bias, 1), 1),
            (whole_of(weight_out.astype(bf16), 0).astype(f32), 0),
            (whole_of(weight_up.astype(bf16), 1).astype(f32), 1),
            (whole_of(ff_bias, 0), 0),
            (whole_of(weight_down.astype(bf16), 0).astype(f32), 0),
        ]
        n_qkv, n_bias, n_out, n_up, n_ff, n_down = (pick_group(x, d, 0) for x, d in both)
        away = [pick_group(x, d, 1) for x, d in both]
        picks = lax.dynamic_slice_in_dim(whole_of(query_picks, 1), head * windows, windows, 0)
        picks = jnp.concatenate([pad_picks(pick_group(picks, 1, g)) for g in range(2)]).astype(f32)
        near_at, far_at = jnp.int32(0), jnp.int32(windows)
    info = jnp.stack([core, near_at, far_at, head * windows] + [side(b) for b in bits[:3]] + [quarter]).astype(jnp.int32)
    quick = head_count == 2 and len(bits) == 3
    hid = n_up.shape[1]
    extra_rows = -(-(windows + 6) // 16) * 16
    buf_rows = 2 * hid + cols
    rest_rows = cols // 4 + width // 2 + 16

    def send_qkv(info, w, bias):
        return call(
            lambda *refs: pack_qkv(windows, *refs),
            [((3 * width // 4 + extra_rows, cols), bf16, VMEM)],
            [SMEM, FAR, FAR, FAR],
            (info, w, bias, picks),
            [
                pltpu.VMEM((3, width // 4, cols), f32),
                pltpu.VMEM((extra_rows, cols), f32),
                pltpu.VMEM(bias.shape, f32),
                pltpu.VMEM(picks.shape, f32),
                pltpu.SemaphoreType.DMA((5,)),
            ],
            12,
            2 * US,
            3e6,
            hbm_out=False,
        )

    def send_rest(info, w_out, w_up, w_down, bias):
        return call(
            pack_rest,
            [
                ((rest_rows, width), bf16, VMEM),
                ((hid // 4, width), bf16, VMEM),
                ((cols, width), bf16, VMEM),
                ((width, hid), bf16, VMEM),
                ((hid, width), bf16, VMEM),
            ],
            [SMEM, VMEM, VMEM, VMEM, VMEM],
            (info, w_out, w_up, w_down, bias[None]),
            [pltpu.VMEM((16, width), f32)],
            24,
            4 * US,
            8e6,
            hbm_in=False,
            hbm_out=False,
        )

    (qkv_piece,) = send_qkv(info, n_qkv, n_bias)
    if head_count == 2:
        qkv_y = hop(qkv_piece, far)
        rest_piece, down_piece, *near_low = send_rest(info, n_out, n_up, n_down, n_ff)
    else:
        near_low = send_rest(info, n_out, n_up, n_down, n_ff)[2:]
        others = [info.at[7].set(quarter ^ i) for i in range(4)]
        qkv_all = [send_qkv(m, away[0], away[1])[0] for m in others]
        rest_all, down_all = zip(*(send_rest(m, away[2], away[3], away[5], away[4])[:2] for m in others))

    block = 2 * length
    steps = (rows // block,)
    wide = windows
    wide_block, wide_steps = wide * length, (windows // wide,)
    back_wide = 4 if windows % 4 == 0 else 2
    back_block, back_steps = back_wide * length, (windows // back_wide,)
    seen = [
        ((rows, cols), bf16, cut(wide_block, cols)),
        ((rows, cols), bf16, cut(wide_block, cols)),
        ((rows, cols), bf16, cut(wide_block, cols)),
        ((rows, cols), bf16, cut(wide_block, cols)),
        ((windows, slots, length), f32, cut(wide, slots, length)),
        ((windows, slots, cols), bf16, cut(wide, slots, cols)),
    ]
    q0, k0, v0, ctx0, att0, picked0, emb, emb_t, wq0 = call(
        lambda *refs: attend_own(length, scale, *refs),
        seen
        + [
            ((rows, width), bf16, cut(wide_block, width)),
            ((width, rows), bf16, pl.BlockSpec((width, wide_block), lambda i: (0, i))),
            ((3, width, cols), bf16, whole(3, width, cols)),
        ],
        [SMEM, SMEM, cut(wide_block, width), whole(NDATA, width), whole(3, width, cols),
         whole(2, cols), whole(*picks.shape)],
        (info, window_group, tokens_in, data_table, n_qkv, n_bias, picks),
        [],
        24,
        9 * US,
        6e6,
        grid=wide_steps,
        hbm_in=False,
    )
    if head_count == 2:

        def spread(x):
            across = hop(x, second_bit)
            return [x, hop(x, core_bit), across, hop(across, core_bit)]

        rest_y = hop(rest_piece, far)
        qkv_y, ctx0, near_low[0] = lax.optimization_barrier((qkv_y, ctx0, near_low[0]))
        qkv_all = spread(qkv_y)
        rest_y, emb, down_piece = lax.optimization_barrier((rest_y, emb, down_piece))
        down_y = hop(down_piece, far)
        rest_all = spread(rest_y)
    q1, k1, v1, ctx1, att1, picked1, wq1, picks1 = call(
        lambda *refs: attend_far(length, scale, *refs),
        seen + [((3, width, cols), bf16, whole(3, width, cols)), ((windows, slots), f32, whole(windows, slots))],
        [SMEM, cut(wide_block, width)] + [HBM] * 4,
        (info, emb, *qkv_all),
        [
            pltpu.VMEM((extra_rows, cols), bf16),
            pltpu.VMEM((2, cols), f32),
            pltpu.SemaphoreType.DMA((13,)),
        ],
        24,
        9 * US,
        6e6,
        grid=wide_steps,
        hbm_in=False,
    )
    if head_count == 2:
        down_y, ctx1 = lax.optimization_barrier((down_y, ctx1))
        down_all = spread(down_y)

    def kinds(x):
        return [jax.ShapeDtypeStruct(x.shape, k) for k in (f32, f32, f32, bf16)]

    few = kinds(first_qkv) + [
        jax.ShapeDtypeStruct(first_out.shape, f32),
        jax.ShapeDtypeStruct((2,) + first_out.shape, f32),
        jax.ShapeDtypeStruct(first_out.shape, bf16),
    ]
    many = kinds(first_up) + kinds(first_down)

    def make_few(gate):
        return blanks_for(gate, few)

    def make_many(gate):
        return blanks_for(gate, many)

    def make_input_grad(gp1):
        return call(
            input_grad,
            [((rows, width), f32, cut(block, width))],
            [cut(block, cols)] * 6 + [whole(3, width, cols)] * 2 + [cut(block, width)],
            (gq0, gk0, gv0, gq1, gk1, gv1, wq0, wq1, gp1),
            [],
            24,
            US // 2,
            1e6,
            grid=steps,
        )[0]

    parts = 2 if windows % 4 == 0 else 1
    output_rows, gp1, ga, keep_one, send_one, sums, wo = call(
        lambda *refs: feed_forward(length, parts, *refs),
        [
            ((rows, width), f32, HBM),
            ((rows, width), f32, HBM),
            ((rows, width), bf16, HBM),
            ((2, buf_rows // 2, width), bf16, HBM),
            ((2, buf_rows // 2, width), bf16, HBM),
            ((16, width), f32, VMEM),
            ((2, cols, width), bf16, HBM),
        ],
        [SMEM, SMEM, VMEM, VMEM, VMEM, VMEM] + [HBM] * 11 + [VMEM, VMEM, VMEM, HBM],
        (info, window_group, tokens_in, data_table, ctx0, ctx1, *near_low, *rest_all, *down_all,
         n_ff[None], norm_gains, shifts, cotangent),
        [
            pltpu.VMEM((2, cols, width), bf16),
            pltpu.VMEM((2, width, hid), bf16),
            pltpu.VMEM((2, hid, width), bf16),
            pltpu.VMEM((rows, 2 * hid), bf16),
            pltpu.VMEM((rows, 2 * hid), bf16),
            pltpu.VMEM((rows, 2 * hid), bf16),
            pltpu.VMEM((rows, width), bf16),
            pltpu.VMEM((rows, width), bf16),
            pltpu.VMEM((rows, width), bf16),
            pltpu.VMEM((rows, width), f32),
            pltpu.VMEM((rows, width), f32),
            pltpu.VMEM((rows, width), f32),
            pltpu.VMEM((rows, width), f32),
            pltpu.VMEM((width, rows), bf16),
            pltpu.VMEM((width, rows), bf16),
            pltpu.VMEM((2, hid), f32),
            pltpu.VMEM((16, width), bf16),
            pltpu.VMEM((2, buf_rows, width), bf16),
            pltpu.SemaphoreType.DMA((21,)),
            pltpu.SemaphoreType.DMA((3,)),
            pltpu.SemaphoreType.DMA((5,)),
        ],
        50,
        24 * US,
        20e6,
    )
    if quick:
        state_one = sum_start(info, keep_one, send_one, bits, far, core_bit)
        ga, held = lax.optimization_barrier((ga, state_one[0]))
        state_one = (held, *state_one[1:])
    else:
        sum_one = plus(keep_one, hop(send_one, core_bit))
        sum_one, ga = lax.optimization_barrier((sum_one, ga))

    def make_back(g, ga, picks, wq, k, v, att, picked, extra_in):
        last = g == 0
        n = 3 * half // 2 + 32 * last
        more = [((16, cols), f32, whole(16, cols)), ((8, width), f32, whole(8, width))]
        return call(
            lambda *refs: attend_back(length, scale, g, *refs),
            [((rows, cols), bf16, cut(back_block, cols))] * 3
            + [((n, width), bf16, HBM)] * 2
            + ([] if last else more),
            [SMEM, SMEM, cut(back_block, width), FAR, whole(2, cols, width), whole(*picks.shape), FAR,
             cut(back_block, cols), cut(back_block, cols), cut(back_wide, slots, length), cut(back_wide, slots, cols)]
            + [whole(*x.shape) for x in extra_in],
            (info, window_group, ga, emb_t, wo, picks, wq, k, v, att, picked, *extra_in),
            [pltpu.VMEM((rows, cols), bf16)] * 3
            + [
                pltpu.VMEM((width, rows), bf16),
                pltpu.VMEM((3, width, cols), bf16),
                pltpu.VMEM((3 * half + 32 * last, width), bf16),
            ]
            + ([pltpu.VMEM((16, cols), f32), pltpu.VMEM((32, width), f32)] if last else [])
            + [pltpu.SemaphoreType.DMA((10,))],
            32,
            6 * US,
            8e6,
            grid=back_steps,
        )

    gq1, gk1, gv1, keep_far, send_far, tsum, table_far = make_back(
        1, ga, picks1, wq1, k1, v1, att1, picked1, ()
    )
    if quick:
        held, keep_far, send_far = lax.optimization_barrier((state_one[0], keep_far, send_far))
        state_one = sum_middle(info, (held, *state_one[1:]), bits, far, width)
        held, ga, send_far = lax.optimization_barrier((state_one[0], ga, send_far))
        state_one = (held, *state_one[1:])
        got_far = hop(send_far, core_bit)
    gq0, gk0, gv0, keep_near, send_near = make_back(
        0, ga, picks, wq0, k0, v0, att0, picked0, (sums, tsum, table_far)
    )

    shards = head_count // 2
    mine = head % shards

    def shard(x, dim):
        n = x.shape[dim] // shards
        return x if shards == 1 else lax.dynamic_slice_in_dim(x, mine * n, n, dim)

    owned = (owner_list == my_rank).astype(jnp.int32)

    rate_wide = width ** (-0.5)
    rate_out = max(width // head_dim, 1) ** (-0.5)
    rate_down = (n_down.shape[0] * 2) ** (-0.5)
    moments_in = (
        weight_qkv, first_qkv, second_qkv, basis_qkv_left, basis_qkv_right,
        weight_out, first_out, second_out, basis_out_left, basis_out_right,
        weight_up, first_up, second_up, basis_up_left, basis_up_right,
        weight_down, first_down, second_down, basis_down_left, basis_down_right,
    )
    if quick:
        held, keep_near, send_near = lax.optimization_barrier((state_one[0], keep_near, send_near))
        beside = (
            lambda gate: make_input_grad(lax.optimization_barrier((gp1, gate))[0]),
            lambda gate: blanks_for(gate, kinds(first_up)),
            make_few,
            lambda gate: blanks_for(gate, kinds(first_down)),
        )
        pieces_one, pieces_two, small, (grad_rows, blanks) = sum_finish(
            info, (held, *state_one[1:]), (keep_near, send_near, keep_far, got_far), bits, far, core_bit, beside
        )
        likes = [first_qkv, first_out, first_up, first_down]
        temps = [first_qkv.shape[1:], first_out.shape, first_up.shape, first_down.shape]
        outs = call(
            lambda *refs: update_all(rate_out, rate_wide, rate_down, cols, hid, *refs),
            [(x.shape, f32, HBM) for x in likes] + [(x.shape, x.dtype, HBM) for x in blanks],
            [SMEM, SMEM] + [HBM] * 4 + [FAR] * 35,
            (owned, info, *pieces_one, *pieces_two, *moments_in, *blanks),
            [pltpu.VMEM(x.shape, f32) for x in moments_in]
            + [pltpu.VMEM((buf_rows, width), bf16), pltpu.VMEM((3 * half, width), bf16)]
            + [pltpu.VMEM(x.shape, f32) for x in likes]
            + [pltpu.VMEM(x.shape, bf16) for x in likes]
            + [
                pltpu.VMEM((width, width), bf16),
                pltpu.VMEM(basis_qkv_right.shape[1:], bf16),
                pltpu.VMEM(basis_up_right.shape, bf16),
            ]
            + [pltpu.VMEM(x, bf16) for x in temps * 2]
            + [
                pltpu.SemaphoreType.DMA((10,)),
                pltpu.SemaphoreType.DMA((6, 5)),
                pltpu.SemaphoreType.DMA((6, 4)),
            ],
            49,
            12 * US,
            30e6,
            {26 + i: 4 + i for i in range(15)},
        )
        grad_qkv_all, grad_out_all, grad_up_all, grad_down_all = outs[:4]
        qkv_outs, rest_outs = outs[3:8], outs[5:19]
        grad_table_all, grad_gains_all, grad_shifts_all, grad_ff_all, grad_bias_all = small
        grad_ff_all = grad_ff_all.reshape(-1)
    else:
        grad_rows = make_input_grad(gp1)
        n = 3 * half // 2
        keep_two, send_two = (
            jnp.stack([near[: n + 16], jnp.concatenate([away_part, near[n + 16 :]])])
            for near, away_part in ((keep_near, keep_far), (send_near, send_far))
        )
        blanks = make_few(sums) + make_many(sums)
        early, late = early_steps(bits, far, core_bit), late_steps(16, bits, far, core_bit)
        state_one, state_two = early[0](sum_one), (keep_two, send_two)
        for i in range(1, max(len(early), len(late) + 1)):
            state_one, state_two = lax.optimization_barrier((state_one, state_two))
            if i < len(early):
                state_one = early[i](state_one)
            if i <= len(late):
                state_two = late[i - 1](state_two)
        sum_one, (sum_two, small) = state_one, state_two
        small = small[0]
        g_up = shard(jnp.concatenate([sum_one[:width], sum_one[width : 2 * width]], 1), 1)
        g_down_t = shard(
            jnp.concatenate([sum_one[2 * width : 3 * width], sum_one[3 * width : 4 * width]], 1), 1
        )
        g_out = shard(sum_one[4 * width :], 0)

        def rest_body(*refs):
            update_rest(rate_out, rate_wide, rate_down, *refs)

        tall, wide, low = first_out.shape, first_up.shape, first_down.shape
        rest_outs = call(
            rest_body,
            [(tall, f32, VMEM), (wide, f32, VMEM), (low, f32, VMEM)]
            + [(x.shape, x.dtype, HBM) for x in blanks[4:]],
            [SMEM, VMEM, VMEM, VMEM] + [HBM] * (15 + 11),
            (owned, g_out, g_up, g_down_t,
             weight_out, first_out, second_out, basis_out_left, basis_out_right,
             weight_up, first_up, second_up, basis_up_left, basis_up_right,
             weight_down, first_down, second_down, basis_down_left, basis_down_right, *blanks[4:]),
            [pltpu.VMEM(tall, f32)] * 3
            + [
                pltpu.VMEM(tall, bf16),
                pltpu.VMEM(basis_out_left.shape, f32),
                pltpu.VMEM(basis_out_right.shape, f32),
                pltpu.VMEM(basis_out_right.shape, bf16),
                pltpu.VMEM(tall, bf16),
                pltpu.VMEM(tall, bf16),
            ]
            + [pltpu.VMEM(wide, f32)] * 3
            + [
                pltpu.VMEM(wide, bf16),
                pltpu.VMEM(basis_up_left.shape, f32),
                pltpu.VMEM(basis_up_right.shape, f32),
                pltpu.VMEM(basis_up_left.shape, bf16),
                pltpu.VMEM(basis_up_right.shape, bf16),
                pltpu.VMEM(wide, bf16),
                pltpu.VMEM(wide, bf16),
            ]
            + [pltpu.VMEM(low, f32)] * 3
            + [pltpu.VMEM(low, bf16)] * 3
            + [pltpu.SemaphoreType.DMA((5,))],
            48,
            12 * US,
            20e6,
            {4 + 15 + i: 3 + i for i in range(11)},
        )
        grad_out_all, grad_up_all, grad_down_all = rest_outs[:3]

        pairs = sum_two.reshape(3, half, width)
        g_qkv = shard(jnp.concatenate([pairs[:, :, :cols], pairs[:, :, cols:]], 1), 2)
        small = small.astype(f32)

        def qkv_body(*refs):
            update_qkv(rate_wide, *refs)

        one = first_qkv.shape[1:]
        qkv_outs = call(
            qkv_body,
            [(first_qkv.shape, f32, VMEM)] + [(x.shape, x.dtype, HBM) for x in blanks[:4]],
            [SMEM, VMEM] + [HBM] * 9,
            (owned, g_qkv, weight_qkv, first_qkv, second_qkv, basis_qkv_left, basis_qkv_right, *blanks[:4]),
            [pltpu.VMEM(one, f32)] * 3
            + [
                pltpu.VMEM(one, bf16),
                pltpu.VMEM(basis_qkv_left.shape[1:], f32),
                pltpu.VMEM(basis_qkv_right.shape[1:], f32),
                pltpu.VMEM(basis_qkv_left.shape[1:], bf16),
                pltpu.VMEM(basis_qkv_right.shape[1:], bf16),
                pltpu.VMEM(one, bf16),
                pltpu.VMEM(one, bf16),
                pltpu.SemaphoreType.DMA((5,)),
            ],
            24,
            6 * US,
            8e6,
            {7 + i: 1 + i for i in range(4)},
        )
        grad_qkv_all = qkv_outs[0]
        grad_table_all = small[0:2]
        grad_gains_all = small[2:4]
        grad_shifts_all = small[4:8]
        grad_ff_all = shard(small[8:10].reshape(-1), 0)
        grad_bias_all = shard(small[10].reshape(2, cols), 1)
    return (
        output_rows,
        grad_rows,
        grad_table_all,
        grad_gains_all,
        grad_shifts_all,
        grad_bias_all,
        grad_ff_all,
        grad_qkv_all,
        grad_out_all,
        grad_up_all,
        grad_down_all,
        *(x[None] for x in qkv_outs[1:]),
        *(x[None] for x in rest_outs[3:]),
    )


def solution(mesh):
    in_specs = (
        P(("dp", "head"), None),
        P(("dp", "head"), None),
        P(),
        P("dp"),
        P("dp", "head", None),
        P(),
        P(None, None, "head"),
        P(None, "head"),
        P("head", None),
        P(None, "head"),
        P("head"),
        P("head", None),
        P(),
        P(),
        P(None, None, "head"),
        P(None, None, "head"),
        P("head", None),
        P("head", None),
        P(None, "head"),
        P(None, "head"),
        P("head", None),
        P("head", None),
        P(),
        P(None, "head", None, None),
        P("head", None, None),
        P(),
        P(),
        P("head", None, None),
        P("head", None, None),
        P(),
    )
    out_specs = (
        P(("dp", "head"), None),
        P(("dp", "head"), None),
        P(),
        P(),
        P(),
        P(None, "head"),
        P("head"),
        P(None, None, "head"),
        P("head", None),
        P(None, "head"),
        P("head", None),
        P("dp", None, None, "head"),
        P("dp", None, None, "head"),
        P("dp", None, None, "head"),
        P("dp", None, None, "head"),
        P("dp", "head", None),
        P("dp", None, "head", None),
        P("dp", "head", None),
        P("dp", None, "head"),
        P("dp", None, "head"),
        P("dp", None, "head"),
        P("dp", None, "head"),
        P("dp", "head", None),
        P("dp", "head", None),
        P("dp", "head", None),
        P("dp", "head", None),
    )
    return jax.shard_map(
        per_device, mesh=mesh, in_specs=in_specs, out_specs=out_specs, check_vma=False
    )
```

```python
import math

import jax
import jax.numpy as jnp
from jax import lax
from jax.experimental import pallas as pl
from jax.experimental.pallas import tpu as pltpu
from jax.sharding import PartitionSpec as P

f32 = jnp.float32
bf16 = jnp.bfloat16

NDATA = 2
EPS_NORM = 1e-05
EPS_ADAM = 1e-08
BETA_ONE = 0.5
BETA_TWO = 0.5

GROUP = 4
SLOTS = 32
MB = 1 << 20


def nn(a, b):
    return jnp.dot(a, b, preferred_element_type=f32)


def nt(a, b):
    return lax.dot_general(a, b, (((1,), (1,)), ((), ())), preferred_element_type=f32)


def col_sum(x):
    return jnp.sum(x, axis=0, keepdims=True)


def row_mean(x):
    return jnp.mean(x, axis=-1, keepdims=True)


VMEM = pl.BlockSpec(memory_space=pltpu.VMEM)
SMEM = pl.BlockSpec(memory_space=pltpu.SMEM)
HBM = pl.BlockSpec(memory_space=pl.ANY)
FAR = pl.BlockSpec(memory_space=pl.ANY)


def whole(*shape):
    return pl.BlockSpec(shape, lambda i: (0,) * len(shape))


def cut(*shape):
    return pl.BlockSpec(shape, lambda i: (i,) + (0,) * (len(shape) - 1))


US = 1_000_000_000


def in_hbm(x, spec):
    small = x.size * x.dtype.itemsize < 1 << 16
    if spec is SMEM or spec is HBM or (small and spec is not FAR):
        return x
    return pltpu.with_memory_space_constraint(x, pltpu.HBM)


def call(body, outs, ins, args, scratch, limit, flops, nbytes, aliases={}, grid=(), hbm_in=True, hbm_out=True):
    if hbm_in:
        args = [in_hbm(x, spec) for x, spec in zip(args, ins)]
    kind = pltpu.HBM if hbm_out else jax.ShapeDtypeStruct
    return pl.pallas_call(
        body,
        grid=grid,
        out_shape=tuple(kind(s, d) for s, d, _ in outs),
        in_specs=ins,
        out_specs=tuple(spec for _, _, spec in outs),
        scratch_shapes=scratch,
        input_output_aliases=aliases,
        compiler_params=pltpu.CompilerParams(vmem_limit_bytes=limit * MB),
        cost_estimate=pl.CostEstimate(
            flops=int(flops), bytes_accessed=int(nbytes), transcendentals=0
        ),
    )(*args)


def head_mask(cols):
    width = cols // GROUP
    shape = (GROUP * SLOTS, cols)
    return (
        lax.broadcasted_iota(jnp.int32, shape, 0) // SLOTS
        == lax.broadcasted_iota(jnp.int32, shape, 1) // width
    )


def one_hot(picks, w, length):
    row = picks[pl.ds(w, 1), :]
    spots = lax.broadcasted_iota(jnp.int32, (length, GROUP * SLOTS), 0).astype(f32)
    columns = (spots == row).astype(f32)
    return columns.astype(bf16), columns.T.astype(bf16)


def copy_all(pairs, sems):
    copies = [pltpu.make_async_copy(a, b, sems.at[i]) for i, (a, b) in enumerate(pairs)]
    for copy in copies:
        copy.start()
    return copies


def split_sum(parts, at):
    return parts[at : at + 1] + parts[at + 1 : at + 2] + parts[at + 2 : at + 3]


def put_parts(extra, at, row):
    for i in range(3):
        part = row.astype(bf16).astype(f32)
        extra[at + i : at + i + 1, :] = part
        row = row - part


def pack_qkv(windows, info, w, bias_in, picks_in, piece, part, extra, bias, picks, sems):
    n = part.shape[1]
    rows = pl.ds(pl.multiple_of(info[7] * n, n), n)
    pairs = [(w.at[j, rows, :], part.at[j]) for j in range(3)] + [(bias_in, bias), (picks_in, picks)]
    copies = copy_all(pairs, sems)
    extra[...] = jnp.zeros_like(extra)
    for copy in copies[3:]:
        copy.wait()
    for i in range(windows):
        extra[i : i + 1, : GROUP * SLOTS] = picks[pl.ds(info[2] + i, 1), :]
    put_parts(extra, windows, bias[0:1, :])
    put_parts(extra, windows + 3, bias[1:2, :])
    piece[3 * n :, :] = extra[...].astype(bf16)
    for j, copy in enumerate(copies[:3]):
        copy.wait()
        piece[j * n : (j + 1) * n, :] = part[j].astype(bf16)


def pack_rest(info, w_out, w_up, w_down, bias, piece, down_piece, out_low, up_low, down_low, extra):
    hid = w_up.shape[1] // 2
    n_out, n_up, n_down = w_out.shape[0] // 4, w_up.shape[0] // 4, w_down.shape[0] // 4
    out_low[...] = w_out[...].astype(bf16)
    up_low[...] = w_up[...].astype(bf16)
    down_low[...] = w_down[...].astype(bf16)
    extra[...] = jnp.zeros_like(extra)
    put_parts(extra, 0, bias[:, :hid])
    put_parts(extra, 3, bias[:, hid:])
    piece[:n_out, :] = out_low[pl.ds(pl.multiple_of(info[7] * n_out, n_out), n_out), :]
    rows = pl.ds(pl.multiple_of(info[7] * n_up, n_up), n_up)
    for h in range(2):
        piece[n_out + h * n_up : n_out + (h + 1) * n_up, :] = up_low[rows, h * hid : (h + 1) * hid]
    piece[n_out + 2 * n_up :, :] = extra[...].astype(bf16)
    down_piece[...] = down_low[pl.ds(pl.multiple_of(info[7] * n_down, n_down), n_down), :]


def attend(wq, bias, picks, start, emb, q_out, k_out, v_out, ctx, att, picked, length, scale):
    cols = wq.shape[2]
    e = emb[...]
    for j, out in enumerate((q_out, k_out, v_out)):
        out[...] = (nn(e, wq[j]) + bias[j]).astype(bf16)
    mask = head_mask(cols)
    mask_low = mask.astype(f32).astype(bf16)
    spots = [slice(i * length, (i + 1) * length) for i in range(emb.shape[0] // length)]
    hots = [one_hot(picks, start + i, length) for i in range(len(spots))]
    sel = [nn(down, q_out[here, :]) for (_, down), here in zip(hots, spots)]
    sel = [jnp.where(mask, x, 0.0).astype(bf16) for x in sel]
    for i, x in enumerate(sel):
        picked[i] = x
    scores = [nt(x, k_out[here, :]) * scale for x, here in zip(sel, spots)]
    active = [nn(up, mask_low) for up, _ in hots]
    exponent = [jnp.exp(x - jnp.max(x, axis=-1, keepdims=True)) for x in scores]
    probs = [x * (1.0 / jnp.sum(x, axis=-1, keepdims=True)) for x in exponent]
    for i, x in enumerate(probs):
        att[i] = x
    mixed = [nn(x.astype(bf16), v_out[here, :]) for x, here in zip(probs, spots)]
    mixed = [jnp.where(mask, x, 0.0).astype(bf16) for x in mixed]
    mean = [col_sum(v_out[here, :].astype(f32)) * (1.0 / length) for here in spots]
    mixed = [nn(up, x) for (up, _), x in zip(hots, mixed)]
    for here, x, act, m in zip(spots, mixed, active, mean):
        ctx[here, :] = (x + (1.0 - act) * m).astype(bf16)


def attend_own(length, scale, info, groups, tokens, table, w, bias, picks,
               q, k, v, ctx, att, picked, emb, emb_t, wq):
    @pl.when(pl.program_id(0) == 0)
    def _():
        for j in range(3):
            wq[j] = w[j].astype(bf16)

    per = tokens.shape[0] // length
    first = pl.program_id(0) * per
    for i in range(per):
        here = slice(i * length, (i + 1) * length)
        row = table[pl.ds(groups[info[3] + first + i], 1), :]
        emb[here, :] = (tokens[here, :].astype(f32) + row).astype(bf16)
    emb_t[...] = emb[...].astype(f32).T.astype(bf16)
    rows = (bias[0:1, :], jnp.zeros_like(bias[0:1, :]), bias[1:2, :])
    attend(wq, rows, picks, info[1] + first, emb, q, k, v, ctx, att, picked, length, scale)


def attend_far(length, scale, info, emb, p0, p1, p2, p3,
               q, k, v, ctx, att, picked, wq, picks, extra, bias, sems):
    n = wq.shape[1] // 4
    windows = picks.shape[0]

    @pl.when(pl.program_id(0) == 0)
    def _():
        pairs = [(p0.at[pl.ds(3 * n, extra.shape[0]), :], extra)]
        for i, piece in enumerate((p0, p1, p2, p3)):
            for j in range(3):
                pairs.append(
                    (
                        piece.at[pl.ds(j * n, n), :],
                        wq.at[j, pl.ds(pl.multiple_of((info[7] ^ i) * n, n), n), :],
                    )
                )
        for copy in copy_all(pairs, sems):
            copy.wait()
        rest = extra[...].astype(f32)
        picks[...] = rest[:windows, : GROUP * SLOTS]
        bias[0:1, :] = split_sum(rest, windows)
        bias[1:2, :] = split_sum(rest, windows + 3)

    rows = (bias[0:1, :], jnp.zeros_like(bias[0:1, :]), bias[1:2, :])
    first = pl.program_id(0) * (emb.shape[0] // length)
    attend(wq, rows, picks, first, emb, q, k, v, ctx, att, picked, length, scale)


def gelu_pair(x):
    bell = jnp.exp2((x * x) * (-0.5 * math.log2(math.e)))
    y = 1.0 + (0.3275911 * math.sqrt(0.5)) * jnp.abs(x)
    t = pl.reciprocal(y, approx=True)
    t = t * (2.0 - y * t)
    poly = t * (
        0.5 * 0.254829592
        + t * (0.5 * -0.284496736 + t * (0.5 * 1.421413741 + t * (0.5 * -1.453152027 + t * (0.5 * 1.061405429))))
    )
    tail = poly * bell
    phi = jnp.where(x >= 0.0, 1.0 - tail, tail)
    return x * phi, phi + (x * (1.0 / math.sqrt(2.0 * math.pi))) * bell


def feed_forward(length, parts, info, groups, tokens, table, ctx0, ctx1, near_out, near_up, near_down,
                 p0, p1, p2, p3, d0, d1, d2, d3, ff_bias, gains, shifts, cot_in,
                 out_far, gp1_far, ga_far, keep, send, sums, wo_far,
                 wo, up, dn, act, gpre, slope, nl, gb, ga, out, gp1, pre, cot, nl_t, gb_t, ffb, extra, buf,
                 sems, row_sems, end_sems):
    core, quarter = info[0], info[7]
    rows, width = tokens.shape
    block = rows // parts
    cols = wo.shape[1]
    hid = up.shape[2]
    half = hid // 2

    def rows_of(x, i, n, *rest):
        return x.at[(1, pl.ds(pl.multiple_of((quarter ^ i) * n, n), n)) + rest]

    n_out, n_up, n_down = cols // 4, width // 4, hid // 4
    pairs = [[(near_out, wo.at[0])], [(near_up, up.at[0])], [(near_down, dn.at[0])], [(cot_in, cot)]]
    pairs[1].append((p0.at[pl.ds(n_out + 2 * n_up, 16), :], extra))
    for i, (p, d) in enumerate(((p0, d0), (p1, d1), (p2, d2), (p3, d3))):
        pairs[0].append((p.at[pl.ds(0, n_out), :], rows_of(wo, i, n_out)))
        for h in range(2):
            pairs[1].append(
                (p.at[pl.ds(n_out + h * n_up, n_up), :], rows_of(up, i, n_up, pl.ds(h * half, half)))
            )
        pairs[2].append((d, rows_of(dn, i, n_down)))
    loads, at = [], 0
    for some in pairs:
        loads.append([pltpu.make_async_copy(a, b, sems.at[at + i]) for i, (a, b) in enumerate(some)])
        at += len(some)
    for some in loads:
        for copy in some:
            copy.start()
    wo_copy = pltpu.make_async_copy(wo, wo_far, end_sems.at[4])
    ffb[0:1, :] = ff_bias[...]
    for i in range(rows // length):
        here = slice(i * length, (i + 1) * length)
        pre[here, :] = tokens[here, :].astype(f32) + table[pl.ds(groups[info[3] + i], 1), :]
    for copy in loads[0]:
        copy.wait()
    wo_copy.start()

    spans = [slice(i * block, (i + 1) * block) for i in range(parts)]
    inv_one = []
    xs = [nn(ctx0[here, :], wo[0]) + nn(ctx1[here, :], wo[1]) for here in spans]
    for here, x in zip(spans, xs):
        x = pre[here, :] + (x + shifts[0:1, :])
        center = x - row_mean(x)
        inv_one.append(lax.rsqrt(row_mean(center * center) + EPS_NORM))
        unit = center * inv_one[-1]
        pre[here, :] = unit
        nl[here, :] = (unit * gains[0:1, :] + shifts[2:3, :]).astype(bf16)
    for some in loads[1:]:
        for copy in some:
            copy.wait()
    rest = extra[...].astype(f32)
    ffb[1:2, :half] = split_sum(rest, 0)
    ffb[1:2, half:] = split_sum(rest, 3)

    order = [(i, ch) for ch in range(4) for i in range(parts)]

    def lift(i, ch):
        g, o = ch // 2, (ch % 2) * half
        return nn(nl[spans[i], :], up[g, :, o : o + half])

    later = lift(*order[0])
    branch = [shifts[1:2, :]] * parts
    for k, (i, ch) in enumerate(order):
        g, o = ch // 2, (ch % 2) * half
        z = later + ffb[g : g + 1, o : o + half]
        if k + 1 < len(order):
            later = lift(*order[k + 1])
        a, d = gelu_pair(z)
        a = a.astype(bf16)
        act[spans[i], ch * half : (ch + 1) * half] = a
        slope[spans[i], ch * half : (ch + 1) * half] = d.astype(bf16)
        branch[i] = branch[i] + nn(a, dn[g, o : o + half, :])
    total = []
    tops = [0.0] * 3
    for here, x in zip(spans, branch):
        y = pre[here, :] * gains[0:1, :] + shifts[2:3, :] + x
        center = y - row_mean(y)
        inv_two = lax.rsqrt(row_mean(center * center) + EPS_NORM)
        unit_two = center * inv_two
        out[here, :] = unit_two * gains[1:2, :] + shifts[3:4, :]
        c = cot[here, :]
        g2 = c * gains[1:2, :]
        gp2 = (g2 - row_mean(g2) - unit_two * row_mean(g2 * unit_two)) * inv_two
        low = gp2.astype(bf16)
        gb[here, :] = low
        tops = [t + col_sum(x) for t, x in zip(tops, (c * unit_two, c, low.astype(f32)))]
        total.append(gp2)
    sums[...] = jnp.zeros_like(sums)
    sums[1:2, :] = tops[0]
    sums[5:6, :] = tops[1]
    sums[3:4, :] = tops[2]

    def lower(i, ch):
        g, o = ch // 2, (ch % 2) * half
        return nt(gb[spans[i], :], dn[g, o : o + half, :])

    later = lower(*order[0])
    for k, (i, ch) in enumerate(order):
        g, o = ch // 2, (ch % 2) * half
        p = later * slope[spans[i], ch * half : (ch + 1) * half].astype(f32)
        if k + 1 < len(order):
            later = lower(*order[k + 1])
        p = p.astype(bf16)
        gpre[spans[i], ch * half : (ch + 1) * half] = p
        sums[6 + ch : 7 + ch, :] += col_sum(p.astype(f32))
        total[i] = total[i] + nt(p, up[g, :, o : o + half])
    tops = [0.0] * 3
    for here, x, inv in zip(spans, total, inv_one):
        unit_one = pre[here, :]
        g1 = x * gains[0:1, :]
        gp = (g1 - row_mean(g1) - unit_one * row_mean(g1 * unit_one)) * inv
        gp1[here, :] = gp
        low_one = gp.astype(bf16)
        ga[here, :] = low_one
        tops = [t + col_sum(v) for t, v in zip(tops, (x * unit_one, x, low_one.astype(f32)))]
    sums[0:1, :] = tops[0]
    sums[4:5, :] = tops[1]
    sums[2:3, :] = tops[2]
    ends = [
        pltpu.make_async_copy(a, b, row_sems.at[j])
        for j, (a, b) in enumerate(((ga, ga_far), (gp1, gp1_far), (out, out_far)))
    ] + [wo_copy]
    for copy in ends[:3]:
        copy.start()
    for i in range(rows // length):
        spot = pl.ds(10 + groups[info[3] + i], 1)
        sums[spot, :] += col_sum(gp1[i * length : (i + 1) * length, :])
    nl_t[...] = nl[...].astype(f32).T.astype(bf16)
    gb_t[...] = gb[...].astype(f32).T.astype(bf16)
    n = buf.shape[1] // 2
    for g, ctx in ((1, ctx1), (0, ctx0)):
        buf[g, 2 * hid : 2 * hid + cols, :] = nn(ctx[...].astype(f32).T.astype(bf16), ga[...]).astype(bf16)
        for ch in (2 * g, 2 * g + 1):
            o = (ch % 2) * half
            at = slice(ch * half, (ch + 1) * half)
            buf[g, o : o + half, :] = nn(nl_t[...], gpre[:, at]).astype(bf16)
            buf[g, hid + o : hid + o + half, :] = nn(gb_t[...], act[:, at]).astype(bf16)
        for dst, spot in ((send, 1 - core), (keep, core)):
            copy = pltpu.make_async_copy(
                buf.at[g, pl.ds(pl.multiple_of(spot * n, 32), n), :], dst.at[g], end_sems.at[2 * g + (dst is keep)]
            )
            copy.start()
            ends.append(copy)
    for copy in ends:
        copy.wait()


def attend_back(length, scale, g, info, groups, ga, emb_in, wo, picks, wq_in, k_in, v_in, att, picked, *refs):
    last = g == 0
    if last:
        sums, tsum_far, total_far, *refs = refs
    gq, gk, gv, keep, send, *refs = refs
    if not last:
        tsum, total_out, *refs = refs
    gq_all, gk_all, gv_all, emb_t, wq, buf, *refs = refs
    if last:
        tsum, small, *refs = refs
    (sems,) = refs
    core = info[0]
    step = pl.program_id(0)
    width, rows = emb_t.shape
    block = ga.shape[0]
    per = block // length
    cols = wq.shape[2]
    half = width // 2
    mask = head_mask(cols)
    mask_low = mask.astype(f32).astype(bf16)
    late = [
        pltpu.make_async_copy(a, b, sems.at[8 + i]) for i, (a, b) in enumerate(((emb_in, emb_t), (wq_in, wq)))
    ]

    @pl.when(step == 0)
    def _():
        for copy in late:
            copy.start()
        tsum[...] = jnp.zeros_like(tsum)

    start = (info[1] if last else 0) + step * per
    spots = [slice(i * length, (i + 1) * length) for i in range(per)]
    g_ctx = nt(ga[...], wo[g]).astype(bf16)
    hots = [one_hot(picks, start + i, length) for i in range(per)]
    ge = [nn(down, g_ctx[here, :]) for here, (_, down) in zip(spots, hots)]
    ge = [jnp.where(mask, x, 0.0).astype(bf16) for x in ge]
    active = [nn(up, mask_low) for up, _ in hots]
    gprobs = [nt(x, v_in[here, :]) for here, x in zip(spots, ge)]
    low_t = [att[i].T.astype(bf16) for i in range(per)]
    gmean = [
        col_sum((1.0 - x) * g_ctx[here, :].astype(f32)) * (1.0 / length) for here, x in zip(spots, active)
    ]
    g_value = [nn(x, y) for x, y in zip(low_t, ge)]
    weighted = [att[i] * x for i, x in enumerate(gprobs)]
    graw = [(x - att[i] * jnp.sum(x, axis=-1, keepdims=True)) * scale for i, x in enumerate(weighted)]
    gpick = [nn(x.astype(bf16), k_in[here, :]) for here, x in zip(spots, graw)]
    graw_t = [x.T.astype(bf16) for x in graw]
    g_value = [(x + m).astype(bf16) for x, m in zip(g_value, gmean)]
    gpick = [jnp.where(mask, x, 0.0).astype(bf16) for x in gpick]
    g_key = [nn(x, picked[i]).astype(bf16) for i, x in enumerate(graw_t)]
    g_query = [nn(up, x).astype(bf16) for (up, _), x in zip(hots, gpick)]
    for i, three in enumerate(zip(g_query, g_key, g_value)):
        rows_here = pl.ds(pl.multiple_of(step * block + i * length, 32), length)
        group = groups[info[3] + step * per + i]
        for j, (x, dst, dst_all) in enumerate(zip(three, (gq, gk, gv), (gq_all, gk_all, gv_all))):
            dst[spots[i], :] = x
            dst_all[rows_here, :] = x
            tsum[pl.ds(2 * j + group, 1), :] += col_sum(x.astype(f32))

    @pl.when(step == rows // block - 1)
    def _():
        for copy in late:
            copy.wait()
        n = 3 * half // 2
        pairs = []
        for j, x in enumerate((gq_all, gk_all, gv_all)):
            r = nn(emb_t[...], x[...]).astype(bf16)
            buf[j * half : (j + 1) * half, :cols] = r[:half]
            buf[j * half : (j + 1) * half, cols:] = r[half:]
        for dst, spot in ((send, 1 - core), (keep, core)):
            pairs.append((buf.at[at_row(spot * n, n), :], dst.at[pl.ds(0, n), :]))
        copies = copy_all(pairs, sems)
        total = jnp.zeros((8, width), f32)
        for j in range(3):
            x = tsum[2 * j : 2 * j + 8, :]
            hi = x.astype(bf16)
            lo = (x - hi.astype(f32)).astype(bf16)
            total = total + nt(hi, wq[j]) + nt(lo, wq[j])
        if last:
            total = total + total_far[...]
            small[...] = jnp.zeros_like(small)
            for m, t in enumerate((tsum, tsum_far)):
                at = 16 * m
                small[at : at + 2, :] = total[0:2] + sums[10:12, :]
                small[at + 2 : at + 8, :] = sums[0:6, :]
                small[at + 8 : at + 10, :] = sums[6 + 2 * m : 8 + 2 * m, :]
                small[at + 10 : at + 11, :cols] = t[0:1, :] + t[1:2, :]
                small[at + 10 : at + 11, cols:] = t[4:5, :] + t[5:6, :]
            buf[2 * n :, :] = small[...].astype(bf16)
            more = [
                pltpu.make_async_copy(buf.at[pl.ds(2 * n, 32), :], dst.at[pl.ds(n, 32), :], sems.at[2 + i])
                for i, dst in enumerate((send, keep))
            ]
            for copy in more:
                copy.start()
            copies += more
        else:
            total_out[...] = total
        for copy in copies:
            copy.wait()


def input_grad(*refs):
    (*grads, wq0, wq1, gp1, out) = refs
    total = gp1[...]
    for i, x in enumerate(grads):
        total = total + nt(x[...], (wq0, wq1)[i // 3][i % 3])
    out[...] = total


def hop(x, *bits):
    heads = lax.axis_size("head")
    flip = sum((1 << k) * (heads if axis == "dp" else 1) for axis, k in bits)
    count = lax.axis_size("dp") * heads
    return lax.ppermute(x, ("dp", "head"), [(i, i ^ flip) for i in range(count)])


def side(bit):
    axis, k = bit
    return (lax.axis_index(axis) >> k) & 1


def subsets(bits):
    return [[b for i, b in enumerate(bits) if (r >> i) & 1] for r in range(1 << len(bits))]


def pair_sum(terms):
    while len(terms) > 1:
        terms = [terms[i] + terms[i + 1] for i in range(0, len(terms), 2)]
    return terms[0]


def pick(x, bits, far, flips):
    for bit in bits:
        flipped = bit in flips
        if bit == far:
            x = x[1:] if flipped else x[:1]
        else:
            n = x.shape[1] // 2
            x = lax.dynamic_slice_in_dim(x, (side(bit) ^ int(flipped)) * n, n, 1)
    return x


def scatter_sum(x, bits, far, small=None):
    terms, rest = [], []
    for flips in subsets(bits):
        part = pick(x, bits, far, flips)
        if small is not None:
            part = jnp.concatenate([part, pick(small, [far] if far in bits else [], far, flips)], 1)
        if flips:
            part = hop(part, *flips)
        terms.append(part.astype(f32))
    total = pair_sum(terms).astype(bf16)
    if small is None:
        return total
    n = total.shape[1] - small.shape[1]
    return total[:, :n], total[:, n:]


def gather(x, bits):
    parts = {}
    for r, flips in enumerate(subsets(bits)):
        parts[r] = hop(x, *flips) if flips else x
    for i, bit in enumerate(bits):
        m = side(bit) == 0
        parts = {
            r: jnp.where(m, parts[r], parts[r ^ (1 << i)]) for r in parts
        }
    order = sorted(parts, key=lambda r: [(r >> i) & 1 for i in range(len(bits))])
    return jnp.concatenate([parts[r] for r in order], axis=0)


def plus(a, b):
    return (a.astype(f32) + b.astype(f32)).astype(bf16)


def late_steps(small_rows, bits, far, core):
    stages = [[far, bits[0]]] + [bits[i : i + 2] for i in range(1, len(bits), 2)]

    def cores(state):
        x = plus(state[0], hop(state[1], core))
        return x[:, :-small_rows], x[:, -small_rows:]

    def down(stage):
        return lambda state: scatter_sum(state[0], stage, far, state[1])

    def up(stage):
        wanted = [b for b in stage if b != far]

        def step(state):
            x = state[0] if state[0].ndim == 2 else state[0][0]
            return gather(x, wanted), state[1]

        return step

    return [cores] + [down(s) for s in stages] + [up(s) for s in reversed(stages)] + [up([core])]


def early_steps(bits, far, core):
    first, second, rest = bits[0], bits[1], bits[2:]
    orders = ((far, first, second), (first, second, far), (second, far, first))

    def start(x):
        part = x.shape[1] // 3
        return down(0)([x[:, i * part : (i + 1) * part] for i in range(3)])

    def down(stage):
        return lambda chunks: [scatter_sum(c, [order[stage]], far) for c, order in zip(chunks, orders)]

    def swap(chunks):
        x = jnp.concatenate(chunks, axis=2)[0]
        for bit in rest:
            x = plus(x, hop(x, bit))
        width = x.shape[1] // 3
        return [x[:, : 2 * width], x[:, 2 * width :]]

    def up_one(parts):
        return [gather(parts[0], [second]), gather(parts[1], [first])]

    def up_two(parts):
        two, one = gather(parts[0], [first]), gather(parts[1], [second])
        width = one.shape[1]
        return jnp.concatenate([two[:, :width], two[:, width:], one], axis=0)

    return [start, down(1), down(2), swap, up_one, up_two, lambda x: gather(x, [core])]


def add(a, b):
    return a.astype(f32) + b.astype(f32)


def at_row(start, n):
    return pl.ds(pl.multiple_of(start, 16), n)


def merge_cores(info, keep_in, got_in, stay0, far0, stay1, first1, stay2, second2, keep, got, sems, more_sems):
    n = keep.shape[1] // 3
    h = n // 2
    a, b = info[4], info[5]
    here = [pl.ds(i * n, n) for i in range(3)]
    loads = copy_all([(got_in.at[:, x, :], got.at[:, x, :]) for x in here], sems)
    more = copy_all([(keep_in.at[:, x, :], keep.at[:, x, :]) for x in here], more_sems)
    loads[0].wait()
    more[0].wait()
    stay0[...] = add(keep[0, :n], got[0, :n]).astype(bf16)
    far0[...] = add(keep[1, :n], got[1, :n]).astype(bf16)
    for base, bit, stay, send in ((n, a, stay1, first1), (2 * n, b, stay2, second2)):
        loads[base // n].wait()
        more[base // n].wait()
        for dst, m in ((stay, bit), (send, 1 - bit)):
            here = at_row(base + m * h, h)
            for g in range(2):
                dst[g] = add(keep[g, here], got[g, here]).astype(bf16)


def merge_two(info, stay0, got0, stay1, got1, stay2, got2, keep0, first0, keep1, second1, keep2, far2):
    a, b = info[4], info[5]
    h = stay0.shape[0] // 2
    for dst, m in ((keep0, a), (first0, 1 - a)):
        here = at_row(m * h, h)
        dst[...] = add(stay0[here], got0[here]).astype(bf16)
    q = stay1.shape[1] // 2
    for dst, m in ((keep1, b), (second1, 1 - b)):
        here = at_row(m * q, q)
        for g in range(2):
            dst[g] = add(stay1[g, here], got1[g, here]).astype(bf16)
    keep2[...] = add(stay2[0], got2[0]).astype(bf16)
    far2[...] = add(stay2[1], got2[1]).astype(bf16)


def merge_three(info, in0, got0, in1, got1, in2, got2, stay, to_second, to_far, to_first):
    a, b = info[4], info[5]
    q = to_far.shape[0]
    stay[:q] = add(in0[at_row(b * q, q)], got0[at_row(b * q, q)]).astype(bf16)
    to_second[...] = add(in0[at_row((1 - b) * q, q)], got0[at_row((1 - b) * q, q)]).astype(bf16)
    stay[q : 2 * q] = add(in1[0], got1[0]).astype(bf16)
    to_far[...] = add(in1[1], got1[1]).astype(bf16)
    stay[2 * q :] = add(in2[at_row(a * q, q)], got2[at_row(a * q, q)]).astype(bf16)
    to_first[...] = add(in2[at_row((1 - a) * q, q)], got2[at_row((1 - a) * q, q)]).astype(bf16)


def merge_four(info, stay, second, far, first, keep0, got0, keep1, got1, part, mine, to_first, to_far, to_both):
    q = second.shape[0]
    for i, x in enumerate((second, far, first)):
        part[i * q : (i + 1) * q] = add(stay[i * q : (i + 1) * q], x[...]).astype(bf16)
    a = info[4]
    h = mine.shape[0] - 16
    for dst, keep, got, g, m in (
        (mine, keep0, got0, 0, a), (to_first, keep0, got0, 0, 1 - a),
        (to_far, keep1, got1, 1, a), (to_both, keep1, got1, 1, 1 - a),
    ):
        here = at_row(m * h, h)
        tail = slice(2 * h + 16 * g, 2 * h + 16 * g + 16)
        dst[:h] = add(keep[here], got[here]).astype(bf16)
        dst[h:] = add(keep0[tail], got0[tail]).astype(bf16)


def merge_five(info, part, third, mine, first, far, both, own, to_second, to_first, total):
    q = part.shape[0] // 3
    to_second[: 2 * q] = add(part[: 2 * q], third[: 2 * q]).astype(bf16)
    to_first[...] = add(part[2 * q :], third[2 * q :]).astype(bf16)
    total[...] = (add(mine[...], first[...]) + add(far[...], both[...])).astype(bf16)
    n = own.shape[0] - 16
    for dst, base, m in ((own, 0, info[5]), (to_second, 2 * q, 1 - info[5])):
        dst[base : base + n] = total[at_row(m * n, n)]
        dst[base + n : base + n + 16] = total[2 * n :]


def merge_six(info, near2, got2, near1, got1, own, to_first, to_second, to_third):
    a, b = info[4], info[5]
    q = near1.shape[0]
    for c in range(2):
        to_first[at_row(2 * c * q + b * q, q)] = near2[c * q : (c + 1) * q]
        to_first[at_row(2 * c * q + (1 - b) * q, q)] = got2[c * q : (c + 1) * q]
    to_second[at_row(a * q, q)] = near1[...]
    to_second[at_row((1 - a) * q, q)] = got1[...]
    to_third[...] = add(own[...], got2[2 * q :]).astype(bf16)


def merge_seven(info, near1, got1, near2, got2, near3, got3, out, two, table, gains, shifts, ff, bias):
    a, b = info[4], info[5]
    h = near1.shape[0] // 2
    for c in range(2):
        out[at_row(2 * c * h + a * h, h)] = near1[c * h : (c + 1) * h]
        out[at_row(2 * c * h + (1 - a) * h, h)] = got1[c * h : (c + 1) * h]
    out[at_row(4 * h + b * h, h)] = near2[...]
    out[at_row(4 * h + (1 - b) * h, h)] = got2[...]
    n = two.shape[0]
    s = add(near3[...], got3[...])
    two[...] = s[:n].astype(bf16)
    s = s[n:]
    width = s.shape[1]
    table[...] = s[0:2]
    gains[...] = s[2:4]
    shifts[...] = s[4:8]
    ff[:, :width] = s[8:9]
    ff[:, width:] = s[9:10]
    bias[0:1] = s[10:11, : width // 2]
    bias[1:2] = s[10:11, width // 2 :]


def merge_eight(info, near, first, second, both, out):
    n = near.shape[0]
    a, b = info[4], info[5]
    for x, i, j in ((near, a, b), (first, 1 - a, b), (second, a, 1 - b), (both, 1 - a, 1 - b)):
        out[at_row(2 * n * i + n * j, n)] = x[...]


def merge(body, info, ins, outs, width, with_info=True):
    shapes = [(s if isinstance(s, tuple) else (s, width), bf16, VMEM) for s in outs]
    return call(
        body,
        shapes,
        [SMEM] * with_info + [VMEM] * len(ins),
        ((info,) if with_info else ()) + tuple(ins),
        [],
        24,
        2 * US,
        2e6,
        hbm_in=False,
        hbm_out=False,
    )


def sum_start(info, keep, send, bits, far, core):
    first, second, _ = bits
    width = keep.shape[2]
    n = keep.shape[1] // 3
    two = (2, n // 2, width)
    stay0, far0, stay1, first1, stay2, second2 = call(
        merge_cores,
        [(x, bf16, VMEM) for x in ((n, width), (n, width), two, two, two, two)],
        [SMEM, FAR, HBM],
        (info, keep, hop(send, core)),
        [pltpu.VMEM(keep.shape, bf16)] * 2 + [pltpu.SemaphoreType.DMA((3,))] * 2,
        24,
        2 * US,
        2e6,
        hbm_out=False,
    )
    return (stay0, hop(far0, far), stay1, hop(first1, first), stay2, hop(second2, second))


def sum_middle(info, state, bits, far, width):
    first, second, _ = bits
    n = state[0].shape[0]
    q = n // 4
    keep0, first0, keep1, second1, keep2, far2 = merge(
        merge_two, info, state, (n // 2, n // 2, (2, q, width), (2, q, width), n // 2, n // 2), width
    )
    return (keep0, hop(first0, first), keep1, hop(second1, second), keep2, hop(far2, far))


def sum_finish(info, state, late, bits, far, core, beside):
    first, second, third = bits
    width = state[0].shape[1]
    q = state[0].shape[0] // 2
    keep0, send0, keep1, got1 = late
    stay, to_second, to_far, to_first = merge(merge_three, info, state, (3 * q, q, q, q), width)
    send0, stay = lax.optimization_barrier((send0, stay))
    got0 = hop(send0, core)
    h = keep1.shape[0] // 2
    part, mine, to_first, to_far, to_both = merge(
        merge_four,
        info,
        (stay, hop(to_second, second), hop(to_far, far), hop(to_first, first), keep0, got0, keep1, got1),
        (3 * q, h + 16, h + 16, h + 16, h + 16),
        width,
    )
    rows = beside[0](part)
    got = hop(part, third), hop(to_first, first), hop(to_far, far), hop(to_both, first, far)
    part, rows = lax.optimization_barrier((part, rows))
    m = h // 2
    own, to_second, to_first, _ = merge(
        merge_five, info, (part, got[0], mine, *got[1:]), (m + 16, 2 * q + m + 16, q, h + 16), width
    )
    blanks_one = beside[1](own)
    got = hop(to_second, second), hop(to_first, first)
    own, blanks_one[0] = lax.optimization_barrier((own, blanks_one[0]))
    to_first, to_second, to_third = merge(
        merge_six, info, (to_second, got[0], to_first, got[1], own), (4 * q, 2 * q, m + 16), width
    )
    blanks_two = beside[2](to_third)
    got = hop(to_first, first), hop(to_second, second), hop(to_third, third)
    to_first, blanks_two[0] = lax.optimization_barrier((to_first, blanks_two[0]))
    one, two, *small = call(
        merge_seven,
        [((12 * q, width), bf16, VMEM), ((m, width), bf16, VMEM)]
        + [(shape, f32, VMEM) for shape in ((2, width), (2, width), (4, width), (1, 2 * width), (2, width // 2))],
        [SMEM] + [VMEM] * 6,
        (info, to_first, got[0], to_second, got[1], to_third, got[2]),
        [],
        24,
        2 * US,
        2e6,
        hbm_in=False,
        hbm_out=False,
    )
    other = hop(one, core)
    got = hop(two, first), hop(two, second), hop(two, first, second)
    blanks_three = beside[3](two)
    two, blanks_three[0] = lax.optimization_barrier((two, blanks_three[0]))
    (two,) = merge(merge_eight, info, (two, *got), (4 * m,), width)
    return (one, other), (two, hop(two, core)), small, (rows, blanks_two + blanks_one + blanks_three)


def wipe(*refs):
    sems = refs[-1]
    count = sems.shape[0]
    outs, zeros = refs[1 : 1 + count], refs[1 + count : -1]
    for zero in zeros:
        zero[...] = jnp.zeros_like(zero)
    copies = []
    for i, out in enumerate(outs):
        src = next(z for z in zeros if z.dtype == out.dtype and z.shape[1] == out.shape[1])
        rows = out.shape[0]
        n = next(c for c in (256, 192, 128, 64, 32, 16) if rows % c == 0)
        for at in range(0, rows, n):
            copies.append(
                pltpu.make_async_copy(
                    src.at[pl.ds(0, n), :], out.at[pl.ds(at, n), :], sems.at[i]
                )
            )
    for copy in copies:
        copy.start()
    for copy in copies:
        copy.wait()


def blanks_for(gate, likes):
    flat = [(math.prod(x.shape[:-1]), x.shape[-1]) for x in likes]
    widths = sorted({n for _, n in flat})
    outs = call(
        wipe,
        [(s, x.dtype, HBM) for s, x in zip(flat, likes)],
        [HBM],
        (gate,),
        [pltpu.VMEM((256, n), k) for n in widths for k in (f32, bf16)]
        + [pltpu.SemaphoreType.DMA((len(likes),))],
        8,
        US // 2,
        1e6,
        hbm_in=False,
    )
    return [x.reshape(like.shape) for x, like in zip(outs, likes)]


def moments(turned, m, v):
    first = BETA_ONE * m[...] + (1.0 - BETA_ONE) * turned
    second = BETA_TWO * v[...] + (1.0 - BETA_TWO) * (turned * turned)
    m[...] = first
    v[...] = second
    return (first / (jnp.sqrt(second) + EPS_ADAM)).astype(bf16)


def fetch(pairs, sems):
    for copy in copy_all(pairs, sems):
        copy.wait()


def step_wide(g, w, m, v, ql, qr, rate, scratch, ready):
    low_l, low_r, mid, back = scratch
    low_l[...] = ql[...].astype(bf16)
    low_r[...] = qr[...].astype(bf16)
    blocks, size = qr.shape[0], qr.shape[1]
    mid[...] = nn(ql[...].T.astype(bf16), g).astype(bf16)
    for b in range(blocks):
        at = slice(b * size, (b + 1) * size)
        u = moments(nn(mid[:, at], low_r[b]), m.at[:, at], v.at[:, at])
        back[:, at] = nt(u, low_r[b]).astype(bf16)
    ready()
    w[...] = w[...] - rate * nn(low_l[...], back[...])


def step_tall(g, w, m, v, ql, qr, rate, scratch, ready):
    low_r, mid, back = scratch
    low_r[...] = qr[...].astype(bf16)
    blocks, size = ql.shape[0], ql.shape[1]
    for b in range(blocks):
        at = slice(b * size, (b + 1) * size)
        mid[at, :] = nn(ql[b].T.astype(bf16), g[at, :]).astype(bf16)
    u = moments(nn(mid[...], low_r[...]), m, v)
    ready()
    back[...] = nt(u, low_r[...]).astype(bf16)
    for b in range(blocks):
        at = slice(b * size, (b + 1) * size)
        w[at, :] = w[at, :] - rate * nn(ql[b].astype(bf16), back[at, :])


def update_qkv(rate, mine, g, w_in, m_in, v_in, ql_in, qr_in, *refs):
    outs, (grad, new, mom, var, copy) = refs[:4], refs[4:9]
    w, m, v, c, ql, qr, low_l, low_r, mid, back, sems = refs[9:]
    for j in range(3):
        grad[j] = g[j].astype(f32)

        @pl.when(mine[j] == 1)
        def _():
            fetch(
                [(w_in.at[j], w), (m_in.at[j], m), (v_in.at[j], v), (ql_in.at[j], ql), (qr_in.at[j], qr)], sems
            )
            step_wide(g[j], w, m, v, ql, qr, rate, (low_l, low_r, mid, back), lambda: None)
            c[...] = w[...].astype(bf16)
            fetch([(w, new.at[j]), (m, mom.at[j]), (v, var.at[j]), (c, copy.at[j])], sems)


def update_rest(rate_out, rate_up, rate_down, mine, g_out, g_up, g_down_t, *refs):
    (wo_in, mo_in, vo_in, lo_in, ro_in, wu_in, mu_in, vu_in, lu_in, ru_in,
     wd_in, md_in, vd_in, ld_in, rd_in) = refs[:15]
    refs = refs[15 + 11 :]
    grad_o, grad_u, grad_d = refs[:3]
    new_o, moments_o, copy_o, new_u, mom_u, var_u, copy_u, new_d, mom_d, var_d, copy_d = refs[3:14]
    (wo, mo, vo, co, lo, ro, low_ro, mid_o, back_o,
     wu, mu, vu, cu, lu, ru, low_lu, low_ru, mid_u, back_u,
     wd, md, vd, cd, mid_d, back_d, sems) = refs[14:]
    grad_o[...] = g_out[...].astype(f32)
    grad_u[...] = g_up[...].astype(f32)
    grad_d[...] = g_down_t[...].astype(f32).T

    @pl.when(mine[3] == 1)
    def _():
        fetch([(wo_in, wo), (mo_in, mo), (vo_in, vo), (lo_in, lo), (ro_in, ro)], sems)
        step_tall(g_out[...], wo, mo, vo, lo, ro, rate_out, (low_ro, mid_o, back_o), lambda: None)
        co[...] = wo[...].astype(bf16)
        fetch([(wo, new_o), (mo, moments_o.at[0]), (vo, moments_o.at[1]), (co, copy_o)], sems)

    @pl.when(mine[4] == 1)
    def _():
        fetch([(wu_in, wu), (mu_in, mu), (vu_in, vu), (lu_in, lu), (ru_in, ru)], sems)
        step_wide(g_up[...], wu, mu, vu, lu, ru, rate_up, (low_lu, low_ru, mid_u, back_u), lambda: None)
        cu[...] = wu[...].astype(bf16)
        fetch([(wu, new_u), (mu, mom_u), (vu, var_u), (cu, copy_u)], sems)

    @pl.when(mine[5] == 1)
    def _():
        fetch([(wd_in, wd), (md_in, md), (vd_in, vd), (ld_in, ru), (rd_in, lu)], sems)
        step_tall(grad_d[...].astype(bf16), wd, md, vd, ru, lu, rate_down, (low_lu, mid_d, back_d), lambda: None)
        cd[...] = wd[...].astype(bf16)
        fetch([(wd, new_d), (md, mom_d), (vd, var_d), (cd, copy_d)], sems)


def update_all(rate_out, rate_wide, rate_down, cols, hid, owned, info, mine, other, mine_q, other_q, *refs):
    ins, refs = refs[:20], refs[20 + 15 :]
    grad_q, grad_o, grad_u, grad_d = refs[:4]
    outs, held, refs = refs[4:19], refs[19:39], refs[39:]
    wq, mq, vq, lq, rq, wo, mo, vo, lo, ro, wu, mu, vu, lu, ru, wd, md, vd, ld, rd = held
    new_q, mom_q, var_q, copy_q, new_o, mom_o, copy_o, new_u, mom_u, var_u, copy_u, new_d, mom_d, var_d, copy_d = outs
    buf, buf_q, gq, go, gu, gd, cq, co, cu, cd = refs[:10]
    low_l, low_r64, low_r256, mid_q, mid_o, mid_u, mid_d, back_q, back_o, back_u, back_d = refs[10:21]
    sems, in_sems, out_sems = refs[21:]
    core = info[0]
    loads = []
    for k in (4, 5, 3, 0, 1, 2):
        base = 5 * max(k - 2, 0)
        some = [(a.at[k], b.at[k]) if k < 3 else (a, b) for a, b in zip(ins[base : base + 5], held[base : base + 5])]
        some = [pltpu.make_async_copy(a, b, in_sems.at[k, i]) for i, (a, b) in enumerate(some)]
        loads.append((k, some))

        @pl.when(owned[k] == 1)
        def _(some=some):
            for copy in some:
                copy.start()

    loads = dict(loads)
    width = buf.shape[1]
    half = width // 2
    n = mine.shape[0]
    n_q = mine_q.shape[0]
    fills = copy_all(
        [(mine, buf.at[at_row(core * n, n)]), (other, buf.at[at_row((1 - core) * n, n)]),
         (mine_q, buf_q.at[at_row(core * n_q, n_q)]), (other_q, buf_q.at[at_row((1 - core) * n_q, n_q)])],
        sems,
    )
    pending = []

    def give(scratch, out, k):
        copy = pltpu.make_async_copy(scratch, out, sems.at[4 + k])
        copy.start()
        pending.append((None, copy))

    def finish(k, w, m, v, c, outs, run):
        stores = [
            pltpu.make_async_copy(a, b, out_sems.at[k, i]) for i, (a, b) in enumerate(zip((w, m, v, c), outs))
        ]

        @pl.when(owned[k] == 1)
        def _():
            for copy in loads[k]:
                copy.wait()

            def ready():
                stores[1].start()
                stores[2].start()

            run(ready)
            stores[0].start()
            c[...] = w[...].astype(bf16)
            stores[3].start()

        pending.extend((owned[k] == 1, copy) for copy in stores)

    fills[0].wait()
    fills[1].wait()
    h = hid // 2
    for i in range(2):
        gu[:, i * h : (i + 1) * h] = buf[i * width : (i + 1) * width, :].astype(f32)
    give(gu, grad_u, 0)
    finish(4, wu, mu, vu, cu, (new_u, mom_u, var_u, copy_u),
           lambda ready: step_wide(gu[...].astype(bf16), wu, mu, vu, lu, ru, rate_wide,
                                   (low_l, low_r256, mid_u, back_u), ready))
    for i in range(2):
        gd[i * h : (i + 1) * h, :] = buf[hid + i * width : hid + (i + 1) * width, :].astype(f32).T
    give(gd, grad_d, 1)
    finish(5, wd, md, vd, cd, (new_d, mom_d, var_d, copy_d),
           lambda ready: step_tall(gd[...].astype(bf16), wd, md, vd, ld, rd, rate_down,
                                   (low_l, mid_d, back_d), ready))
    go[...] = buf[2 * hid : 2 * hid + cols, :].astype(f32)
    give(go, grad_o, 2)
    finish(3, wo, mo, vo, co, (new_o, mom_o.at[0], mom_o.at[1], copy_o),
           lambda ready: step_tall(go[...].astype(bf16), wo, mo, vo, lo, ro, rate_out,
                                   (low_l, mid_o, back_o), ready))
    fills[2].wait()
    fills[3].wait()
    for j in range(3):
        x = buf_q[j * half : (j + 1) * half, :].astype(f32)
        gq[j, :half, :] = x[:, :cols]
        gq[j, half:, :] = x[:, cols:]
        give(gq.at[j], grad_q.at[j], 3 + j)
        finish(j, wq.at[j], mq.at[j], vq.at[j], cq.at[j], [x.at[j] for x in (new_q, mom_q, var_q, copy_q)],
               lambda ready, j=j: step_wide(gq[j].astype(bf16), wq.at[j], mq.at[j], vq.at[j], lq.at[j], rq.at[j],
                                            rate_wide, (low_l, low_r64, mid_q, back_q), ready))
    for flag, copy in pending:
        if flag is None:
            copy.wait()
        else:

            @pl.when(flag)
            def _(copy=copy):
                copy.wait()


def pad_picks(picks):
    windows, heads, slots = picks.shape
    return jnp.pad(picks, ((0, 0), (0, 0), (0, SLOTS - slots)), constant_values=-1).reshape(
        windows, heads * SLOTS
    )


def per_device(
    tokens_in,
    cotangent,
    data_table,
    window_group,
    query_picks,
    owner_list,
    weight_qkv,
    head_bias,
    weight_out,
    weight_up,
    ff_bias,
    weight_down,
    norm_gains,
    shifts,
    first_qkv,
    second_qkv,
    first_out,
    second_out,
    first_up,
    second_up,
    first_down,
    second_down,
    basis_qkv_left,
    basis_qkv_right,
    basis_out_left,
    basis_out_right,
    basis_up_left,
    basis_up_right,
    basis_down_left,
    basis_down_right,
):
    head_count = lax.axis_size("head")
    head = lax.axis_index("head")
    my_rank = lax.axis_index("dp")
    rows, width = tokens_in.shape
    length = rows * head_count // window_group.shape[0]
    windows = rows // length
    head_dim = basis_qkv_right.shape[-1]
    cols = GROUP * head_dim
    scale = 1.0 / math.sqrt(head_dim)
    head_bits = head_count.bit_length() - 1
    far = ("head", head_bits - 1)
    core_bit = ("dp", 0)
    dp_bits = lax.axis_size("dp").bit_length() - 1
    bits = [("dp", k) for k in range(1, dp_bits)] + [("head", k) for k in range(head_bits - 1)]
    core = my_rank & 1
    quarter = my_rank & 3
    second_bit = ("dp", 1)
    slots = GROUP * SLOTS
    half = width // 2

    if head_count == 2:
        n_qkv, n_bias, n_out, n_up, n_ff, n_down = (
            weight_qkv, head_bias, weight_out, weight_up, ff_bias, weight_down
        )
        picks = pad_picks(query_picks).astype(f32)
        near_at, far_at = head * windows, (1 - head) * windows
    else:
        def whole_of(x, dim):
            return lax.all_gather(x, "head", axis=dim, tiled=True)

        def pick_group(x, dim, g):
            n = x.shape[dim] // 2
            return lax.dynamic_slice_in_dim(x, (side(far) ^ g) * n, n, dim)

        both = [
            (whole_of(weight_qkv.astype(bf16), 2).astype(f32), 2),
            (whole_of(head_bias, 1), 1),
            (whole_of(weight_out.astype(bf16), 0).astype(f32), 0),
            (whole_of(weight_up.astype(bf16), 1).astype(f32), 1),
            (whole_of(ff_bias, 0), 0),
            (whole_of(weight_down.astype(bf16), 0).astype(f32), 0),
        ]
        n_qkv, n_bias, n_out, n_up, n_ff, n_down = (pick_group(x, d, 0) for x, d in both)
        away = [pick_group(x, d, 1) for x, d in both]
        picks = lax.dynamic_slice_in_dim(whole_of(query_picks, 1), head * windows, windows, 0)
        picks = jnp.concatenate([pad_picks(pick_group(picks, 1, g)) for g in range(2)]).astype(f32)
        near_at, far_at = jnp.int32(0), jnp.int32(windows)
    info = jnp.stack([core, near_at, far_at, head * windows] + [side(b) for b in bits[:3]] + [quarter]).astype(jnp.int32)
    quick = head_count == 2 and len(bits) == 3
    hid = n_up.shape[1]
    extra_rows = -(-(windows + 6) // 16) * 16
    buf_rows = 2 * hid + cols
    rest_rows = cols // 4 + width // 2 + 16

    def send_qkv(info, w, bias):
        return call(
            lambda *refs: pack_qkv(windows, *refs),
            [((3 * width // 4 + extra_rows, cols), bf16, VMEM)],
            [SMEM, FAR, FAR, HBM],
            (info, w, bias, picks),
            [
                pltpu.VMEM((3, width // 4, cols), f32),
                pltpu.VMEM((extra_rows, cols), f32),
                pltpu.VMEM(bias.shape, f32),
                pltpu.VMEM(picks.shape, f32),
                pltpu.SemaphoreType.DMA((5,)),
            ],
            12,
            2 * US,
            3e6,
            hbm_out=False,
        )

    def send_rest(info, w_out, w_up, w_down, bias):
        return call(
            pack_rest,
            [
                ((rest_rows, width), bf16, VMEM),
                ((hid // 4, width), bf16, VMEM),
                ((cols, width), bf16, VMEM),
                ((width, hid), bf16, VMEM),
                ((hid, width), bf16, VMEM),
            ],
            [SMEM, VMEM, VMEM, VMEM, VMEM],
            (info, w_out, w_up, w_down, bias[None]),
            [pltpu.VMEM((16, width), f32)],
            24,
            4 * US,
            8e6,
            hbm_in=False,
            hbm_out=False,
        )

    (qkv_piece,) = send_qkv(info, n_qkv, n_bias)
    if head_count == 2:
        qkv_y = hop(qkv_piece, far)
        rest_piece, down_piece, *near_low = send_rest(info, n_out, n_up, n_down, n_ff)
    else:
        near_low = send_rest(info, n_out, n_up, n_down, n_ff)[2:]
        others = [info.at[7].set(quarter ^ i) for i in range(4)]
        qkv_all = [send_qkv(m, away[0], away[1])[0] for m in others]
        rest_all, down_all = zip(*(send_rest(m, away[2], away[3], away[5], away[4])[:2] for m in others))

    block = 2 * length
    steps = (rows // block,)
    wide = windows
    wide_block, wide_steps = wide * length, (windows // wide,)
    back_wide = 4 if windows % 4 == 0 else 2
    back_block, back_steps = back_wide * length, (windows // back_wide,)
    seen = [
        ((rows, cols), bf16, cut(wide_block, cols)),
        ((rows, cols), bf16, cut(wide_block, cols)),
        ((rows, cols), bf16, cut(wide_block, cols)),
        ((rows, cols), bf16, cut(wide_block, cols)),
        ((windows, slots, length), f32, cut(wide, slots, length)),
        ((windows, slots, cols), bf16, cut(wide, slots, cols)),
    ]
    q0, k0, v0, ctx0, att0, picked0, emb, emb_t, wq0 = call(
        lambda *refs: attend_own(length, scale, *refs),
        seen
        + [
            ((rows, width), bf16, cut(wide_block, width)),
            ((width, rows), bf16, pl.BlockSpec((width, wide_block), lambda i: (0, i))),
            ((3, width, cols), bf16, whole(3, width, cols)),
        ],
        [SMEM, SMEM, cut(wide_block, width), whole(NDATA, width), whole(3, width, cols),
         whole(2, cols), whole(*picks.shape)],
        (info, window_group, tokens_in, data_table, n_qkv, n_bias, picks),
        [],
        24,
        9 * US,
        6e6,
        grid=wide_steps,
        hbm_in=False,
    )
    if head_count == 2:

        def spread(x):
            across = hop(x, second_bit)
            return [x, hop(x, core_bit), across, hop(across, core_bit)]

        rest_y = hop(rest_piece, far)
        qkv_y, ctx0, near_low[0] = lax.optimization_barrier((qkv_y, ctx0, near_low[0]))
        qkv_all = spread(qkv_y)
        rest_y, emb, down_piece = lax.optimization_barrier((rest_y, emb, down_piece))
        down_y = hop(down_piece, far)
        rest_all = spread(rest_y)
    q1, k1, v1, ctx1, att1, picked1, wq1, picks1 = call(
        lambda *refs: attend_far(length, scale, *refs),
        seen + [((3, width, cols), bf16, whole(3, width, cols)), ((windows, slots), f32, whole(windows, slots))],
        [SMEM, cut(wide_block, width)] + [HBM] * 4,
        (info, emb, *qkv_all),
        [
            pltpu.VMEM((extra_rows, cols), bf16),
            pltpu.VMEM((2, cols), f32),
            pltpu.SemaphoreType.DMA((13,)),
        ],
        24,
        9 * US,
        6e6,
        grid=wide_steps,
        hbm_in=False,
    )
    if head_count == 2:
        down_y, ctx1 = lax.optimization_barrier((down_y, ctx1))
        down_all = spread(down_y)

    def kinds(x):
        return [jax.ShapeDtypeStruct(x.shape, k) for k in (f32, f32, f32, bf16)]

    few = kinds(first_qkv) + [
        jax.ShapeDtypeStruct(first_out.shape, f32),
        jax.ShapeDtypeStruct((2,) + first_out.shape, f32),
        jax.ShapeDtypeStruct(first_out.shape, bf16),
    ]
    many = kinds(first_up) + kinds(first_down)

    def make_few(gate):
        return blanks_for(gate, few)

    def make_many(gate):
        return blanks_for(gate, many)

    def make_input_grad(gp1):
        return call(
            input_grad,
            [((rows, width), f32, cut(block, width))],
            [cut(block, cols)] * 6 + [whole(3, width, cols)] * 2 + [cut(block, width)],
            (gq0, gk0, gv0, gq1, gk1, gv1, wq0, wq1, gp1),
            [],
            24,
            US // 2,
            1e6,
            grid=steps,
        )[0]

    parts = 2 if windows % 4 == 0 else 1
    output_rows, gp1, ga, keep_one, send_one, sums, wo = call(
        lambda *refs: feed_forward(length, parts, *refs),
        [
            ((rows, width), f32, HBM),
            ((rows, width), f32, HBM),
            ((rows, width), bf16, HBM),
            ((2, buf_rows // 2, width), bf16, HBM),
            ((2, buf_rows // 2, width), bf16, HBM),
            ((16, width), f32, VMEM),
            ((2, cols, width), bf16, HBM),
        ],
        [SMEM, SMEM, VMEM, VMEM, VMEM, VMEM] + [HBM] * 11 + [VMEM, VMEM, VMEM, HBM],
        (info, window_group, tokens_in, data_table, ctx0, ctx1, *near_low, *rest_all, *down_all,
         n_ff[None], norm_gains, shifts, cotangent),
        [
            pltpu.VMEM((2, cols, width), bf16),
            pltpu.VMEM((2, width, hid), bf16),
            pltpu.VMEM((2, hid, width), bf16),
            pltpu.VMEM((rows, 2 * hid), bf16),
            pltpu.VMEM((rows, 2 * hid), bf16),
            pltpu.VMEM((rows, 2 * hid), bf16),
            pltpu.VMEM((rows, width), bf16),
            pltpu.VMEM((rows, width), bf16),
            pltpu.VMEM((rows, width), bf16),
            pltpu.VMEM((rows, width), f32),
            pltpu.VMEM((rows, width), f32),
            pltpu.VMEM((rows, width), f32),
            pltpu.VMEM((rows, width), f32),
            pltpu.VMEM((width, rows), bf16),
            pltpu.VMEM((width, rows), bf16),
            pltpu.VMEM((2, hid), f32),
            pltpu.VMEM((16, width), bf16),
            pltpu.VMEM((2, buf_rows, width), bf16),
            pltpu.SemaphoreType.DMA((21,)),
            pltpu.SemaphoreType.DMA((3,)),
            pltpu.SemaphoreType.DMA((5,)),
        ],
        50,
        24 * US,
        20e6,
    )
    if quick:
        state_one = sum_start(info, keep_one, send_one, bits, far, core_bit)
        ga, held = lax.optimization_barrier((ga, state_one[0]))
        state_one = (held, *state_one[1:])
    else:
        sum_one = plus(keep_one, hop(send_one, core_bit))
        sum_one, ga = lax.optimization_barrier((sum_one, ga))

    def make_back(g, ga, picks, wq, k, v, att, picked, extra_in):
        last = g == 0
        n = 3 * half // 2 + 32 * last
        more = [((16, cols), f32, whole(16, cols)), ((8, width), f32, whole(8, width))]
        return call(
            lambda *refs: attend_back(length, scale, g, *refs),
            [((rows, cols), bf16, cut(back_block, cols))] * 3
            + [((n, width), bf16, HBM)] * 2
            + ([] if last else more),
            [SMEM, SMEM, cut(back_block, width), FAR, whole(2, cols, width), whole(*picks.shape), FAR,
             cut(back_block, cols), cut(back_block, cols), cut(back_wide, slots, length), cut(back_wide, slots, cols)]
            + [whole(*x.shape) for x in extra_in],
            (info, window_group, ga, emb_t, wo, picks, wq, k, v, att, picked, *extra_in),
            [pltpu.VMEM((rows, cols), bf16)] * 3
            + [
                pltpu.VMEM((width, rows), bf16),
                pltpu.VMEM((3, width, cols), bf16),
                pltpu.VMEM((3 * half + 32 * last, width), bf16),
            ]
            + ([pltpu.VMEM((16, cols), f32), pltpu.VMEM((32, width), f32)] if last else [])
            + [pltpu.SemaphoreType.DMA((10,))],
            32,
            6 * US,
            8e6,
            grid=back_steps,
        )

    gq1, gk1, gv1, keep_far, send_far, tsum, table_far = make_back(
        1, ga, picks1, wq1, k1, v1, att1, picked1, ()
    )
    if quick:
        held, keep_far, send_far = lax.optimization_barrier((state_one[0], keep_far, send_far))
        state_one = sum_middle(info, (held, *state_one[1:]), bits, far, width)
        held, ga, send_far = lax.optimization_barrier((state_one[0], ga, send_far))
        state_one = (held, *state_one[1:])
        got_far = hop(send_far, core_bit)
    gq0, gk0, gv0, keep_near, send_near = make_back(
        0, ga, picks, wq0, k0, v0, att0, picked0, (sums, tsum, table_far)
    )

    shards = head_count // 2
    mine = head % shards

    def shard(x, dim):
        n = x.shape[dim] // shards
        return x if shards == 1 else lax.dynamic_slice_in_dim(x, mine * n, n, dim)

    owned = (owner_list == my_rank).astype(jnp.int32)

    rate_wide = width ** (-0.5)
    rate_out = max(width // head_dim, 1) ** (-0.5)
    rate_down = (n_down.shape[0] * 2) ** (-0.5)
    moments_in = (
        weight_qkv, first_qkv, second_qkv, basis_qkv_left, basis_qkv_right,
        weight_out, first_out, second_out, basis_out_left, basis_out_right,
        weight_up, first_up, second_up, basis_up_left, basis_up_right,
        weight_down, first_down, second_down, basis_down_left, basis_down_right,
    )
    if quick:
        held, keep_near, send_near = lax.optimization_barrier((state_one[0], keep_near, send_near))
        beside = (
            lambda gate: make_input_grad(lax.optimization_barrier((gp1, gate))[0]),
            lambda gate: blanks_for(gate, kinds(first_up)),
            make_few,
            lambda gate: blanks_for(gate, kinds(first_down)),
        )
        pieces_one, pieces_two, small, (grad_rows, blanks) = sum_finish(
            info, (held, *state_one[1:]), (keep_near, send_near, keep_far, got_far), bits, far, core_bit, beside
        )
        likes = [first_qkv, first_out, first_up, first_down]
        temps = [first_qkv.shape[1:], first_out.shape, first_up.shape, first_down.shape]
        outs = call(
            lambda *refs: update_all(rate_out, rate_wide, rate_down, cols, hid, *refs),
            [(x.shape, f32, HBM) for x in likes] + [(x.shape, x.dtype, HBM) for x in blanks],
            [SMEM, SMEM] + [HBM] * 4 + [FAR] * 35,
            (owned, info, *pieces_one, *pieces_two, *moments_in, *blanks),
            [pltpu.VMEM(x.shape, f32) for x in moments_in]
            + [pltpu.VMEM((buf_rows, width), bf16), pltpu.VMEM((3 * half, width), bf16)]
            + [pltpu.VMEM(x.shape, f32) for x in likes]
            + [pltpu.VMEM(x.shape, bf16) for x in likes]
            + [
                pltpu.VMEM((width, width), bf16),
                pltpu.VMEM(basis_qkv_right.shape[1:], bf16),
                pltpu.VMEM(basis_up_right.shape, bf16),
            ]
            + [pltpu.VMEM(x, bf16) for x in temps * 2]
            + [
                pltpu.SemaphoreType.DMA((10,)),
                pltpu.SemaphoreType.DMA((6, 5)),
                pltpu.SemaphoreType.DMA((6, 4)),
            ],
            49,
            12 * US,
            30e6,
            {26 + i: 4 + i for i in range(15)},
        )
        grad_qkv_all, grad_out_all, grad_up_all, grad_down_all = outs[:4]
        qkv_outs, rest_outs = outs[3:8], outs[5:19]
        grad_table_all, grad_gains_all, grad_shifts_all, grad_ff_all, grad_bias_all = small
        grad_ff_all = grad_ff_all.reshape(-1)
    else:
        grad_rows = make_input_grad(gp1)
        n = 3 * half // 2
        keep_two, send_two = (
            jnp.stack([near[: n + 16], jnp.concatenate([away_part, near[n + 16 :]])])
            for near, away_part in ((keep_near, keep_far), (send_near, send_far))
        )
        blanks = make_few(sums) + make_many(sums)
        early, late = early_steps(bits, far, core_bit), late_steps(16, bits, far, core_bit)
        state_one, state_two = early[0](sum_one), (keep_two, send_two)
        for i in range(1, max(len(early), len(late) + 1)):
            state_one, state_two = lax.optimization_barrier((state_one, state_two))
            if i < len(early):
                state_one = early[i](state_one)
            if i <= len(late):
                state_two = late[i - 1](state_two)
        sum_one, (sum_two, small) = state_one, state_two
        small = small[0]
        g_up = shard(jnp.concatenate([sum_one[:width], sum_one[width : 2 * width]], 1), 1)
        g_down_t = shard(
            jnp.concatenate([sum_one[2 * width : 3 * width], sum_one[3 * width : 4 * width]], 1), 1
        )
        g_out = shard(sum_one[4 * width :], 0)

        def rest_body(*refs):
            update_rest(rate_out, rate_wide, rate_down, *refs)

        tall, wide, low = first_out.shape, first_up.shape, first_down.shape
        rest_outs = call(
            rest_body,
            [(tall, f32, VMEM), (wide, f32, VMEM), (low, f32, VMEM)]
            + [(x.shape, x.dtype, HBM) for x in blanks[4:]],
            [SMEM, VMEM, VMEM, VMEM] + [HBM] * (15 + 11),
            (owned, g_out, g_up, g_down_t,
             weight_out, first_out, second_out, basis_out_left, basis_out_right,
             weight_up, first_up, second_up, basis_up_left, basis_up_right,
             weight_down, first_down, second_down, basis_down_left, basis_down_right, *blanks[4:]),
            [pltpu.VMEM(tall, f32)] * 3
            + [
                pltpu.VMEM(tall, bf16),
                pltpu.VMEM(basis_out_left.shape, f32),
                pltpu.VMEM(basis_out_right.shape, f32),
                pltpu.VMEM(basis_out_right.shape, bf16),
                pltpu.VMEM(tall, bf16),
                pltpu.VMEM(tall, bf16),
            ]
            + [pltpu.VMEM(wide, f32)] * 3
            + [
                pltpu.VMEM(wide, bf16),
                pltpu.VMEM(basis_up_left.shape, f32),
                pltpu.VMEM(basis_up_right.shape, f32),
                pltpu.VMEM(basis_up_left.shape, bf16),
                pltpu.VMEM(basis_up_right.shape, bf16),
                pltpu.VMEM(wide, bf16),
                pltpu.VMEM(wide, bf16),
            ]
            + [pltpu.VMEM(low, f32)] * 3
            + [pltpu.VMEM(low, bf16)] * 3
            + [pltpu.SemaphoreType.DMA((5,))],
            48,
            12 * US,
            20e6,
            {4 + 15 + i: 3 + i for i in range(11)},
        )
        grad_out_all, grad_up_all, grad_down_all = rest_outs[:3]

        pairs = sum_two.reshape(3, half, width)
        g_qkv = shard(jnp.concatenate([pairs[:, :, :cols], pairs[:, :, cols:]], 1), 2)
        small = small.astype(f32)

        def qkv_body(*refs):
            update_qkv(rate_wide, *refs)

        one = first_qkv.shape[1:]
        qkv_outs = call(
            qkv_body,
            [(first_qkv.shape, f32, VMEM)] + [(x.shape, x.dtype, HBM) for x in blanks[:4]],
            [SMEM, VMEM] + [HBM] * 9,
            (owned, g_qkv, weight_qkv, first_qkv, second_qkv, basis_qkv_left, basis_qkv_right, *blanks[:4]),
            [pltpu.VMEM(one, f32)] * 3
            + [
                pltpu.VMEM(one, bf16),
                pltpu.VMEM(basis_qkv_left.shape[1:], f32),
                pltpu.VMEM(basis_qkv_right.shape[1:], f32),
                pltpu.VMEM(basis_qkv_left.shape[1:], bf16),
                pltpu.VMEM(basis_qkv_right.shape[1:], bf16),
                pltpu.VMEM(one, bf16),
                pltpu.VMEM(one, bf16),
                pltpu.SemaphoreType.DMA((5,)),
            ],
            24,
            6 * US,
            8e6,
            {7 + i: 1 + i for i in range(4)},
        )
        grad_qkv_all = qkv_outs[0]
        grad_table_all = small[0:2]
        grad_gains_all = small[2:4]
        grad_shifts_all = small[4:8]
        grad_ff_all = shard(small[8:10].reshape(-1), 0)
        grad_bias_all = shard(small[10].reshape(2, cols), 1)
    return (
        output_rows,
        grad_rows,
        grad_table_all,
        grad_gains_all,
        grad_shifts_all,
        grad_bias_all,
        grad_ff_all,
        grad_qkv_all,
        grad_out_all,
        grad_up_all,
        grad_down_all,
        *(x[None] for x in qkv_outs[1:]),
        *(x[None] for x in rest_outs[3:]),
    )


def solution(mesh):
    in_specs = (
        P(("dp", "head"), None),
        P(("dp", "head"), None),
        P(),
        P("dp"),
        P("dp", "head", None),
        P(),
        P(None, None, "head"),
        P(None, "head"),
        P("head", None),
        P(None, "head"),
        P("head"),
        P("head", None),
        P(),
        P(),
        P(None, None, "head"),
        P(None, None, "head"),
        P("head", None),
        P("head", None),
        P(None, "head"),
        P(None, "head"),
        P("head", None),
        P("head", None),
        P(),
        P(None, "head", None, None),
        P("head", None, None),
        P(),
        P(),
        P("head", None, None),
        P("head", None, None),
        P(),
    )
    out_specs = (
        P(("dp", "head"), None),
        P(("dp", "head"), None),
        P(),
        P(),
        P(),
        P(None, "head"),
        P("head"),
        P(None, None, "head"),
        P("head", None),
        P(None, "head"),
        P("head", None),
        P("dp", None, None, "head"),
        P("dp", None, None, "head"),
        P("dp", None, None, "head"),
        P("dp", None, None, "head"),
        P("dp", "head", None),
        P("dp", None, "head", None),
        P("dp", "head", None),
        P("dp", None, "head"),
        P("dp", None, "head"),
        P("dp", None, "head"),
        P("dp", None, "head"),
        P("dp", "head", None),
        P("dp", "head", None),
        P("dp", "head", None),
        P("dp", "head", None),
    )
    return jax.shard_map(
        per_device, mesh=mesh, in_specs=in_specs, out_specs=out_specs, check_vma=False
    )
```
